32 devices in a mesh: gz: 4 (over x, core), row: 4 (over z), col: 2 (over y).
Axes of the slice: x: 2, y: 2, z: 4, core: 2. Of those that a mesh axis runs over, the one named last changes fastest.
Arguments:
- leaf_rhs: float32 [64, 256, 512], P(('gz', 'col')), may hold values from -6 to 6
- leaf_inv: bfloat16 [64, 512, 512], P(('gz', 'col'), 'row'), as said below
- leaf_lower_mid: bfloat16 [64, 512, 512], P(('gz', 'col'), None, 'row'), may hold values from -0.09375 to 0.09375
- leaf_lower_coupling: bfloat16 [64, 3, 512, 512], P(('gz', 'col'), None, None, 'row'), may hold values from -0.046875 to 0.046875
- leaf_parent: int32 [64], P(('gz', 'col')), may hold values from 0 to 1
- leaf_pattern: int32 [64, 3], P(('gz', 'col')), may hold values 0 or 1
- mid_rhs: float32 [8, 256, 512], P(('gz', 'col')), may hold values from -6 to 6
- parent_diagonal_inverse: bfloat16 [8, 512, 512], P(('gz', 'col'), 'row'), as said below
- mid_lower: bfloat16 [8, 3, 512, 512], P(('gz', 'col'), None, None, 'row'), may hold values from -0.125 to 0.125
- mid_pattern: int32 [8, 2], P(('gz', 'col')), may hold values 0 or 1
- top_rhs: float32 [4, 256, 512], P('gz'), may hold values from -6 to 6
- top_inv: bfloat16 [4, 512, 512], P('gz', 'row'), as said below
- top_lower: bfloat16 [4, 2, 512, 512], P('gz', None, None, 'row'), may hold values from -0.1875 to 0.1875
- apex_rhs: float32 [3, 256, 512], replicated, may hold values from -6 to 6
- apex_inv: bfloat16 [3, 512, 512], P(None, 'row'), as said below
- apex_lower: bfloat16 [2, 512, 512], P(None, None, 'row'), may hold values from -0.25 to 0.25
Outputs:
- leaf_solution: float32 [64, 256, 512], P(('gz', 'col'), None, 'row')
- mid_solution: float32 [8, 256, 512], P(('gz', 'col'), None, 'row')
- top_solution: float32 [4, 256, 512], P('gz', None, 'row')
- apex_solution: float32 [3, 256, 512], P(None, 'gz', 'row')
The draws below stay inside these ranges and needn't reach their ends.
Inputs may be any that keep to these rules, and one draw needn't show every extreme that they name: `leaf_inv`: each diagonal-block inverse is lower triangular with a unit diagonal. `parent_diagonal_inverse`: lower triangular with a unit diagonal. `top_inv`: lower triangular with a unit diagonal. `apex_inv`: lower triangular with a unit diagonal.
All inputs are finite; a program needn't handle non-finite values. No bound on the sum of `leaf_pattern` or of `mid_pattern` on one device may be relied on, other than what follows from the above.
Results may differ from the reference program's by a relative error of at most 0.015.
Values may be sent and summed in bfloat16 or wider, within the bound.
No kernel may reach another device: no remote copies, remote signals or barrier semaphores. Data moves between devices by JAX's collectives and lax.ppermute only.
A program may use at most 128 MiB of HBM per device.

```python
import jax
import jax.numpy as jnp
from jax import lax

B = 512
R = 256
LEAF_DEV = 8
LEAVES = 64
MIDS = 8
N_GZ = 4
N_COL = 2


def unit_lower(values):
    row_ids = lax.broadcasted_iota(jnp.int32, (B, B), 0)
    col_ids = lax.broadcasted_iota(jnp.int32, (B, B), 1)
    below = jnp.where(row_ids > col_ids, values * (0.7 / B ** 0.5), 0.0)
    return (below + jnp.where(row_ids == col_ids, 1.0, 0.0)).astype(jnp.bfloat16)


def draw_leaf_inv(key, part):
    key = jax.random.fold_in(key, 11)
    values = jax.random.normal(key, (LEAVES, B, B), jnp.float32)
    return unit_lower(values)


def draw_parent_diagonal_inverse(key, part):
    key = jax.random.fold_in(key, 12)
    values = jax.random.normal(key, (MIDS, B, B), jnp.float32)
    return unit_lower(values)


def draw_top_inv(key, part):
    key = jax.random.fold_in(key, 13)
    values = jax.random.normal(key, (N_GZ, B, B), jnp.float32)
    return unit_lower(values)


def draw_apex_inv(key, part):
    key = jax.random.fold_in(key, 14)
    values = jax.random.normal(key, (3, B, B), jnp.float32)
    return unit_lower(values)


def touch_ends(result, stream_key, least, high):
    place = [jax.random.randint(jax.random.fold_in(stream_key, axis), (), 0, length) for axis, length in enumerate(result.shape)]
    main_axis = result.shape.index(max(result.shape))
    beside = place[:main_axis] + [(place[main_axis] + 1) % result.shape[main_axis]] + place[main_axis + 1:]
    return result.at[tuple(place)].set(least).at[tuple(beside)].set(high)


def shard_levels(rng, extent, pieces, least, top_value):
    gain = 1.0
    for dim, shards_of in pieces:
        heights = jax.random.uniform(jax.random.fold_in(jax.random.fold_in(rng, 6), dim), (shards_of,), jnp.float32, least / len(pieces), top_value / len(pieces))
        gain = gain * jnp.repeat(jnp.exp(heights), extent[dim] // shards_of).reshape((-1,) + (1,) * (len(extent) - 1 - dim))
    return gain


def gaussian(rng, extent, deviation, reach, cuts=(), kind=jnp.bfloat16):
    result = deviation * jax.random.normal(rng, extent, jnp.float32)
    if cuts:
        result = result * shard_levels(rng, extent, cuts, -0.22, 0.18)
    return jnp.clip(result, -reach, reach).astype(kind)


def setup_inputs(seed: int = 0) -> dict:
    key_list = jax.random.split(jax.random.key(seed), 17)
    leaf_rhs = gaussian(key_list[0], (LEAVES, R, B), 1.0, 6.0, ((0, 8),), jnp.float32)
    leaf_inv = draw_leaf_inv(jax.random.fold_in(key_list[16], 71), 0)
    leaf_lower_mid = gaussian(key_list[2], (LEAVES, B, B), (B * LEAF_DEV) ** -0.5, 0.09375, ((0, 8), (2, 4)))
    leaf_lower_coupling = gaussian(key_list[3], (LEAVES, 3, B, B), (B * LEAF_DEV * N_COL * 2) ** -0.5, 0.046875, ((0, 8), (3, 4)))
    leaf_parent = touch_ends(jax.random.randint(key_list[4], (LEAVES,), 0, N_COL), jax.random.fold_in(key_list[4], 1), 0, N_COL - 1).astype(jnp.int32)
    leaf_pattern = touch_ends((jax.random.randint(key_list[5], (LEAVES, 3), 0, 2) < 1).astype(jnp.int32), jax.random.fold_in(key_list[5], 1), 0, 1)
    mid_rhs = gaussian(key_list[6], (MIDS, R, B), 1.0, 6.0, ((0, 8),), jnp.float32)
    parent_diagonal_inverse = draw_parent_diagonal_inverse(jax.random.fold_in(key_list[16], 71), 0)
    mid_lower = gaussian(key_list[8], (MIDS, 3, B, B), (B * N_COL * 2) ** -0.5, 0.125, ((0, 8), (3, 4)))
    mid_pattern = touch_ends((jax.random.randint(key_list[9], (MIDS, 2), 0, 2) < 1).astype(jnp.int32), jax.random.fold_in(key_list[9], 1), 0, 1)
    top_rhs = gaussian(key_list[10], (N_GZ, R, B), 1.0, 6.0, ((0, 4),), jnp.float32)
    top_inv = draw_top_inv(jax.random.fold_in(key_list[16], 71), 0)
    top_lower = gaussian(key_list[12], (N_GZ, 2, B, B), (B * 2) ** -0.5, 0.1875, ((0, 4), (3, 4)))
    apex_rhs = gaussian(key_list[13], (3, R, B), 1.0, 6.0, (), jnp.float32)
    apex_inv = draw_apex_inv(jax.random.fold_in(key_list[16], 71), 0)
    apex_lower = gaussian(key_list[15], (2, B, B), B ** -0.5, 0.25, ((2, 4),))
    return {"leaf_rhs": leaf_rhs, "leaf_inv": leaf_inv, "leaf_lower_mid": leaf_lower_mid, "leaf_lower_coupling": leaf_lower_coupling, "leaf_parent": leaf_parent, "leaf_pattern": leaf_pattern, "mid_rhs": mid_rhs, "parent_diagonal_inverse": parent_diagonal_inverse, "mid_lower": mid_lower, "mid_pattern": mid_pattern, "top_rhs": top_rhs, "top_inv": top_inv, "top_lower": top_lower, "apex_rhs": apex_rhs, "apex_inv": apex_inv, "apex_lower": apex_lower}


def solve_one(items):
    inverse, right = items
    return jnp.dot(right.astype(jnp.bfloat16), inverse.T, preferred_element_type=jnp.float32)


def three_terms(items):
    solved, blocks = items
    return jnp.stack([jnp.dot(solved, blocks[k].T, preferred_element_type=jnp.float32) for k in range(blocks.shape[0])])


def reference(leaf_rhs, leaf_inv, leaf_lower_mid, leaf_lower_coupling, leaf_parent, leaf_pattern, mid_rhs, parent_diagonal_inverse, mid_lower, mid_pattern, top_rhs, top_inv, top_lower, apex_rhs, apex_inv, apex_lower):
    leaf_solved = lax.map(solve_one, (leaf_inv, leaf_rhs))
    leaf_round = leaf_solved.astype(jnp.bfloat16)

    def leaf_terms(items):
        solved, lower_mid, lower_up = items
        toward_parent = jnp.dot(solved, lower_mid.T, preferred_element_type=jnp.float32)
        return toward_parent, three_terms((solved, lower_up))

    toward_parent, to_up = lax.map(leaf_terms, (leaf_round, leaf_lower_mid, leaf_lower_coupling))
    to_up = to_up * leaf_pattern.astype(jnp.float32)[:, :, None, None]
    layer_lookup = jnp.arange(LEAVES, dtype=jnp.int32) // (LEAF_DEV * N_COL)
    mid_index = (layer_lookup * N_COL + leaf_parent).astype(jnp.int32)
    mid_total = mid_rhs - jax.ops.segment_sum(toward_parent, mid_index, num_segments=MIDS)
    parent_unknowns = lax.map(solve_one, (parent_diagonal_inverse, mid_total))
    mid_round = parent_unknowns.astype(jnp.bfloat16)
    mid_up = lax.map(three_terms, (mid_round, mid_lower))
    mid_weight = jnp.concatenate([jnp.ones((MIDS, 1), jnp.float32), mid_pattern.astype(jnp.float32)], axis=1)
    mid_up = mid_up * mid_weight[:, :, None, None]
    mid_layer = jnp.arange(MIDS, dtype=jnp.int32) // N_COL
    top_total = top_rhs - jax.ops.segment_sum(to_up[:, 0], layer_lookup, num_segments=N_GZ) - jax.ops.segment_sum(mid_up[:, 0], mid_layer, num_segments=N_GZ)
    top_solved = lax.map(solve_one, (top_inv, top_total))
    top_round = top_solved.astype(jnp.bfloat16)
    top_up = lax.map(three_terms, (top_round, top_lower))
    top_pair = jnp.arange(N_GZ, dtype=jnp.int32) // 2
    front_total = apex_rhs[:2] - jax.ops.segment_sum(to_up[:, 1], layer_lookup // 2, num_segments=2)
    front_total = front_total - jax.ops.segment_sum(mid_up[:, 1], mid_layer // 2, num_segments=2)
    front_total = front_total - jax.ops.segment_sum(top_up[:, 0], top_pair, num_segments=2)
    front_solved = lax.map(solve_one, (apex_inv[:2], front_total))
    front_round = front_solved.astype(jnp.bfloat16)
    front_up = jnp.dot(front_round[0], apex_lower[0].T, preferred_element_type=jnp.float32) + jnp.dot(front_round[1], apex_lower[1].T, preferred_element_type=jnp.float32)
    last_total = apex_rhs[2] - jnp.sum(to_up[:, 2], axis=0) - jnp.sum(mid_up[:, 2], axis=0) - jnp.sum(top_up[:, 1], axis=0) - front_up
    last_solved = solve_one((apex_inv[2], last_total))
    apex_unknowns = jnp.concatenate([front_solved, last_solved[None]], axis=0)
    return leaf_solved, parent_unknowns, top_solved, apex_unknowns
```

```python
import functools

import jax
import jax.numpy as jnp
from jax import lax
from jax.experimental import pallas as pl
from jax.experimental.pallas import tpu as pltpu
from jax.sharding import PartitionSpec as P

BF16 = jnp.bfloat16
F32 = jnp.float32
VMEM_BYTES = 48 * 1024 * 1024


def times_transposed(left, right):
    return lax.dot_general(left, right, (((1,), (1,)), ((), ())), preferred_element_type=F32)


def leaf_kernel(per_step, slots, slot_ref, rhs_ref, inv_ref, mid_ref, solved_ref, round_ref, terms_ref, total):
    step = pl.program_id(0)

    @pl.when(step == 0)
    def _():
        total[...] = jnp.zeros_like(total)

    for i in range(per_step):
        solved = times_transposed(rhs_ref[i].astype(BF16), inv_ref[i])
        solved_ref[i] = solved
        rounded = solved.astype(BF16)
        round_ref[i] = rounded
        slot = slot_ref[step * per_step + i]
        total[slot] += times_transposed(rounded, mid_ref[i])

    @pl.when(step == pl.num_programs(0) - 1)
    def _():
        for s in range(slots):
            terms_ref[s] = total[s].astype(BF16)


def leaf_solve(slot, rhs, inv, lower_mid, slots):
    leaves, rows, size = rhs.shape
    width = inv.shape[1]
    per_step = 2 if leaves % 2 == 0 else 1
    return pl.pallas_call(
        functools.partial(leaf_kernel, per_step, slots),
        grid=(leaves // per_step,),
        in_specs=[
            pl.BlockSpec(memory_space=pltpu.SMEM),
            pl.BlockSpec((per_step, rows, size), lambda i: (i, 0, 0)),
            pl.BlockSpec((per_step, width, size), lambda i: (i, 0, 0)),
            pl.BlockSpec((per_step, size, width), lambda i: (i, 0, 0)),
        ],
        out_specs=[
            pl.BlockSpec((per_step, rows, width), lambda i: (i, 0, 0)),
            pl.BlockSpec((per_step, rows, width), lambda i: (i, 0, 0)),
            pl.BlockSpec((slots, rows, size), lambda i: (0, 0, 0)),
        ],
        out_shape=[
            jax.ShapeDtypeStruct((leaves, rows, width), F32),
            jax.ShapeDtypeStruct((leaves, rows, width), BF16),
            jax.ShapeDtypeStruct((slots, rows, size), BF16),
        ],
        scratch_shapes=[pltpu.VMEM((slots, rows, size), F32)],
        compiler_params=pltpu.CompilerParams(
            dimension_semantics=("arbitrary",), vmem_limit_bytes=VMEM_BYTES
        ),
        cost_estimate=pl.CostEstimate(
            flops=4 * leaves * rows * size * width,
            bytes_accessed=leaves * (rows * size * 4 + 4 * width * size + rows * width * 6),
            transcendentals=0,
        ),
        name="leaf_solve",
    )(slot, rhs, inv, lower_mid)


def coupling_kernel(per_step, pattern_ref, round_ref, lower_ref, up_ref):
    step = pl.program_id(0)

    @pl.when(step == 0)
    def _():
        up_ref[...] = jnp.zeros_like(up_ref)

    for k in range(up_ref.shape[0]):
        left, right = [], []
        for i in range(per_step):
            weight = pattern_ref[step * per_step + i, k].astype(F32).astype(BF16)
            left.append(round_ref[i] * weight)
            right.append(lower_ref[i, k])
        left = left[0] if per_step == 1 else jnp.concatenate(left, axis=1)
        right = right[0] if per_step == 1 else jnp.concatenate(right, axis=1)
        up_ref[k] += times_transposed(left, right)


def leaf_coupling(pattern, rounded, lower):
    leaves, rows, width = rounded.shape
    kinds, size = lower.shape[1:3]
    per_step = 2 if leaves % 2 == 0 else 1
    return pl.pallas_call(
        functools.partial(coupling_kernel, per_step),
        grid=(leaves // per_step,),
        in_specs=[
            pl.BlockSpec(memory_space=pltpu.SMEM),
            pl.BlockSpec((per_step, rows, width), lambda i: (i, 0, 0)),
            pl.BlockSpec((per_step, kinds, size, width), lambda i: (i, 0, 0, 0)),
        ],
        out_specs=pl.BlockSpec((kinds, rows, size), lambda i: (0, 0, 0)),
        out_shape=jax.ShapeDtypeStruct((kinds, rows, size), F32),
        compiler_params=pltpu.CompilerParams(
            dimension_semantics=("arbitrary",), vmem_limit_bytes=VMEM_BYTES
        ),
        cost_estimate=pl.CostEstimate(
            flops=2 * leaves * kinds * rows * size * width,
            bytes_accessed=leaves * (rows * width * 2 + kinds * size * width * 2) + kinds * rows * size * 4,
            transcendentals=0,
        ),
        name="leaf_coupling",
    )(pattern, rounded, lower)


def swap(block, axis, bit):
    count = lax.axis_size(axis)
    return lax.ppermute(block, axis, [(i, i ^ 1 << bit) for i in range(count)])


def swap_sum(halves, axis, bit):
    here = lax.axis_index(axis) >> bit & 1
    kept = lax.dynamic_index_in_dim(halves, here, 0, keepdims=False)
    given = lax.dynamic_index_in_dim(halves, 1 - here, 0, keepdims=False)
    return kept.astype(F32) + swap(given.astype(BF16), axis, bit).astype(F32)


def exchange(pieces, axis):
    return lax.all_to_all(pieces, axis, split_axis=0, concat_axis=0, tiled=True)


def scatter_sum(pieces, axis):
    return jnp.sum(exchange(pieces.astype(BF16), axis).astype(F32), axis=0)


def col_sum(pieces):
    if pieces.shape[0] == 2:
        return swap_sum(pieces, "col", 0)
    return scatter_sum(pieces, "col")


def spread(piece, axis):
    count = lax.axis_size(axis)
    return exchange(jnp.broadcast_to(piece[None], (count,) + piece.shape), axis)


def col_spread(piece):
    if lax.axis_size("col") == 2:
        other = swap(piece, "col", 0)
        first = lax.axis_index("col") == 0
        return jnp.stack([jnp.where(first, piece, other), jnp.where(first, other, piece)])
    return spread(piece, "col")


def per_device(
    leaf_rhs,
    leaf_inv,
    leaf_lower_mid,
    leaf_lower_coupling,
    leaf_parent,
    leaf_pattern,
    mid_rhs,
    parent_diagonal_inverse,
    mid_lower,
    mid_pattern,
    top_rhs,
    top_inv,
    top_lower,
    apex_rhs,
    apex_inv,
    apex_lower,
):
    cols = lax.axis_size("col")
    rows = lax.axis_size("row")
    col = lax.axis_index("col")
    row = lax.axis_index("row")
    gz = lax.axis_index("gz")
    pair, core = gz // 2, gz % 2
    rhs_count, size = leaf_rhs.shape[1:]
    part = rhs_count // (4 * cols)

    first = col if cols == 2 else 0
    slot = lax.rem(leaf_parent - first + cols, cols)
    leaf_solved, leaf_round, terms = leaf_solve(slot, leaf_rhs, leaf_inv, leaf_lower_mid, cols)
    if cols == 2:
        mid_part = terms[0].astype(F32) + swap(terms[1], "col", 0).astype(F32)
    else:
        mid_part = scatter_sum(terms, "col")
    layer_up = leaf_coupling(leaf_pattern, leaf_round, leaf_lower_coupling)
    quarter = rhs_count // rows
    mid_sum = scatter_sum(mid_part.reshape(rows, quarter, size), "row")
    mid_total = lax.dynamic_slice_in_dim(mid_rhs[0], row * quarter, quarter, 0) - mid_sum
    mid_ready = spread(mid_total.astype(BF16), "row").reshape(rhs_count, size)
    mid_solved = times_transposed(mid_ready, parent_diagonal_inverse[0])
    mid_round = mid_solved.astype(BF16)
    mid_weight = mid_pattern[0].astype(F32)

    top_part = layer_up[0] + times_transposed(mid_round, mid_lower[0, 0])
    top_part = top_part.astype(BF16).reshape(rows, cols, part, size).swapaxes(0, 1)
    top_sum = scatter_sum(top_part.reshape(rows * cols, part, size), ("col", "row"))
    top_start = (row * cols + col) * part
    top_total = lax.dynamic_slice_in_dim(top_rhs[0], top_start, part, 0) - top_sum
    top_ready = spread(top_total.astype(BF16), "row").reshape(rows * part, size)
    top_solved = times_transposed(top_ready, top_inv[0])
    top_round = top_solved.astype(BF16)

    late = jnp.stack([layer_up[k] + mid_weight[k - 1] * times_transposed(mid_round, mid_lower[0, k]) for k in (1, 2)])
    late = late.reshape(2, 2, 2, cols, part, size)
    late = swap_sum(late.transpose(2, 0, 1, 3, 4, 5), "gz", 0)
    late = col_sum(late.transpose(2, 0, 1, 3, 4))

    up = jnp.stack([times_transposed(top_round, top_lower[0, k]) for k in (0, 1)])
    up = swap_sum(up.reshape(2, 2, 2, part, size).transpose(2, 0, 1, 3, 4), "gz", 0) + late
    half = part // 2
    front_sum = scatter_sum(up[0].reshape(rows, half, size), "row")
    front_start = row // 2 * (rhs_count // 2) + (core * cols + col) * part + row % 2 * half
    front_rhs = lax.dynamic_slice(apex_rhs, (pair, front_start, 0), (1, half, size))[0]
    front_ready = spread((front_rhs - front_sum).astype(BF16), "row").reshape(2 * part, size)
    front_inv = lax.dynamic_index_in_dim(apex_inv, pair, 0, keepdims=False)
    front_lower = lax.dynamic_index_in_dim(apex_lower, pair, 0, keepdims=False)
    front_solved = times_transposed(front_ready, front_inv)

    own_up = times_transposed(front_solved.astype(BF16), front_lower)
    last_part = swap_sum(up[1] + own_up.reshape(2, part, size), "gz", 1)
    last_sum = jnp.sum(spread(last_part.astype(BF16), "row").astype(F32), axis=0)
    last_start = (pair * 2 * cols + core * cols + col) * part
    last_rhs = lax.dynamic_slice_in_dim(apex_rhs[2], last_start, part, 0)
    last_solved = times_transposed((last_rhs - last_sum).astype(BF16), apex_inv[2])

    width = last_solved.shape[1]
    front_solved = front_solved.reshape(2, part, width)
    own_front = lax.dynamic_index_in_dim(front_solved, pair, 0, keepdims=False)
    other_front = swap(lax.dynamic_index_in_dim(front_solved, 1 - pair, 0, keepdims=False), "gz", 1)
    leading = pair == 0
    fronts = jnp.stack([jnp.where(leading, own_front, other_front), jnp.where(leading, other_front, own_front)])
    fronts = col_spread(fronts).swapaxes(0, 1).reshape(2, cols * part, width)
    last = col_spread(last_solved).reshape(1, cols * part, width)
    top_all = col_spread(top_solved.reshape(rows, part, width)).swapaxes(0, 1).reshape(1, rhs_count, width)
    return (leaf_solved, mid_solved[None], top_all, jnp.concatenate([fronts, last], axis=0))


def solution(mesh):
    placed = (
        P(("gz", "col"), None, None),
        P(("gz", "col"), "row", None),
        P(("gz", "col"), None, "row"),
        P(("gz", "col"), None, None, "row"),
        P(("gz", "col")),
        P(("gz", "col"), None),
        P(("gz", "col"), None, None),
        P(("gz", "col"), "row", None),
        P(("gz", "col"), None, None, "row"),
        P(("gz", "col"), None),
        P("gz", None, None),
        P("gz", "row", None),
        P("gz", None, None, "row"),
        P(),
        P(None, "row", None),
        P(None, None, "row"),
    )
    return jax.shard_map(
        per_device,
        mesh=mesh,
        in_specs=placed,
        out_specs=(
            P(("gz", "col"), None, "row"),
            P(("gz", "col"), None, "row"),
            P("gz", None, "row"),
            P(None, "gz", "row"),
        ),
        check_vma=False,
    )
```

```python
import functools
import math

import jax
import jax.numpy as jnp
from jax import lax
from jax.experimental import pallas as pl
from jax.experimental.pallas import tpu as pltpu
from jax.sharding import PartitionSpec as P

BF16 = jnp.bfloat16
F32 = jnp.float32
VMEM_BYTES = 60 * 1024 * 1024
STEP_VMEM_BYTES = 32 * 1024 * 1024


def times_transposed(left, right):
    return lax.dot_general(left, right, (((1,), (1,)), ((), ())), preferred_element_type=F32)


def leaf_kernel(per_step, slots, parent_ref, rhs_ref, inv_ref, mid_ref, solved_ref, round_ref, *rest):
    terms_refs, total = rest[:-1], rest[-1]
    step = pl.program_id(0)
    first = lax.axis_index("col") if slots == 2 else 0

    @pl.when(step == 0)
    def _():
        total[...] = jnp.zeros_like(total)

    for i in range(per_step):
        solved = times_transposed(rhs_ref[i].astype(BF16), inv_ref[i])
        solved_ref[i] = solved
        rounded = solved.astype(BF16)
        round_ref[step * per_step + i] = rounded
        slot = parent_ref[step * per_step + i] ^ first
        total[slot] += times_transposed(rounded, mid_ref[i])

    @pl.when(step == pl.num_programs(0) - 1)
    def _():
        for s, ref in enumerate(terms_refs):
            ref[...] = total[s].astype(ref.dtype)


def leaf_solve(parent, rhs, inv, lower_mid, slots):
    leaves, rows, size = rhs.shape
    width = inv.shape[1]
    per_step = 2 if leaves % 2 == 0 else 1
    return pl.pallas_call(
        functools.partial(leaf_kernel, per_step, slots),
        grid=(leaves // per_step,),
        in_specs=[
            pl.BlockSpec(memory_space=pltpu.SMEM),
            pl.BlockSpec((per_step, rows, size), lambda i: (i, 0, 0)),
            pl.BlockSpec((per_step, width, size), lambda i: (i, 0, 0)),
            pl.BlockSpec((per_step, size, width), lambda i: (i, 0, 0)),
        ],
        out_specs=[
            pl.BlockSpec((per_step, rows, width), lambda i: (i, 0, 0)),
        ]
        + [pl.BlockSpec(memory_space=pltpu.VMEM)] * (1 + slots),
        out_shape=[
            jax.ShapeDtypeStruct((leaves, rows, width), F32),
            jax.ShapeDtypeStruct((leaves, rows, width), BF16),
        ]
        + [jax.ShapeDtypeStruct((rows, size), BF16)] * slots,
        scratch_shapes=[pltpu.VMEM((slots, rows, size), F32)],
        compiler_params=pltpu.CompilerParams(
            dimension_semantics=("arbitrary",), vmem_limit_bytes=VMEM_BYTES
        ),
        cost_estimate=pl.CostEstimate(
            flops=4 * leaves * rows * size * width,
            bytes_accessed=leaves * (rows * size * 4 + 4 * width * size + rows * width * 6),
            transcendentals=0,
        ),
        name="leaf_solve",
    )(parent, rhs, inv, lower_mid)


def coupling_kernel(per_step, pattern_ref, round_ref, lower_ref, up_ref):
    step = pl.program_id(0)

    @pl.when(step == 0)
    def _():
        up_ref[...] = jnp.zeros_like(up_ref)

    for k in range(up_ref.shape[0]):
        left, right = [], []
        for i in range(per_step):
            weight = pattern_ref[step * per_step + i, k].astype(F32).astype(BF16)
            left.append(round_ref[step * per_step + i] * weight)
            right.append(lower_ref[i, k])
        left = left[0] if per_step == 1 else jnp.concatenate(left, axis=1)
        right = right[0] if per_step == 1 else jnp.concatenate(right, axis=1)
        up_ref[k] += times_transposed(left, right)


def leaf_coupling(pattern, rounded, lower):
    leaves, rows, width = rounded.shape
    kinds, size = lower.shape[1:3]
    per_step = 2 if leaves % 2 == 0 else 1
    return pl.pallas_call(
        functools.partial(coupling_kernel, per_step),
        grid=(leaves // per_step,),
        in_specs=[
            pl.BlockSpec(memory_space=pltpu.SMEM),
            pl.BlockSpec(memory_space=pltpu.VMEM),
            pl.BlockSpec((per_step, kinds, size, width), lambda i: (i, 0, 0, 0)),
        ],
        out_specs=pl.BlockSpec(memory_space=pltpu.VMEM),
        out_shape=jax.ShapeDtypeStruct((kinds, rows, size), F32),
        compiler_params=pltpu.CompilerParams(
            dimension_semantics=("arbitrary",), vmem_limit_bytes=VMEM_BYTES
        ),
        cost_estimate=pl.CostEstimate(
            flops=2 * leaves * kinds * rows * size * width,
            bytes_accessed=leaves * (rows * width * 2 + kinds * size * width * 2) + kinds * rows * size * 4,
            transcendentals=0,
        ),
        name="leaf_coupling",
    )(pattern, rounded, lower)


def swap(block, axis, bit):
    count = lax.axis_size(axis)
    return lax.ppermute(block, axis, [(i, i ^ 1 << bit) for i in range(count)])


def swap_sum(halves, axis, bit):
    here = lax.axis_index(axis) >> bit & 1
    kept = lax.dynamic_index_in_dim(halves, here, 0, keepdims=False)
    given = lax.dynamic_index_in_dim(halves, 1 - here, 0, keepdims=False)
    return kept.astype(F32) + swap(given.astype(BF16), axis, bit).astype(F32)


def exchange(pieces, axis):
    return lax.all_to_all(pieces, axis, split_axis=0, concat_axis=0, tiled=True)


def scatter_sum(pieces, axis):
    return jnp.sum(exchange(pieces.astype(BF16), axis).astype(F32), axis=0)


def col_sum(pieces):
    if pieces.shape[0] == 2:
        return swap_sum(pieces, "col", 0)
    return scatter_sum(pieces, "col")


def spread(piece, axis):
    count = lax.axis_size(axis)
    return exchange(jnp.broadcast_to(piece[None], (count,) + piece.shape), axis)


def col_spread(piece):
    if lax.axis_size("col") == 2:
        other = swap(piece, "col", 0)
        first = lax.axis_index("col") == 0
        return jnp.stack([jnp.where(first, piece, other), jnp.where(first, other, piece)])
    return spread(piece, "col")


def any_cols(
    leaf_rhs,
    leaf_inv,
    leaf_lower_mid,
    leaf_lower_coupling,
    leaf_parent,
    leaf_pattern,
    mid_rhs,
    parent_diagonal_inverse,
    mid_lower,
    mid_pattern,
    top_rhs,
    top_inv,
    top_lower,
    apex_rhs,
    apex_inv,
    apex_lower,
):
    cols = lax.axis_size("col")
    rows = lax.axis_size("row")
    col = lax.axis_index("col")
    row = lax.axis_index("row")
    gz = lax.axis_index("gz")
    pair, core = gz // 2, gz % 2
    rhs_count, size = leaf_rhs.shape[1:]
    part = rhs_count // (4 * cols)

    leaf_solved, leaf_round, *terms = leaf_solve(leaf_parent, leaf_rhs, leaf_inv, leaf_lower_mid, cols)
    if cols == 2:
        mid_part = terms[0].astype(F32) + swap(terms[1], "col", 0).astype(F32)
    else:
        mid_part = scatter_sum(jnp.stack(terms), "col")
    layer_up = leaf_coupling(leaf_pattern, leaf_round, leaf_lower_coupling)
    quarter = rhs_count // rows
    mid_sum = scatter_sum(mid_part.reshape(rows, quarter, size), "row")
    mid_total = lax.dynamic_slice_in_dim(mid_rhs[0], row * quarter, quarter, 0) - mid_sum
    mid_ready = spread(mid_total.astype(BF16), "row").reshape(rhs_count, size)
    mid_solved = times_transposed(mid_ready, parent_diagonal_inverse[0])
    mid_round = mid_solved.astype(BF16)
    mid_weight = mid_pattern[0].astype(F32)

    top_part = layer_up[0] + times_transposed(mid_round, mid_lower[0, 0])
    top_part = top_part.astype(BF16).reshape(rows, cols, part, size).swapaxes(0, 1)
    top_sum = scatter_sum(top_part.reshape(rows * cols, part, size), ("col", "row"))
    top_start = (row * cols + col) * part
    top_total = lax.dynamic_slice_in_dim(top_rhs[0], top_start, part, 0) - top_sum
    top_ready = spread(top_total.astype(BF16), "row").reshape(rows * part, size)
    top_solved = times_transposed(top_ready, top_inv[0])
    top_round = top_solved.astype(BF16)

    late = jnp.stack([layer_up[k] + mid_weight[k - 1] * times_transposed(mid_round, mid_lower[0, k]) for k in (1, 2)])
    late = late.reshape(2, 2, 2, cols, part, size)
    late = swap_sum(late.transpose(2, 0, 1, 3, 4, 5), "gz", 0)
    late = col_sum(late.transpose(2, 0, 1, 3, 4))

    up = jnp.stack([times_transposed(top_round, top_lower[0, k]) for k in (0, 1)])
    up = swap_sum(up.reshape(2, 2, 2, part, size).transpose(2, 0, 1, 3, 4), "gz", 0) + late
    half = part // 2
    front_sum = scatter_sum(up[0].reshape(rows, half, size), "row")
    front_start = row // 2 * (rhs_count // 2) + (core * cols + col) * part + row % 2 * half
    front_rhs = lax.dynamic_slice(apex_rhs, (pair, front_start, 0), (1, half, size))[0]
    front_ready = spread((front_rhs - front_sum).astype(BF16), "row").reshape(2 * part, size)
    front_inv = lax.dynamic_index_in_dim(apex_inv, pair, 0, keepdims=False)
    front_lower = lax.dynamic_index_in_dim(apex_lower, pair, 0, keepdims=False)
    front_solved = times_transposed(front_ready, front_inv)

    own_up = times_transposed(front_solved.astype(BF16), front_lower)
    last_part = swap_sum(up[1] + own_up.reshape(2, part, size), "gz", 1)
    last_sum = jnp.sum(spread(last_part.astype(BF16), "row").astype(F32), axis=0)
    last_start = (pair * 2 * cols + core * cols + col) * part
    last_rhs = lax.dynamic_slice_in_dim(apex_rhs[2], last_start, part, 0)
    last_solved = times_transposed((last_rhs - last_sum).astype(BF16), apex_inv[2])

    width = last_solved.shape[1]
    front_solved = front_solved.reshape(2, part, width)
    own_front = lax.dynamic_index_in_dim(front_solved, pair, 0, keepdims=False)
    other_front = swap(lax.dynamic_index_in_dim(front_solved, 1 - pair, 0, keepdims=False), "gz", 1)
    leading = pair == 0
    fronts = jnp.stack([jnp.where(leading, own_front, other_front), jnp.where(leading, other_front, own_front)])
    fronts = col_spread(fronts).swapaxes(0, 1).reshape(2, cols * part, width)
    last = col_spread(last_solved).reshape(1, cols * part, width)
    top_all = col_spread(top_solved.reshape(rows, part, width)).swapaxes(0, 1).reshape(1, rhs_count, width)
    return (leaf_solved, mid_solved[None], top_all, jnp.concatenate([fronts, last], axis=0))


def partners(block, moves):
    blocks = block if isinstance(block, (list, tuple)) else [block] * len(moves)
    arrived = []
    for item, move in zip(blocks, moves):
        axes = tuple(move)
        sizes = [lax.axis_size(axis) for axis in axes]
        route = []
        for source in range(math.prod(sizes)):
            place, rest = [], source
            for count in reversed(sizes):
                place.insert(0, rest % count)
                rest //= count
            target = 0
            for at, count, axis in zip(place, sizes, axes):
                target = target * count + (at ^ move[axis])
            route.append((source, target))
        arrived.append(lax.ppermute(item, axes, route))
    return arrived


def whole_call(kernel, name, operands, results, flops=0, scratch=(), scalars=0, after=()):
    moved = sum(math.prod(a.shape) * a.dtype.itemsize for a in operands)
    moved += sum(math.prod(shape) * jnp.dtype(kind).itemsize for shape, kind in results)
    smem, vmem = pl.BlockSpec(memory_space=pltpu.SMEM), pl.BlockSpec(memory_space=pltpu.VMEM)

    def body(*refs):
        kernel(*refs[len(after) :])

    return pl.pallas_call(
        body,
        in_specs=[pl.BlockSpec(memory_space=pl.ANY)] * len(after)
        + [smem] * scalars
        + [vmem] * (len(operands) - scalars),
        out_specs=[vmem] * len(results),
        out_shape=[jax.ShapeDtypeStruct(shape, kind) for shape, kind in results],
        scratch_shapes=list(scratch),
        compiler_params=pltpu.CompilerParams(vmem_limit_bytes=STEP_VMEM_BYTES),
        cost_estimate=pl.CostEstimate(flops=flops, bytes_accessed=moved, transcendentals=0),
        name=name,
    )(*after, *operands)


def piece(index, length):
    return pl.ds(pl.multiple_of(index * length, length), length)


def widened(*refs):
    total = refs[0][...].astype(F32)
    for ref in refs[1:]:
        total = total + ref[...].astype(F32)
    return total


ROW_MOVES = [{"row": d} for d in (3, 2, 1)]


def mid_pieces_kernel(terms_ref, other_ref, kept_ref, *given_refs):
    row, length = lax.axis_index("row"), kept_ref.shape[0]
    for d, ref in zip((0, 3, 2, 1), (kept_ref,) + given_refs):
        at = piece(row ^ d, length)
        ref[...] = (terms_ref[at].astype(F32) + other_ref[at].astype(F32)).astype(ref.dtype)


def mid_total_kernel(rhs_ref, kept_ref, r1, r2, r3, ready_ref):
    at = piece(lax.axis_index("row"), ready_ref.shape[0])
    ready_ref[...] = (rhs_ref[0, at] - widened(kept_ref, r1, r2, r3)).astype(BF16)


def mid_solve_kernel(
    pattern_ref, p0, p3, p2, p1, inv_ref, lower_ref, up_ref,
    solved_ref, top_ref, top_given_ref, late_ref, late_given_ref, rounded, total,
):
    row, col, core = lax.axis_index("row"), lax.axis_index("col"), lax.axis_index("gz") & 1
    length, part = p0.shape[0], top_ref.shape[1]
    for d, ref in zip((0, 3, 2, 1), (p0, p3, p2, p1)):
        at = piece(row ^ d, length)
        solved = times_transposed(ref[...], inv_ref[0])
        solved_ref[at] = solved
        rounded[at] = solved.astype(BF16)
    total[...] = up_ref[0] + times_transposed(rounded[...], lower_ref[0, 0])
    for i in range(4):
        top_ref[i] = total[piece(i * 2 + col, part)]
        top_given_ref[i] = total[piece(i * 2 + 1 - col, part)].astype(BF16)
    for k in (1, 2):
        weight = pattern_ref[0, k - 1].astype(F32)
        total[...] = up_ref[k] + weight * times_transposed(rounded[...], lower_ref[0, k])
        for half in (0, 1):
            late_ref[k - 1, half] = total[piece(half * 2 + core, length)]
            late_given_ref[k - 1, half] = total[piece(half * 2 + 1 - core, length)].astype(BF16)


def repeat_top_kernel(inv_ref, share_ref):
    half = lax.axis_index("col")
    block = share_ref.shape[3]
    for i in (0, 1):
        share = inv_ref[0, :, piece(half * 2 + i, block)]
        for r in range(share_ref.shape[0]):
            share_ref[r, i] = share


def whole_top_kernel(own_ref, other_ref, whole_ref):
    half = lax.axis_index("col")
    block = own_ref.shape[3]
    for r in range(own_ref.shape[0]):
        for i in (0, 1):
            whole_ref[pl.ds(r * block, block), piece(half * 2 + i, block)] = own_ref[r, i]
            whole_ref[pl.ds(r * block, block), piece((1 - half) * 2 + i, block)] = other_ref[r, i]


def repeat_apex_kernel(inv_ref, lower_ref, share_ref):
    gz, col = lax.axis_index("gz"), lax.axis_index("col")
    pair, block = gz >> 1, share_ref.shape[3]
    quarter = piece((gz & 1) * 2 + col, block)
    shares = (inv_ref[pair, :, quarter], inv_ref[2, :, quarter], lower_ref[pair, quarter, :])
    for i, share in enumerate(shares):
        for r in range(share_ref.shape[0]):
            share_ref[r, i] = share


def whole_apex_kernel(own_ref, col_ref, core_ref, both_ref, front_ref, last_ref, lower_ref):
    core, col = lax.axis_index("gz") & 1, lax.axis_index("col")
    block = own_ref.shape[3]
    for d, ref in enumerate((own_ref, col_ref, core_ref, both_ref)):
        quarter = piece((core ^ d >> 1) * 2 + (col ^ d & 1), block)
        for r in range(own_ref.shape[0]):
            at = pl.ds(r * block, block)
            front_ref[at, quarter] = ref[r, 0]
            last_ref[at, quarter] = ref[r, 1]
            lower_ref[quarter, at] = ref[r, 2]


def on_first_row(rhs):
    return jnp.where(lax.axis_index("row") == 0, rhs, 0.0)


def top_blocks_kernel(rhs_ref, top_ref, other_ref, inv_ref, late_ref, late_other_ref, blocks_ref, out_ref, given_ref, ready):
    col, part = lax.axis_index("col"), top_ref.shape[1]
    block = blocks_ref.shape[2]
    for i in range(4):
        total = top_ref[i] + other_ref[i].astype(F32)
        ready[pl.ds(i * part, part)] = (on_first_row(rhs_ref[0, piece(i * 2 + col, part)]) - total).astype(BF16)
    solved = times_transposed(ready[...], inv_ref[...])
    for r in range(blocks_ref.shape[0]):
        blocks_ref[r] = solved[:, r * block : (r + 1) * block].astype(BF16)
    for k in (0, 1):
        for half in (0, 1):
            for ref, side in ((out_ref, col), (given_ref, 1 - col)):
                at = piece(side, part)
                total = late_ref[k, half, at] + late_other_ref[k, half, at].astype(F32)
                ref[k, half] = total.astype(ref.dtype)


def top_up_kernel(blocks_ref, lower_ref, late_ref, late_other_ref, solved_ref, send_ref, kept_ref, given_ref, total):
    core = lax.axis_index("gz") & 1
    part = solved_ref.shape[1]
    solved = sum(blocks_ref[r].astype(F32) for r in range(blocks_ref.shape[0]))
    rounded = solved.astype(BF16)
    for i in range(4):
        solved_ref[i] = solved[i * part : (i + 1) * part]
        send_ref[i] = rounded[i * part : (i + 1) * part]
    for k in (0, 1):
        total[...] = times_transposed(rounded, lower_ref[0, k])
        for half in (0, 1):
            late = late_ref[k, half] + late_other_ref[k, half].astype(F32)
            kept_ref[k, half] = total[piece(half * 2 + core, part)] + late
            given_ref[k, half] = total[piece(half * 2 + 1 - core, part)].astype(BF16)


def apex_rows(rhs_ref, which, half, part):
    core, col = lax.axis_index("gz") & 1, lax.axis_index("col")
    return on_first_row(rhs_ref[which, piece(half * 4 + core * 2 + col, part)])


def front_kernel(rhs_ref, kept_ref, other_ref, inv_ref, lower_ref, front_ref, last_ref, given_ref, ready, fronts, ups):
    pair, part = lax.axis_index("gz") >> 1, last_ref.shape[0]
    for half in (0, 1):
        total = kept_ref[0, half] + other_ref[0, half].astype(F32)
        ready[pl.ds(half * part, part)] = (apex_rows(rhs_ref, pair, half, part) - total).astype(BF16)
    fronts[...] = times_transposed(ready[...], inv_ref[...])
    front_ref[...] = fronts[piece(pair, part)].astype(BF16)
    given_ref[0] = fronts[piece(1 - pair, part)].astype(BF16)
    ups[...] = times_transposed(fronts[...].astype(BF16), lower_ref[...])
    for half in (0, 1):
        ups[pl.ds(half * part, part)] += kept_ref[1, half] + other_ref[1, half].astype(F32)
    last_ref[...] = ups[piece(pair, part)]
    given_ref[1] = ups[piece(1 - pair, part)].astype(BF16)


def last_kernel(rhs_ref, inv_ref, front_ref, last_ref, other_ref, top_ref, other_top_ref, blocks_ref, top_all_ref):
    pair, col, part = lax.axis_index("gz") >> 1, lax.axis_index("col"), last_ref.shape[0]
    block = blocks_ref.shape[3]
    ready = (apex_rows(rhs_ref, 2, pair, part) - (last_ref[...] + other_ref[1].astype(F32))).astype(BF16)
    solved = times_transposed(ready, inv_ref[...])
    for r in range(blocks_ref.shape[0]):
        at = slice(r * block, (r + 1) * block)
        blocks_ref[r, 2] = solved[:, at].astype(BF16)
        blocks_ref[r, pair] = front_ref[:, at]
        blocks_ref[r, 1 - pair] = other_ref[0, :, at]
    for i in range(top_ref.shape[0]):
        top_all_ref[0, piece(i * 2 + col, part)] = top_ref[i]
        top_all_ref[0, piece(i * 2 + 1 - col, part)] = other_top_ref[i].astype(F32)


def apex_sum_kernel(blocks_ref, solved_ref, send_ref):
    solved = sum(blocks_ref[r].astype(F32) for r in range(blocks_ref.shape[0]))
    solved_ref[...] = solved
    send_ref[...] = solved.astype(BF16)


def place_apex_kernel(solved_ref, other_ref, apex_ref):
    col, part = lax.axis_index("col"), solved_ref.shape[1]
    for k in range(3):
        apex_ref[k, piece(col, part)] = solved_ref[k]
        apex_ref[k, piece(1 - col, part)] = other_ref[k].astype(F32)


def two_cols(
    leaf_rhs,
    leaf_inv,
    leaf_lower_mid,
    leaf_lower_coupling,
    leaf_parent,
    leaf_pattern,
    mid_rhs,
    parent_diagonal_inverse,
    mid_lower,
    mid_pattern,
    top_rhs,
    top_inv,
    top_lower,
    apex_rhs,
    apex_inv,
    apex_lower,
):
    count, size = leaf_rhs.shape[1:]
    width = leaf_inv.shape[1]
    quarter, part = count // 4, count // 8

    rows = lax.axis_size("row")
    leaf_solved, leaf_round, terms, other_terms = leaf_solve(leaf_parent, leaf_rhs, leaf_inv, leaf_lower_mid, 2)
    (other_terms,) = partners(other_terms, [{"col": 1}])
    layer_up = leaf_coupling(leaf_pattern, leaf_round, leaf_lower_coupling)

    (share,) = whole_call(
        repeat_top_kernel, "repeat_top", [top_inv], [((rows, 2, width, width), BF16)], after=[leaf_round]
    )
    top_share = exchange(share, "row")

    kept, *given = whole_call(
        mid_pieces_kernel, "mid_pieces", [terms, other_terms],
        [((quarter, size), F32)] + [((quarter, size), BF16)] * 3,
        after=[top_share],
    )
    arrived = partners(given, ROW_MOVES)
    (top_other,) = partners(top_share, [{"col": 1}])
    (ready,) = whole_call(mid_total_kernel, "mid_total", [mid_rhs, kept, *arrived], [((quarter, size), BF16)])
    arrived = partners(ready, ROW_MOVES)
    (top_whole,) = whole_call(whole_top_kernel, "whole_top", [top_share, top_other], [((size, size), BF16)])
    mid_solved, kept, given, late_kept, late_given = whole_call(
        mid_solve_kernel, "mid_solve", [mid_pattern, ready, *arrived, parent_diagonal_inverse, mid_lower, layer_up],
        [((count, width), F32), ((4, part, size), F32), ((4, part, size), BF16)]
        + [((2, 2, quarter, size), F32), ((2, 2, quarter, size), BF16)],
        flops=8 * count * size * width,
        scratch=[pltpu.VMEM((count, width), BF16), pltpu.VMEM((count, size), F32)],
        scalars=1,
        after=[top_whole],
    )

    (other,) = partners(given, [{"col": 1}])
    (late_other,) = partners(late_given, [{"gz": 1}])
    (share,) = whole_call(
        repeat_apex_kernel, "repeat_apex", [apex_inv, apex_lower], [((rows, 3, width, width), BF16)], after=[given]
    )
    apex_share = exchange(share, "row")
    blocks, late_kept, late_given = whole_call(
        top_blocks_kernel, "top_blocks", [top_rhs, kept, other, top_whole, late_kept, late_other],
        [((rows, count // 2, width), BF16), ((2, 2, part, size), F32), ((2, 2, part, size), BF16)],
        flops=count * size * size,
        scratch=[pltpu.VMEM((count // 2, size), BF16)],
    )
    blocks = exchange(blocks, "row")
    (late_other,) = partners(late_given, [{"col": 1}])
    apex_share, _ = lax.optimization_barrier((apex_share, other))
    (apex_col,) = partners(apex_share, [{"col": 1}])
    apex_share, apex_col, blocks = lax.optimization_barrier((apex_share, apex_col, blocks))
    top_solved, top_send, kept, given = whole_call(
        top_up_kernel, "top_up", [blocks, top_lower, late_kept, late_other],
        [((4, part, width), F32), ((4, part, width), BF16), ((2, 2, part, size), F32), ((2, 2, part, size), BF16)],
        flops=2 * count * size * width,
        scratch=[pltpu.VMEM((4 * part, size), F32)],
    )
    (other,) = partners(given, [{"gz": 1}])
    (other_top,) = partners(top_send, [{"col": 1}])

    (apex_core,) = partners(apex_share, [{"gz": 1}])
    (apex_both,) = partners(apex_col, [{"gz": 1}])
    front_whole, last_whole, lower_whole = whole_call(
        whole_apex_kernel, "whole_apex", [apex_share, apex_col, apex_core, apex_both], [((size, size), BF16)] * 3
    )
    front, last, given = whole_call(
        front_kernel, "front", [apex_rhs, kept, other, front_whole, lower_whole],
        [((part, size), BF16), ((part, size), F32), ((2, part, size), BF16)],
        flops=count * size * size,
        scratch=[pltpu.VMEM((2 * part, size), BF16)] + [pltpu.VMEM((2 * part, size), F32)] * 2,
    )
    (other,) = partners(given, [{"gz": 2}])
    blocks, top_all = whole_call(
        last_kernel, "last", [apex_rhs, last_whole, front, last, other, top_solved, other_top],
        [((rows, 3, part, width), BF16), ((1, count, width), F32)],
        flops=count * size * size // 4,
    )
    solved, send = whole_call(
        apex_sum_kernel, "apex_sum", [exchange(blocks, "row")], [((3, part, width), F32), ((3, part, width), BF16)]
    )
    (other,) = partners(send, [{"col": 1}])
    (apex,) = whole_call(place_apex_kernel, "place_apex", [solved, other], [((3, 2 * part, width), F32)])
    return (leaf_solved, mid_solved[None], top_all, apex)


def solution(mesh):
    placed = (
        P(("gz", "col"), None, None),
        P(("gz", "col"), "row", None),
        P(("gz", "col"), None, "row"),
        P(("gz", "col"), None, None, "row"),
        P(("gz", "col")),
        P(("gz", "col"), None),
        P(("gz", "col"), None, None),
        P(("gz", "col"), "row", None),
        P(("gz", "col"), None, None, "row"),
        P(("gz", "col"), None),
        P("gz", None, None),
        P("gz", "row", None),
        P("gz", None, None, "row"),
        P(),
        P(None, "row", None),
        P(None, None, "row"),
    )
    return jax.shard_map(
        two_cols if mesh.shape["col"] == 2 else any_cols,
        mesh=mesh,
        in_specs=placed,
        out_specs=(
            P(("gz", "col"), None, "row"),
            P(("gz", "col"), None, "row"),
            P("gz", None, "row"),
            P(None, "gz", "row"),
        ),
        check_vma=False,
    )
```

```python
import functools
import math

import jax
import jax.numpy as jnp
from jax import lax
from jax.experimental import pallas as pl
from jax.experimental.pallas import tpu as pltpu
from jax.sharding import PartitionSpec as P

BF16 = jnp.bfloat16
F32 = jnp.float32
VMEM_BYTES = 56 * 1024 * 1024
STEP_VMEM_BYTES = 16 * 1024 * 1024


def times_transposed(left, right):
    return lax.dot_general(left, right, (((1,), (1,)), ((), ())), preferred_element_type=F32)


def leaf_kernel(
    slots, parent_ref, rhs_ref, inv_ref, mid_ref, solved_ref, round_ref, *rest
):
    terms_refs, (rhs, inv, mid, solved, total, rhs_sems, inv_sems, mid_sem, out_sems) = rest[:slots], rest[slots:]
    leaves = rhs.shape[0]
    first = lax.axis_index("col") if slots == 2 else 0
    rhs_copies = [pltpu.make_async_copy(rhs_ref.at[i], rhs.at[i], rhs_sems.at[i]) for i in range(leaves)]
    inv_copies = [pltpu.make_async_copy(inv_ref.at[i], inv.at[i], inv_sems.at[i]) for i in range(leaves)]
    mid_copy = pltpu.make_async_copy(mid_ref, mid, mid_sem)
    for i in range(leaves):
        inv_copies[i].start()
        rhs_copies[i].start()
    mid_copy.start()
    out_copies = []
    for i in range(leaves):
        inv_copies[i].wait()
        rhs_copies[i].wait()
        solved[i] = times_transposed(rhs[i].astype(BF16), inv[i])
        out_copies.append(pltpu.make_async_copy(solved.at[i], solved_ref.at[i], out_sems.at[i]))
        out_copies[i].start()
        round_ref[i] = solved[i].astype(BF16)
    mid_copy.wait()
    if slots == 2:
        right = jnp.concatenate([mid[i] for i in range(leaves)], axis=1)
        for s, ref in enumerate(terms_refs):
            weights = [jnp.where(parent_ref[i] ^ first == s, 1.0, 0.0).astype(BF16) for i in range(leaves)]
            left = jnp.concatenate([round_ref[i] * weights[i] for i in range(leaves)], axis=1)
            ref[...] = times_transposed(left, right).astype(ref.dtype)
    else:
        total[...] = jnp.zeros_like(total)
        for i in range(leaves):
            total[parent_ref[i]] += times_transposed(round_ref[i], mid[i])
        for s, ref in enumerate(terms_refs):
            ref[...] = total[s].astype(ref.dtype)
    for copy in out_copies:
        copy.wait()


def leaf_solve(parent, rhs, inv, lower_mid, slots):
    leaves, rows, size = rhs.shape
    width = inv.shape[1]
    hbm, vmem = pl.BlockSpec(memory_space=pltpu.HBM), pl.BlockSpec(memory_space=pltpu.VMEM)
    return pl.pallas_call(
        functools.partial(leaf_kernel, slots),
        in_specs=[pl.BlockSpec(memory_space=pltpu.SMEM), hbm, hbm, hbm],
        out_specs=[hbm] + [vmem] * (1 + slots),
        out_shape=[
            jax.ShapeDtypeStruct((leaves, rows, width), F32),
            jax.ShapeDtypeStruct((leaves, rows, width), BF16),
        ]
        + [jax.ShapeDtypeStruct((rows, size), BF16)] * slots,
        scratch_shapes=[
            pltpu.VMEM(rhs.shape, F32),
            pltpu.VMEM(inv.shape, BF16),
            pltpu.VMEM(lower_mid.shape, BF16),
            pltpu.VMEM((leaves, rows, width), F32),
            pltpu.VMEM((8, 128) if slots == 2 else (slots, rows, size), F32),
            pltpu.SemaphoreType.DMA((leaves,)),
            pltpu.SemaphoreType.DMA((leaves,)),
            pltpu.SemaphoreType.DMA,
            pltpu.SemaphoreType.DMA((leaves,)),
        ],
        compiler_params=pltpu.CompilerParams(vmem_limit_bytes=VMEM_BYTES),
        cost_estimate=pl.CostEstimate(
            flops=4 * leaves * rows * size * width,
            bytes_accessed=leaves * (rows * size * 4 + 4 * width * size + rows * width * 6),
            transcendentals=0,
        ),
        name="leaf_solve",
    )(parent, rhs, inv, lower_mid)


def coupling_kernel(pattern_ref, round_ref, lower_ref, up_ref, rounded, lower, round_sem, sems):
    leaves, kinds = lower.shape[:2]
    round_copy = pltpu.make_async_copy(round_ref, rounded, round_sem)
    round_copy.start()
    copies = [pltpu.make_async_copy(lower_ref.at[:, k], lower.at[:, k], sems.at[k]) for k in range(kinds)]
    for copy in copies:
        copy.start()
    round_copy.wait()
    for k in range(kinds):
        copies[k].wait()
        left = [rounded[i] * pattern_ref[i, k].astype(F32).astype(BF16) for i in range(leaves)]
        right = [lower[i, k] for i in range(leaves)]
        up_ref[k] = times_transposed(jnp.concatenate(left, axis=1), jnp.concatenate(right, axis=1))


def leaf_coupling(pattern, rounded, lower):
    leaves, rows, width = rounded.shape
    kinds, size = lower.shape[1:3]
    hbm = pl.BlockSpec(memory_space=pltpu.HBM)
    return pl.pallas_call(
        coupling_kernel,
        in_specs=[pl.BlockSpec(memory_space=pltpu.SMEM), hbm, hbm],
        out_specs=pl.BlockSpec(memory_space=pltpu.VMEM),
        out_shape=jax.ShapeDtypeStruct((kinds, rows, size), F32),
        scratch_shapes=[
            pltpu.VMEM(rounded.shape, BF16),
            pltpu.VMEM(lower.shape, BF16),
            pltpu.SemaphoreType.DMA,
            pltpu.SemaphoreType.DMA((kinds,)),
        ],
        compiler_params=pltpu.CompilerParams(vmem_limit_bytes=STEP_VMEM_BYTES),
        cost_estimate=pl.CostEstimate(
            flops=2 * leaves * kinds * rows * size * width,
            bytes_accessed=leaves * (rows * width * 2 + kinds * size * width * 2) + kinds * rows * size * 4,
            transcendentals=0,
        ),
        name="leaf_coupling",
    )(pattern, rounded, lower)


def swap(block, axis, bit):
    count = lax.axis_size(axis)
    return lax.ppermute(block, axis, [(i, i ^ 1 << bit) for i in range(count)])


def swap_sum(halves, axis, bit):
    here = lax.axis_index(axis) >> bit & 1
    kept = lax.dynamic_index_in_dim(halves, here, 0, keepdims=False)
    given = lax.dynamic_index_in_dim(halves, 1 - here, 0, keepdims=False)
    return kept.astype(F32) + swap(given.astype(BF16), axis, bit).astype(F32)


def exchange(pieces, axis):
    return lax.all_to_all(pieces, axis, split_axis=0, concat_axis=0, tiled=True)


def scatter_sum(pieces, axis):
    return jnp.sum(exchange(pieces.astype(BF16), axis).astype(F32), axis=0)


def col_sum(pieces):
    if pieces.shape[0] == 2:
        return swap_sum(pieces, "col", 0)
    return scatter_sum(pieces, "col")


def spread(piece, axis):
    count = lax.axis_size(axis)
    return exchange(jnp.broadcast_to(piece[None], (count,) + piece.shape), axis)


def col_spread(piece):
    if lax.axis_size("col") == 2:
        other = swap(piece, "col", 0)
        first = lax.axis_index("col") == 0
        return jnp.stack([jnp.where(first, piece, other), jnp.where(first, other, piece)])
    return spread(piece, "col")


def any_cols(
    leaf_rhs,
    leaf_inv,
    leaf_lower_mid,
    leaf_lower_coupling,
    leaf_parent,
    leaf_pattern,
    mid_rhs,
    parent_diagonal_inverse,
    mid_lower,
    mid_pattern,
    top_rhs,
    top_inv,
    top_lower,
    apex_rhs,
    apex_inv,
    apex_lower,
):
    cols = lax.axis_size("col")
    rows = lax.axis_size("row")
    col = lax.axis_index("col")
    row = lax.axis_index("row")
    gz = lax.axis_index("gz")
    pair, core = gz // 2, gz % 2
    rhs_count, size = leaf_rhs.shape[1:]
    part = rhs_count // (4 * cols)

    leaf_solved, leaf_round, *terms = leaf_solve(leaf_parent, leaf_rhs, leaf_inv, leaf_lower_mid, cols)
    if cols == 2:
        mid_part = terms[0].astype(F32) + swap(terms[1], "col", 0).astype(F32)
    else:
        mid_part = scatter_sum(jnp.stack(terms), "col")
    layer_up = leaf_coupling(leaf_pattern, leaf_round, leaf_lower_coupling)
    quarter = rhs_count // rows
    mid_sum = scatter_sum(mid_part.reshape(rows, quarter, size), "row")
    mid_total = lax.dynamic_slice_in_dim(mid_rhs[0], row * quarter, quarter, 0) - mid_sum
    mid_ready = spread(mid_total.astype(BF16), "row").reshape(rhs_count, size)
    mid_solved = times_transposed(mid_ready, parent_diagonal_inverse[0])
    mid_round = mid_solved.astype(BF16)
    mid_weight = mid_pattern[0].astype(F32)

    top_part = layer_up[0] + times_transposed(mid_round, mid_lower[0, 0])
    top_part = top_part.astype(BF16).reshape(rows, cols, part, size).swapaxes(0, 1)
    top_sum = scatter_sum(top_part.reshape(rows * cols, part, size), ("col", "row"))
    top_start = (row * cols + col) * part
    top_total = lax.dynamic_slice_in_dim(top_rhs[0], top_start, part, 0) - top_sum
    top_ready = spread(top_total.astype(BF16), "row").reshape(rows * part, size)
    top_solved = times_transposed(top_ready, top_inv[0])
    top_round = top_solved.astype(BF16)

    late = jnp.stack([layer_up[k] + mid_weight[k - 1] * times_transposed(mid_round, mid_lower[0, k]) for k in (1, 2)])
    late = late.reshape(2, 2, 2, cols, part, size)
    late = swap_sum(late.transpose(2, 0, 1, 3, 4, 5), "gz", 0)
    late = col_sum(late.transpose(2, 0, 1, 3, 4))

    up = jnp.stack([times_transposed(top_round, top_lower[0, k]) for k in (0, 1)])
    up = swap_sum(up.reshape(2, 2, 2, part, size).transpose(2, 0, 1, 3, 4), "gz", 0) + late
    half = part // 2
    front_sum = scatter_sum(up[0].reshape(rows, half, size), "row")
    front_start = row // 2 * (rhs_count // 2) + (core * cols + col) * part + row % 2 * half
    front_rhs = lax.dynamic_slice(apex_rhs, (pair, front_start, 0), (1, half, size))[0]
    front_ready = spread((front_rhs - front_sum).astype(BF16), "row").reshape(2 * part, size)
    front_inv = lax.dynamic_index_in_dim(apex_inv, pair, 0, keepdims=False)
    front_lower = lax.dynamic_index_in_dim(apex_lower, pair, 0, keepdims=False)
    front_solved = times_transposed(front_ready, front_inv)

    own_up = times_transposed(front_solved.astype(BF16), front_lower)
    last_part = swap_sum(up[1] + own_up.reshape(2, part, size), "gz", 1)
    last_sum = jnp.sum(spread(last_part.astype(BF16), "row").astype(F32), axis=0)
    last_start = (pair * 2 * cols + core * cols + col) * part
    last_rhs = lax.dynamic_slice_in_dim(apex_rhs[2], last_start, part, 0)
    last_solved = times_transposed((last_rhs - last_sum).astype(BF16), apex_inv[2])

    width = last_solved.shape[1]
    front_solved = front_solved.reshape(2, part, width)
    own_front = lax.dynamic_index_in_dim(front_solved, pair, 0, keepdims=False)
    other_front = swap(lax.dynamic_index_in_dim(front_solved, 1 - pair, 0, keepdims=False), "gz", 1)
    leading = pair == 0
    fronts = jnp.stack([jnp.where(leading, own_front, other_front), jnp.where(leading, other_front, own_front)])
    fronts = col_spread(fronts).swapaxes(0, 1).reshape(2, cols * part, width)
    last = col_spread(last_solved).reshape(1, cols * part, width)
    top_all = col_spread(top_solved.reshape(rows, part, width)).swapaxes(0, 1).reshape(1, rhs_count, width)
    return (leaf_solved, mid_solved[None], top_all, jnp.concatenate([fronts, last], axis=0))


def partners(block, moves):
    blocks = block if isinstance(block, (list, tuple)) else [block] * len(moves)
    arrived = []
    for item, move in zip(blocks, moves):
        axes = tuple(move)
        sizes = [lax.axis_size(axis) for axis in axes]
        route = []
        for source in range(math.prod(sizes)):
            place, rest = [], source
            for count in reversed(sizes):
                place.insert(0, rest % count)
                rest //= count
            target = 0
            for at, count, axis in zip(place, sizes, axes):
                target = target * count + (at ^ move[axis])
            route.append((source, target))
        arrived.append(lax.ppermute(item, axes, route))
    return arrived


def whole_call(kernel, name, operands, results, flops=0, scratch=(), scalars=0, after=()):
    moved = sum(math.prod(a.shape) * a.dtype.itemsize for a in operands)
    moved += sum(math.prod(shape) * jnp.dtype(kind).itemsize for shape, kind in results)
    smem, vmem = pl.BlockSpec(memory_space=pltpu.SMEM), pl.BlockSpec(memory_space=pltpu.VMEM)

    def body(*refs):
        kernel(*refs[len(after) :])

    return pl.pallas_call(
        body,
        in_specs=[pl.BlockSpec(memory_space=pl.ANY)] * len(after)
        + [smem] * scalars
        + [vmem] * (len(operands) - scalars),
        out_specs=[vmem] * len(results),
        out_shape=[jax.ShapeDtypeStruct(shape, kind) for shape, kind in results],
        scratch_shapes=list(scratch),
        compiler_params=pltpu.CompilerParams(vmem_limit_bytes=STEP_VMEM_BYTES),
        cost_estimate=pl.CostEstimate(flops=flops, bytes_accessed=moved, transcendentals=0),
        name=name,
    )(*after, *operands)


def piece(index, length):
    return pl.ds(pl.multiple_of(index * length, length), length)


def widened(*refs):
    total = refs[0][...].astype(F32)
    for ref in refs[1:]:
        total = total + ref[...].astype(F32)
    return total


ROW_MOVES = [{"row": d} for d in (3, 2, 1)]


def mid_pieces_kernel(terms_ref, other_ref, kept_ref, *given_refs):
    row, length = lax.axis_index("row"), kept_ref.shape[0]
    for d, ref in zip((0, 3, 2, 1), (kept_ref,) + given_refs):
        at = piece(row ^ d, length)
        ref[...] = (terms_ref[at].astype(F32) + other_ref[at].astype(F32)).astype(ref.dtype)


def mid_total_kernel(rhs_ref, kept_ref, r1, r2, r3, ready_ref):
    at = piece(lax.axis_index("row"), ready_ref.shape[0])
    ready_ref[...] = (rhs_ref[0, at] - widened(kept_ref, r1, r2, r3)).astype(BF16)


def mid_solve_kernel(
    pattern_ref, p0, p3, p2, p1, inv_ref, lower_ref, up_ref,
    solved_ref, top_ref, top_given_ref, late_ref, late_given_ref, rounded, total,
):
    row, col, core = lax.axis_index("row"), lax.axis_index("col"), lax.axis_index("gz") & 1
    length, part = p0.shape[0], top_ref.shape[1]
    for d, ref in zip((0, 3, 2, 1), (p0, p3, p2, p1)):
        at = piece(row ^ d, length)
        solved = times_transposed(ref[...], inv_ref[0])
        solved_ref[at] = solved
        rounded[at] = solved.astype(BF16)
    total[...] = up_ref[0] + times_transposed(rounded[...], lower_ref[0, 0])
    for i in range(4):
        top_ref[i] = total[piece(i * 2 + col, part)]
        top_given_ref[i] = total[piece(i * 2 + 1 - col, part)].astype(BF16)
    for k in (1, 2):
        weight = pattern_ref[0, k - 1].astype(F32)
        total[...] = up_ref[k] + weight * times_transposed(rounded[...], lower_ref[0, k])
        for half in (0, 1):
            late_ref[k - 1, half] = total[piece(half * 2 + core, length)]
            late_given_ref[k - 1, half] = total[piece(half * 2 + 1 - core, length)].astype(BF16)


def top_share_kernel(terms_ref, inv_ref, own_ref, share_ref):
    own_ref[...] = terms_ref[...]
    length = share_ref.shape[1]
    share_ref[...] = inv_ref[0, :, piece(lax.axis_index("col"), length)]


def half_top_kernel(p0, p3, p2, p1, half_ref):
    row = lax.axis_index("row")
    for d, ref in zip((0, 3, 2, 1), (p0, p3, p2, p1)):
        half_ref[piece(row ^ d, ref.shape[0])] = ref[...]


def whole_top_kernel(own_ref, other_ref, whole_ref):
    col, length = lax.axis_index("col"), own_ref.shape[1]
    whole_ref[:, piece(col, length)] = own_ref[...]
    whole_ref[:, piece(1 - col, length)] = other_ref[...]


def on_first_row(rhs):
    return jnp.where(lax.axis_index("row") == 0, rhs, 0.0)


def late_pieces_kernel(late_ref, other_ref, out_ref, given_ref):
    col, part = lax.axis_index("col"), out_ref.shape[2]
    for k in (0, 1):
        for half in (0, 1):
            for ref, side in ((out_ref, col), (given_ref, 1 - col)):
                at = piece(side, part)
                total = late_ref[k, half, at] + other_ref[k, half, at].astype(F32)
                ref[k, half] = total.astype(ref.dtype)


def top_blocks_kernel(rhs_ref, top_ref, other_ref, inv_ref, kept_ref, g3, g2, g1, ready, solved):
    row, col, part = lax.axis_index("row"), lax.axis_index("col"), top_ref.shape[1]
    for i in range(4):
        total = top_ref[i] + other_ref[i].astype(F32)
        ready[pl.ds(i * part, part)] = (on_first_row(rhs_ref[0, piece(i * 2 + col, part)]) - total).astype(BF16)
    solved[...] = times_transposed(ready[...], inv_ref[...])
    for d, ref in zip((0, 3, 2, 1), (kept_ref, g3, g2, g1)):
        ref[...] = solved[:, piece(row ^ d, ref.shape[1])].astype(ref.dtype)


def top_up_kernel(
    kept_ref, r3, r2, r1, lower_ref, late_ref, late_other_ref, solved_ref, send_ref, out_ref, given_ref, total
):
    core = lax.axis_index("gz") & 1
    part = solved_ref.shape[1]
    solved = widened(kept_ref, r3, r2, r1)
    rounded = solved.astype(BF16)
    for i in range(4):
        solved_ref[i] = solved[i * part : (i + 1) * part]
        send_ref[i] = rounded[i * part : (i + 1) * part]
    for k in (0, 1):
        total[...] = times_transposed(rounded, lower_ref[0, k])
        for half in (0, 1):
            late = late_ref[k, half] + late_other_ref[k, half].astype(F32)
            out_ref[k, half] = total[piece(half * 2 + core, part)] + late
            given_ref[k, half] = total[piece(half * 2 + 1 - core, part)].astype(BF16)


def front_pieces_kernel(kept_ref, other_ref, own_ref, send_ref, last_ref):
    part = kept_ref.shape[2]
    for half in (0, 1):
        at = pl.ds(half * part, part)
        total = kept_ref[0, half] + other_ref[0, half].astype(F32)
        own_ref[at] = total
        send_ref[at] = total.astype(BF16)
        last_ref[half] = kept_ref[1, half] + other_ref[1, half].astype(F32)


def apex_rows(rhs_ref, which, half, part):
    core, col = lax.axis_index("gz") & 1, lax.axis_index("col")
    return rhs_ref[which, piece(half * 4 + core * 2 + col, part)]


def front_solve_kernel(rhs_ref, own_ref, r3, r2, r1, inv_ref, lower_ref, last_ref, front_ref, kept_ref, given_ref, total, fronts):
    pair = lax.axis_index("gz") >> 1
    part, size = kept_ref.shape
    rhs = jnp.concatenate([apex_rows(rhs_ref, pair, half, part) for half in (0, 1)])
    ready = (rhs - widened(own_ref, r3, r2, r1)).astype(BF16)
    fronts[...] = times_transposed(ready, inv_ref[pair])
    total[...] = times_transposed(fronts[...].astype(BF16), lower_ref[pair])
    front_ref[...] = fronts[piece(pair, part)]
    kept_ref[...] = total[piece(pair, part)] + last_ref[pair]
    given_ref[:, :size] = (total[piece(1 - pair, part)] + last_ref[1 - pair]).astype(BF16)
    given_ref[:, size:] = fronts[piece(1 - pair, part)].astype(BF16)


def last_pieces_kernel(kept_ref, other_ref, own_ref, send_ref):
    total = kept_ref[...] + other_ref[:, : own_ref.shape[1]].astype(F32)
    own_ref[...] = total
    send_ref[...] = total.astype(BF16)


def last_solve_kernel(
    rhs_ref, inv_ref, own_ref, r3, r2, r1, front_ref, other_ref, top_ref, other_top_ref, solved_ref, send_ref, top_all_ref
):
    pair, col = lax.axis_index("gz") >> 1, lax.axis_index("col")
    part, size = own_ref.shape
    ready = (apex_rows(rhs_ref, 2, pair, part) - widened(own_ref, r3, r2, r1)).astype(BF16)
    solved_ref[2] = times_transposed(ready, inv_ref[2])
    solved_ref[pair] = front_ref[...]
    solved_ref[1 - pair] = other_ref[:, size:].astype(F32)
    send_ref[...] = solved_ref[...].astype(BF16)
    for i in range(top_ref.shape[0]):
        top_all_ref[0, piece(i * 2 + col, part)] = top_ref[i]
        top_all_ref[0, piece(i * 2 + 1 - col, part)] = other_top_ref[i].astype(F32)


def place_apex_kernel(solved_ref, other_ref, apex_ref):
    col, part = lax.axis_index("col"), solved_ref.shape[1]
    for k in range(3):
        apex_ref[k, piece(col, part)] = solved_ref[k]
        apex_ref[k, piece(1 - col, part)] = other_ref[k].astype(F32)


def two_cols(
    leaf_rhs,
    leaf_inv,
    leaf_lower_mid,
    leaf_lower_coupling,
    leaf_parent,
    leaf_pattern,
    mid_rhs,
    parent_diagonal_inverse,
    mid_lower,
    mid_pattern,
    top_rhs,
    top_inv,
    top_lower,
    apex_rhs,
    apex_inv,
    apex_lower,
):
    count, size = leaf_rhs.shape[1:]
    width = leaf_inv.shape[1]
    quarter, part = count // 4, count // 8

    rows = lax.axis_size("row")

    leaf_solved, leaf_round, terms, other_terms = leaf_solve(leaf_parent, leaf_rhs, leaf_inv, leaf_lower_mid, 2)
    (other_terms,) = partners(other_terms, [{"col": 1}])
    layer_up = leaf_coupling(leaf_pattern, leaf_round, leaf_lower_coupling)

    terms, share = whole_call(
        top_share_kernel, "top_share", [terms, top_inv], [((count, size), BF16), ((width, size // 2), BF16)]
    )
    shares = partners(share, ROW_MOVES)

    kept, *given = whole_call(
        mid_pieces_kernel, "mid_pieces", [terms, other_terms],
        [((quarter, size), F32)] + [((quarter, size), BF16)] * 3,
        after=shares,
    )
    arrived = partners(given, ROW_MOVES)
    (top_half,) = whole_call(half_top_kernel, "half_top", [share, *shares], [((size, size // 2), BF16)], after=[kept])
    (top_other,) = partners(top_half, [{"col": 1}])
    (ready,) = whole_call(mid_total_kernel, "mid_total", [mid_rhs, kept, *arrived], [((quarter, size), BF16)])
    arrived = partners(ready, ROW_MOVES)
    (top_whole,) = whole_call(whole_top_kernel, "whole_top", [top_half, top_other], [((size, size), BF16)])
    mid_solved, kept, given, late_kept, late_given = whole_call(
        mid_solve_kernel, "mid_solve", [mid_pattern, ready, *arrived, parent_diagonal_inverse, mid_lower, layer_up],
        [((count, width), F32), ((4, part, size), F32), ((4, part, size), BF16)]
        + [((2, 2, quarter, size), F32), ((2, 2, quarter, size), BF16)],
        flops=8 * count * size * width,
        scratch=[pltpu.VMEM((count, width), BF16), pltpu.VMEM((count, size), F32)],
        scalars=1,
        after=[top_whole],
    )

    (other,) = partners(given, [{"col": 1}])
    (late_other,) = partners(late_given, [{"gz": 1}])
    late_kept, late_given = whole_call(
        late_pieces_kernel, "late_pieces", [late_kept, late_other],
        [((2, 2, part, size), F32), ((2, 2, part, size), BF16)],
    )
    (late_other,) = partners(late_given, [{"col": 1}])
    kept, *given = whole_call(
        top_blocks_kernel, "top_blocks", [top_rhs, kept, other, top_whole],
        [((count // 2, width), F32)] + [((count // 2, width), BF16)] * 3,
        flops=count * size * size,
        scratch=[pltpu.VMEM((count // 2, size), BF16), pltpu.VMEM((count // 2, size), F32)],
        after=[late_given],
    )
    arrived = partners(given, ROW_MOVES)
    top_solved, top_send, kept, given = whole_call(
        top_up_kernel, "top_up", [kept, *arrived, top_lower, late_kept, late_other],
        [((4, part, width), F32), ((4, part, width), BF16), ((2, 2, part, size), F32), ((2, 2, part, size), BF16)],
        flops=2 * count * size * width,
        scratch=[pltpu.VMEM((4 * part, size), F32)],
    )
    (other,) = partners(given, [{"gz": 1}])
    (other_top,) = partners(top_send, [{"col": 1}])

    own, send, last = whole_call(
        front_pieces_kernel, "front_pieces", [kept, other],
        [((2 * part, size), F32), ((2 * part, size), BF16), ((2, part, size), F32)],
    )
    arrived = partners(send, ROW_MOVES)
    front, kept, given = whole_call(
        front_solve_kernel, "front_solve", [apex_rhs, own, *arrived, apex_inv, apex_lower, last],
        [((part, width), F32), ((part, size), F32), ((part, size + width), BF16)],
        flops=count * size * width,
        scratch=[pltpu.VMEM((2 * part, size), F32), pltpu.VMEM((2 * part, width), F32)],
    )

    (other,) = partners(given, [{"gz": 2}])
    own, send = whole_call(
        last_pieces_kernel, "last_pieces", [kept, other], [((part, size), F32), ((part, size), BF16)]
    )
    arrived = partners(send, ROW_MOVES)
    solved, send, top_all = whole_call(
        last_solve_kernel, "last_solve",
        [apex_rhs, apex_inv, own, *arrived, front, other, top_solved, other_top],
        [((3, part, width), F32), ((3, part, width), BF16), ((1, count, width), F32)],
        flops=count * size * width // 4,
    )
    (other,) = partners(send, [{"col": 1}])
    (apex,) = whole_call(place_apex_kernel, "place_apex", [solved, other], [((3, 2 * part, width), F32)])
    return (leaf_solved, mid_solved[None], top_all, apex)


def solution(mesh):
    placed = (
        P(("gz", "col"), None, None),
        P(("gz", "col"), "row", None),
        P(("gz", "col"), None, "row"),
        P(("gz", "col"), None, None, "row"),
        P(("gz", "col")),
        P(("gz", "col"), None),
        P(("gz", "col"), None, None),
        P(("gz", "col"), "row", None),
        P(("gz", "col"), None, None, "row"),
        P(("gz", "col"), None),
        P("gz", None, None),
        P("gz", "row", None),
        P("gz", None, None, "row"),
        P(),
        P(None, "row", None),
        P(None, None, "row"),
    )
    return jax.shard_map(
        two_cols if mesh.shape["col"] == 2 else any_cols,
        mesh=mesh,
        in_specs=placed,
        out_specs=(
            P(("gz", "col"), None, "row"),
            P(("gz", "col"), None, "row"),
            P("gz", None, "row"),
            P(None, "gz", "row"),
        ),
        check_vma=False,
    )
```

```python
import functools
import math

import jax
import jax.numpy as jnp
from jax import lax
from jax.experimental import pallas as pl
from jax.experimental.pallas import tpu as pltpu
from jax.sharding import PartitionSpec as P

BF16 = jnp.bfloat16
F32 = jnp.float32
LEAF_VMEM_BYTES = 56 * 1024 * 1024
OWN_VMEM_BYTES = 52 * 1024 * 1024
LARGE_VMEM_BYTES = 50 * 1024 * 1024
STEP_VMEM_BYTES = 16 * 1024 * 1024


def times_transposed(left, right):
    return lax.dot_general(left, right, (((1,), (1,)), ((), ())), preferred_element_type=F32)


def masked_terms(parent_ref, wanted, rounded, mid):
    leaves = mid.shape[0]
    weights = [jnp.where(parent_ref[i] == wanted, 1.0, 0.0).astype(BF16) for i in range(leaves)]
    left = jnp.concatenate([rounded[i] * weights[i] for i in range(leaves)], axis=1)
    right = jnp.concatenate([mid[i] for i in range(leaves)], axis=1)
    return times_transposed(left, right)


def leaf_kernel(
    slots, parent_ref, rhs_ref, inv_ref, mid_ref, solved_ref, round_ref, *rest
):
    terms_refs = rest[: len(rest) - 11]
    rhs, inv, mid, solved, rounded, total, rhs_sems, inv_sems, mid_sem, out_sems, round_sems = rest[len(rest) - 11 :]
    leaves = rhs.shape[0]
    rhs_copies = [pltpu.make_async_copy(rhs_ref.at[i], rhs.at[i], rhs_sems.at[i]) for i in range(leaves)]
    inv_copies = [pltpu.make_async_copy(inv_ref.at[i], inv.at[i], inv_sems.at[i]) for i in range(leaves)]
    mid_copy = pltpu.make_async_copy(mid_ref, mid, mid_sem)
    for i in range(leaves):
        inv_copies[i].start()
        rhs_copies[i].start()
    mid_copy.start()
    out_copies = []
    for i in range(leaves):
        inv_copies[i].wait()
        rhs_copies[i].wait()
        solved[i] = times_transposed(rhs[i].astype(BF16), inv[i])
        rounded[i] = solved[i].astype(BF16)
        out_copies.append(pltpu.make_async_copy(solved.at[i], solved_ref.at[i], out_sems.at[i]))
        out_copies.append(pltpu.make_async_copy(rounded.at[i], round_ref.at[i], round_sems.at[i]))
        for copy in out_copies[-2:]:
            copy.start()
    mid_copy.wait()
    if slots == 2:
        terms_refs[0][...] = masked_terms(parent_ref, 1 - lax.axis_index("col"), rounded, mid).astype(BF16)
    else:
        total[...] = jnp.zeros_like(total)
        for i in range(leaves):
            total[parent_ref[i]] += times_transposed(rounded[i], mid[i])
        for s, ref in enumerate(terms_refs):
            ref[...] = total[s].astype(ref.dtype)
    for copy in out_copies:
        copy.wait()


def leaf_solve(parent, rhs, inv, lower_mid, slots):
    leaves, rows, size = rhs.shape
    width = inv.shape[1]
    given = 1 if slots == 2 else slots
    hbm, vmem = pl.BlockSpec(memory_space=pltpu.HBM), pl.BlockSpec(memory_space=pltpu.VMEM)
    return pl.pallas_call(
        functools.partial(leaf_kernel, slots),
        in_specs=[pl.BlockSpec(memory_space=pltpu.SMEM), hbm, hbm, hbm],
        out_specs=[hbm, hbm] + [vmem] * given,
        out_shape=[
            jax.ShapeDtypeStruct((leaves, rows, width), F32),
            jax.ShapeDtypeStruct((leaves, rows, width), BF16),
        ]
        + [jax.ShapeDtypeStruct((rows, size), BF16)] * given,
        scratch_shapes=[
            pltpu.VMEM(rhs.shape, F32),
            pltpu.VMEM(inv.shape, BF16),
            pltpu.VMEM(lower_mid.shape, BF16),
            pltpu.VMEM((leaves, rows, width), F32),
            pltpu.VMEM((leaves, rows, width), BF16),
            pltpu.VMEM((8, 128) if slots == 2 else (slots, rows, size), F32),
            pltpu.SemaphoreType.DMA((leaves,)),
            pltpu.SemaphoreType.DMA((leaves,)),
            pltpu.SemaphoreType.DMA,
            pltpu.SemaphoreType.DMA((leaves,)),
            pltpu.SemaphoreType.DMA((leaves,)),
        ],
        compiler_params=pltpu.CompilerParams(vmem_limit_bytes=LEAF_VMEM_BYTES),
        cost_estimate=pl.CostEstimate(
            flops=4 * leaves * rows * size * width,
            bytes_accessed=leaves * (rows * size * 4 + 4 * width * size + rows * width * 6),
            transcendentals=0,
        ),
        name="leaf_solve",
    )(parent, rhs, inv, lower_mid)


def own_terms_kernel(parent_ref, round_ref, mid_ref, rhs_ref, terms_ref, rhs_rows_ref, rounded, mid, sems):
    length = rhs_rows_ref.shape[0]
    copies = [
        pltpu.make_async_copy(round_ref, rounded, sems.at[0]),
        pltpu.make_async_copy(mid_ref, mid, sems.at[1]),
        pltpu.make_async_copy(rhs_ref.at[0, piece(lax.axis_index("row"), length)], rhs_rows_ref, sems.at[2]),
    ]
    for copy in copies:
        copy.start()
    for copy in copies:
        copy.wait()
    terms_ref[...] = masked_terms(parent_ref, lax.axis_index("col"), rounded, mid).astype(BF16)


def own_terms(parent, rounded, lower_mid, mid_rhs):
    rows, size = mid_rhs.shape[1:]
    hbm, vmem = pl.BlockSpec(memory_space=pltpu.HBM), pl.BlockSpec(memory_space=pltpu.VMEM)
    return pl.pallas_call(
        own_terms_kernel,
        in_specs=[pl.BlockSpec(memory_space=pltpu.SMEM), hbm, hbm, hbm],
        out_specs=[vmem, vmem],
        out_shape=[
            jax.ShapeDtypeStruct((rows, size), BF16),
            jax.ShapeDtypeStruct((rows // lax.axis_size("row"), size), F32),
        ],
        scratch_shapes=[
            pltpu.VMEM(rounded.shape, BF16),
            pltpu.VMEM(lower_mid.shape, BF16),
            pltpu.SemaphoreType.DMA((3,)),
        ],
        compiler_params=pltpu.CompilerParams(vmem_limit_bytes=OWN_VMEM_BYTES),
        cost_estimate=pl.CostEstimate(
            flops=2 * rows * size * lower_mid.shape[0] * lower_mid.shape[2],
            bytes_accessed=2 * (math.prod(rounded.shape) + math.prod(lower_mid.shape)),
            transcendentals=0,
        ),
        name="own_terms",
    )(parent, rounded, lower_mid, mid_rhs)


def coupling_kernel(pattern_ref, round_ref, lower_ref, up_ref, rounded, lower, round_sem, sems):
    leaves, kinds = lower.shape[:2]
    round_copy = pltpu.make_async_copy(round_ref, rounded, round_sem)
    round_copy.start()
    copies = [pltpu.make_async_copy(lower_ref.at[:, k], lower.at[:, k], sems.at[k]) for k in range(kinds)]
    for copy in copies:
        copy.start()
    round_copy.wait()
    for k in range(kinds):
        copies[k].wait()
        left = [rounded[i] * pattern_ref[k, i].astype(F32).astype(BF16) for i in range(leaves)]
        right = [lower[i, k] for i in range(leaves)]
        up_ref[k] = times_transposed(jnp.concatenate(left, axis=1), jnp.concatenate(right, axis=1))


def leaf_coupling(pattern, rounded, lower):
    leaves, rows, width = rounded.shape
    kinds, size = lower.shape[1:3]
    hbm = pl.BlockSpec(memory_space=pltpu.HBM)
    return pl.pallas_call(
        coupling_kernel,
        in_specs=[pl.BlockSpec(memory_space=pltpu.SMEM), hbm, hbm],
        out_specs=pl.BlockSpec(memory_space=pltpu.VMEM),
        out_shape=jax.ShapeDtypeStruct((kinds, rows, size), F32),
        scratch_shapes=[
            pltpu.VMEM(rounded.shape, BF16),
            pltpu.VMEM(lower.shape, BF16),
            pltpu.SemaphoreType.DMA,
            pltpu.SemaphoreType.DMA((kinds,)),
        ],
        compiler_params=pltpu.CompilerParams(vmem_limit_bytes=LARGE_VMEM_BYTES),
        cost_estimate=pl.CostEstimate(
            flops=2 * leaves * kinds * rows * size * width,
            bytes_accessed=leaves * (rows * width * 2 + kinds * size * width * 2) + kinds * rows * size * 4,
            transcendentals=0,
        ),
        name="leaf_coupling",
    )(pattern, rounded, lower)


def swap(block, axis, bit):
    count = lax.axis_size(axis)
    return lax.ppermute(block, axis, [(i, i ^ 1 << bit) for i in range(count)])


def swap_sum(halves, axis, bit):
    here = lax.axis_index(axis) >> bit & 1
    kept = lax.dynamic_index_in_dim(halves, here, 0, keepdims=False)
    given = lax.dynamic_index_in_dim(halves, 1 - here, 0, keepdims=False)
    return kept.astype(F32) + swap(given.astype(BF16), axis, bit).astype(F32)


def exchange(pieces, axis):
    return lax.all_to_all(pieces, axis, split_axis=0, concat_axis=0, tiled=True)


def scatter_sum(pieces, axis):
    return jnp.sum(exchange(pieces.astype(BF16), axis).astype(F32), axis=0)


def col_sum(pieces):
    if pieces.shape[0] == 2:
        return swap_sum(pieces, "col", 0)
    return scatter_sum(pieces, "col")


def spread(piece, axis):
    count = lax.axis_size(axis)
    return exchange(jnp.broadcast_to(piece[None], (count,) + piece.shape), axis)


def col_spread(piece):
    if lax.axis_size("col") == 2:
        other = swap(piece, "col", 0)
        first = lax.axis_index("col") == 0
        return jnp.stack([jnp.where(first, piece, other), jnp.where(first, other, piece)])
    return spread(piece, "col")


def any_cols(
    leaf_rhs,
    leaf_inv,
    leaf_lower_mid,
    leaf_lower_coupling,
    leaf_parent,
    leaf_pattern,
    mid_rhs,
    parent_diagonal_inverse,
    mid_lower,
    mid_pattern,
    top_rhs,
    top_inv,
    top_lower,
    apex_rhs,
    apex_inv,
    apex_lower,
):
    cols = lax.axis_size("col")
    rows = lax.axis_size("row")
    col = lax.axis_index("col")
    row = lax.axis_index("row")
    gz = lax.axis_index("gz")
    pair, core = gz // 2, gz % 2
    rhs_count, size = leaf_rhs.shape[1:]
    part = rhs_count // (4 * cols)

    leaf_solved, leaf_round, *terms = leaf_solve(leaf_parent, leaf_rhs, leaf_inv, leaf_lower_mid, cols)
    if cols == 2:
        own, _ = own_terms(leaf_parent, leaf_round, leaf_lower_mid, mid_rhs)
        mid_part = own.astype(F32) + swap(terms[0], "col", 0).astype(F32)
    else:
        mid_part = scatter_sum(jnp.stack(terms), "col")
    layer_up = leaf_coupling(leaf_pattern.T, leaf_round, leaf_lower_coupling)
    quarter = rhs_count // rows
    mid_sum = scatter_sum(mid_part.reshape(rows, quarter, size), "row")
    mid_total = lax.dynamic_slice_in_dim(mid_rhs[0], row * quarter, quarter, 0) - mid_sum
    mid_ready = spread(mid_total.astype(BF16), "row").reshape(rhs_count, size)
    mid_solved = times_transposed(mid_ready, parent_diagonal_inverse[0])
    mid_round = mid_solved.astype(BF16)
    mid_weight = mid_pattern[0].astype(F32)

    top_part = layer_up[0] + times_transposed(mid_round, mid_lower[0, 0])
    top_part = top_part.astype(BF16).reshape(rows, cols, part, size).swapaxes(0, 1)
    top_sum = scatter_sum(top_part.reshape(rows * cols, part, size), ("col", "row"))
    top_start = (row * cols + col) * part
    top_total = lax.dynamic_slice_in_dim(top_rhs[0], top_start, part, 0) - top_sum
    top_ready = spread(top_total.astype(BF16), "row").reshape(rows * part, size)
    top_solved = times_transposed(top_ready, top_inv[0])
    top_round = top_solved.astype(BF16)

    late = jnp.stack([layer_up[k] + mid_weight[k - 1] * times_transposed(mid_round, mid_lower[0, k]) for k in (1, 2)])
    late = late.reshape(2, 2, 2, cols, part, size)
    late = swap_sum(late.transpose(2, 0, 1, 3, 4, 5), "gz", 0)
    late = col_sum(late.transpose(2, 0, 1, 3, 4))

    up = jnp.stack([times_transposed(top_round, top_lower[0, k]) for k in (0, 1)])
    up = swap_sum(up.reshape(2, 2, 2, part, size).transpose(2, 0, 1, 3, 4), "gz", 0) + late
    half = part // 2
    front_sum = scatter_sum(up[0].reshape(rows, half, size), "row")
    front_start = row // 2 * (rhs_count // 2) + (core * cols + col) * part + row % 2 * half
    front_rhs = lax.dynamic_slice(apex_rhs, (pair, front_start, 0), (1, half, size))[0]
    front_ready = spread((front_rhs - front_sum).astype(BF16), "row").reshape(2 * part, size)
    front_inv = lax.dynamic_index_in_dim(apex_inv, pair, 0, keepdims=False)
    front_lower = lax.dynamic_index_in_dim(apex_lower, pair, 0, keepdims=False)
    front_solved = times_transposed(front_ready, front_inv)

    own_up = times_transposed(front_solved.astype(BF16), front_lower)
    last_part = swap_sum(up[1] + own_up.reshape(2, part, size), "gz", 1)
    last_sum = jnp.sum(spread(last_part.astype(BF16), "row").astype(F32), axis=0)
    last_start = (pair * 2 * cols + core * cols + col) * part
    last_rhs = lax.dynamic_slice_in_dim(apex_rhs[2], last_start, part, 0)
    last_solved = times_transposed((last_rhs - last_sum).astype(BF16), apex_inv[2])

    width = last_solved.shape[1]
    front_solved = front_solved.reshape(2, part, width)
    own_front = lax.dynamic_index_in_dim(front_solved, pair, 0, keepdims=False)
    other_front = swap(lax.dynamic_index_in_dim(front_solved, 1 - pair, 0, keepdims=False), "gz", 1)
    leading = pair == 0
    fronts = jnp.stack([jnp.where(leading, own_front, other_front), jnp.where(leading, other_front, own_front)])
    fronts = col_spread(fronts).swapaxes(0, 1).reshape(2, cols * part, width)
    last = col_spread(last_solved).reshape(1, cols * part, width)
    top_all = col_spread(top_solved.reshape(rows, part, width)).swapaxes(0, 1).reshape(1, rhs_count, width)
    return (leaf_solved, mid_solved[None], top_all, jnp.concatenate([fronts, last], axis=0))


def partners(block, moves):
    blocks = block if isinstance(block, (list, tuple)) else [block] * len(moves)
    arrived = []
    for item, move in zip(blocks, moves):
        axes = tuple(move)
        sizes = [lax.axis_size(axis) for axis in axes]
        route = []
        for source in range(math.prod(sizes)):
            place, rest = [], source
            for count in reversed(sizes):
                place.insert(0, rest % count)
                rest //= count
            target = 0
            for at, count, axis in zip(place, sizes, axes):
                target = target * count + (at ^ move[axis])
            route.append((source, target))
        arrived.append(lax.ppermute(item, axes, route))
    return arrived


def whole_call(kernel, name, operands, results, flops=0, scratch=(), scalars=0, after=()):
    moved = sum(math.prod(a.shape) * a.dtype.itemsize for a in operands)
    moved += sum(math.prod(shape) * jnp.dtype(kind).itemsize for shape, kind in results)
    smem, vmem = pl.BlockSpec(memory_space=pltpu.SMEM), pl.BlockSpec(memory_space=pltpu.VMEM)

    def body(*refs):
        kernel(*refs[len(after) :])

    return pl.pallas_call(
        body,
        in_specs=[pl.BlockSpec(memory_space=pl.ANY)] * len(after)
        + [smem] * scalars
        + [vmem] * (len(operands) - scalars),
        out_specs=[vmem] * len(results),
        out_shape=[jax.ShapeDtypeStruct(shape, kind) for shape, kind in results],
        scratch_shapes=list(scratch),
        compiler_params=pltpu.CompilerParams(vmem_limit_bytes=STEP_VMEM_BYTES),
        cost_estimate=pl.CostEstimate(flops=flops, bytes_accessed=moved, transcendentals=0),
        name=name,
    )(*after, *operands)


def piece(index, length):
    return pl.ds(pl.multiple_of(index * length, length), length)


def widened(*refs):
    total = refs[0][...].astype(F32)
    for ref in refs[1:]:
        total = total + ref[...].astype(F32)
    return total


ROW_MOVES = [{"row": d} for d in (3, 2, 1)]


def mid_pieces_kernel(rhs_ref, terms_ref, other_ref, kept_ref, *given_refs):
    row, length = lax.axis_index("row"), kept_ref.shape[0]
    for d, ref in zip((0, 3, 2, 1), (kept_ref,) + given_refs):
        at = piece(row ^ d, length)
        total = terms_ref[at].astype(F32) + other_ref[at].astype(F32)
        ref[...] = rhs_ref[...] - total if d == 0 else total.astype(BF16)


def mid_total_kernel(kept_ref, r1, r2, r3, ready_ref):
    ready_ref[...] = (kept_ref[...] - widened(r1, r2, r3)).astype(BF16)


def mid_solve_kernel(
    pattern_ref, p0, p3, p2, p1, inv_ref, lower_ref, up_ref,
    solved_ref, top_ref, top_given_ref, late_ref, late_given_ref, rounded, total,
):
    row, col, core = lax.axis_index("row"), lax.axis_index("col"), lax.axis_index("gz") & 1
    length, part = p0.shape[0], top_ref.shape[1]
    for d, ref in zip((0, 3, 2, 1), (p0, p3, p2, p1)):
        at = piece(row ^ d, length)
        solved = times_transposed(ref[...], inv_ref[0])
        solved_ref[at] = solved
        rounded[at] = solved.astype(BF16)
    total[...] = up_ref[0] + times_transposed(rounded[...], lower_ref[0, 0])
    for i in range(4):
        top_ref[i] = total[piece(i * 2 + col, part)]
        top_given_ref[i] = total[piece(i * 2 + 1 - col, part)].astype(BF16)
    for k in (1, 2):
        weight = pattern_ref[0, k - 1].astype(F32)
        total[...] = up_ref[k] + weight * times_transposed(rounded[...], lower_ref[0, k])
        for half in (0, 1):
            late_ref[k - 1, half] = total[piece(half * 2 + core, length)]
            late_given_ref[k - 1, half] = total[piece(half * 2 + 1 - core, length)].astype(BF16)


def top_share_kernel(inv_ref, share_ref):
    length = share_ref.shape[1]
    share_ref[...] = inv_ref[0, :, piece(lax.axis_index("col"), length)]


def half_top_kernel(p0, p3, p2, p1, half_ref):
    row = lax.axis_index("row")
    for d, ref in zip((0, 3, 2, 1), (p0, p3, p2, p1)):
        half_ref[piece(row ^ d, ref.shape[0])] = ref[...]


def whole_top_kernel(own_ref, other_ref, whole_ref):
    col, length = lax.axis_index("col"), own_ref.shape[1]
    whole_ref[:, piece(col, length)] = own_ref[...]
    whole_ref[:, piece(1 - col, length)] = other_ref[...]


def on_first_row(rhs):
    return jnp.where(lax.axis_index("row") == 0, rhs, 0.0)


def late_pieces_kernel(late_ref, other_ref, out_ref, given_ref):
    col, part = lax.axis_index("col"), out_ref.shape[2]
    for k in (0, 1):
        for half in (0, 1):
            for ref, side in ((out_ref, col), (given_ref, 1 - col)):
                at = piece(side, part)
                total = late_ref[k, half, at] + other_ref[k, half, at].astype(F32)
                ref[k, half] = total.astype(ref.dtype)


def top_blocks_kernel(rhs_ref, top_ref, other_ref, inv_ref, kept_ref, g3, g2, g1, ready, solved):
    row, col, part = lax.axis_index("row"), lax.axis_index("col"), top_ref.shape[1]
    for i in range(4):
        total = top_ref[i] + other_ref[i].astype(F32)
        ready[pl.ds(i * part, part)] = (on_first_row(rhs_ref[0, piece(i * 2 + col, part)]) - total).astype(BF16)
    solved[...] = times_transposed(ready[...], inv_ref[...])
    for d, ref in zip((0, 3, 2, 1), (kept_ref, g3, g2, g1)):
        ref[...] = solved[:, piece(row ^ d, ref.shape[1])].astype(ref.dtype)


def top_up_kernel(
    kept_ref, r3, r2, r1, lower_ref, late_ref, late_other_ref, solved_ref, send_ref, out_ref, given_ref, total
):
    core = lax.axis_index("gz") & 1
    part = solved_ref.shape[1]
    solved = widened(kept_ref, r3, r2, r1)
    rounded = solved.astype(BF16)
    for i in range(4):
        solved_ref[i] = solved[i * part : (i + 1) * part]
        send_ref[i] = rounded[i * part : (i + 1) * part]
    for k in (0, 1):
        total[...] = times_transposed(rounded, lower_ref[0, k])
        for half in (0, 1):
            late = late_ref[k, half] + late_other_ref[k, half].astype(F32)
            out_ref[k, half] = total[piece(half * 2 + core, part)] + late
            given_ref[k, half] = total[piece(half * 2 + 1 - core, part)].astype(BF16)


def front_pieces_kernel(kept_ref, other_ref, own_ref, send_ref, last_ref):
    part = kept_ref.shape[2]
    for half in (0, 1):
        at = pl.ds(half * part, part)
        total = kept_ref[0, half] + other_ref[0, half].astype(F32)
        own_ref[at] = total
        send_ref[at] = total.astype(BF16)
        last_ref[half] = kept_ref[1, half] + other_ref[1, half].astype(F32)


def apex_rows(rhs_ref, which, half, part):
    core, col = lax.axis_index("gz") & 1, lax.axis_index("col")
    return rhs_ref[which, piece(half * 4 + core * 2 + col, part)]


def front_solve_kernel(rhs_ref, own_ref, r3, r2, r1, inv_ref, lower_ref, last_ref, front_ref, kept_ref, given_ref, total, fronts):
    pair = lax.axis_index("gz") >> 1
    part, size = kept_ref.shape
    rhs = jnp.concatenate([apex_rows(rhs_ref, pair, half, part) for half in (0, 1)])
    ready = (rhs - widened(own_ref, r3, r2, r1)).astype(BF16)
    fronts[...] = times_transposed(ready, inv_ref[pair])
    total[...] = times_transposed(fronts[...].astype(BF16), lower_ref[pair])
    front_ref[...] = fronts[piece(pair, part)]
    kept_ref[...] = total[piece(pair, part)] + last_ref[pair]
    given_ref[:, :size] = (total[piece(1 - pair, part)] + last_ref[1 - pair]).astype(BF16)
    given_ref[:, size:] = fronts[piece(1 - pair, part)].astype(BF16)


def last_pieces_kernel(kept_ref, other_ref, own_ref, send_ref):
    total = kept_ref[...] + other_ref[:, : own_ref.shape[1]].astype(F32)
    own_ref[...] = total
    send_ref[...] = total.astype(BF16)


def place_top_kernel(top_ref, other_ref, top_all_ref, done_ref):
    done_ref[...] = jnp.zeros_like(done_ref)
    col, part = lax.axis_index("col"), top_ref.shape[1]
    for i in range(top_ref.shape[0]):
        top_all_ref[0, piece(i * 2 + col, part)] = top_ref[i]
        top_all_ref[0, piece(i * 2 + 1 - col, part)] = other_ref[i].astype(F32)


def last_solve_kernel(rhs_ref, inv_ref, own_ref, r3, r2, r1, front_ref, other_ref, solved_ref, send_ref):
    pair = lax.axis_index("gz") >> 1
    part, size = own_ref.shape
    ready = (apex_rows(rhs_ref, 2, pair, part) - widened(own_ref, r3, r2, r1)).astype(BF16)
    solved_ref[2] = times_transposed(ready, inv_ref[2])
    solved_ref[pair] = front_ref[...]
    solved_ref[1 - pair] = other_ref[:, size:].astype(F32)
    send_ref[...] = solved_ref[...].astype(BF16)


def place_apex_kernel(solved_ref, other_ref, apex_ref):
    col, part = lax.axis_index("col"), solved_ref.shape[1]
    for k in range(3):
        apex_ref[k, piece(col, part)] = solved_ref[k]
        apex_ref[k, piece(1 - col, part)] = other_ref[k].astype(F32)


def two_cols(
    leaf_rhs,
    leaf_inv,
    leaf_lower_mid,
    leaf_lower_coupling,
    leaf_parent,
    leaf_pattern,
    mid_rhs,
    parent_diagonal_inverse,
    mid_lower,
    mid_pattern,
    top_rhs,
    top_inv,
    top_lower,
    apex_rhs,
    apex_inv,
    apex_lower,
):
    count, size = leaf_rhs.shape[1:]
    width = leaf_inv.shape[1]
    quarter, part = count // 4, count // 8

    rows = lax.axis_size("row")

    leaf_solved, leaf_round, other_terms = leaf_solve(leaf_parent, leaf_rhs, leaf_inv, leaf_lower_mid, 2)
    (other_terms,) = partners(other_terms, [{"col": 1}])
    layer_up = leaf_coupling(leaf_pattern.T, leaf_round, leaf_lower_coupling)

    (share,) = whole_call(top_share_kernel, "top_share", [top_inv], [((width, size // 2), BF16)])
    shares = partners(share, ROW_MOVES)

    terms, rhs_rows = own_terms(leaf_parent, leaf_round, leaf_lower_mid, mid_rhs)
    kept, *given = whole_call(
        mid_pieces_kernel, "mid_pieces", [rhs_rows, terms, other_terms],
        [((quarter, size), F32)] + [((quarter, size), BF16)] * 3,
        after=shares,
    )
    arrived = partners(given, ROW_MOVES)
    (top_half,) = whole_call(half_top_kernel, "half_top", [share, *shares], [((size, size // 2), BF16)], after=[kept])
    (top_other,) = partners(top_half, [{"col": 1}])
    (ready,) = whole_call(
        mid_total_kernel, "mid_total", [kept, *arrived], [((quarter, size), BF16)], after=[layer_up]
    )
    arrived = partners(ready, ROW_MOVES)
    (top_whole,) = whole_call(whole_top_kernel, "whole_top", [top_half, top_other], [((size, size), BF16)])
    mid_solved, kept, given, late_kept, late_given = whole_call(
        mid_solve_kernel, "mid_solve", [mid_pattern, ready, *arrived, parent_diagonal_inverse, mid_lower, layer_up],
        [((count, width), F32), ((4, part, size), F32), ((4, part, size), BF16)]
        + [((2, 2, quarter, size), F32), ((2, 2, quarter, size), BF16)],
        flops=8 * count * size * width,
        scratch=[pltpu.VMEM((count, width), BF16), pltpu.VMEM((count, size), F32)],
        scalars=1,
        after=[top_whole],
    )

    (other,) = partners(given, [{"col": 1}])
    (late_other,) = partners(late_given, [{"gz": 1}])
    late_kept, late_given = whole_call(
        late_pieces_kernel, "late_pieces", [late_kept, late_other],
        [((2, 2, part, size), F32), ((2, 2, part, size), BF16)],
    )
    (late_other,) = partners(late_given, [{"col": 1}])
    kept, *given = whole_call(
        top_blocks_kernel, "top_blocks", [top_rhs, kept, other, top_whole],
        [((count // 2, width), F32)] + [((count // 2, width), BF16)] * 3,
        flops=count * size * size,
        scratch=[pltpu.VMEM((count // 2, size), BF16), pltpu.VMEM((count // 2, size), F32)],
        after=[late_given],
    )
    arrived = partners(given, ROW_MOVES)
    top_solved, top_send, kept, given = whole_call(
        top_up_kernel, "top_up", [kept, *arrived, top_lower, late_kept, late_other],
        [((4, part, width), F32), ((4, part, width), BF16), ((2, 2, part, size), F32), ((2, 2, part, size), BF16)],
        flops=2 * count * size * width,
        scratch=[pltpu.VMEM((4 * part, size), F32)],
    )
    (other,) = partners(given, [{"gz": 1}])
    (other_top,) = partners(top_send, [{"col": 1}])

    own, send, last = whole_call(
        front_pieces_kernel, "front_pieces", [kept, other],
        [((2 * part, size), F32), ((2 * part, size), BF16), ((2, part, size), F32)],
    )
    arrived = partners(send, ROW_MOVES)
    front, kept, given = whole_call(
        front_solve_kernel, "front_solve", [apex_rhs, own, *arrived, apex_inv, apex_lower, last],
        [((part, width), F32), ((part, size), F32), ((part, size + width), BF16)],
        flops=count * size * width,
        scratch=[pltpu.VMEM((2 * part, size), F32), pltpu.VMEM((2 * part, width), F32)],
    )

    (other,) = partners(given, [{"gz": 2}])
    own, send = whole_call(
        last_pieces_kernel, "last_pieces", [kept, other], [((part, size), F32), ((part, size), BF16)]
    )
    arrived = partners(send, ROW_MOVES)
    top_all, placed = whole_call(
        place_top_kernel, "place_top", [top_solved, other_top], [((1, count, width), F32), ((8, width), F32)], after=[own]
    )
    solved, send = whole_call(
        last_solve_kernel, "last_solve", [apex_rhs, apex_inv, own, *arrived, front, other],
        [((3, part, width), F32), ((3, part, width), BF16)],
        flops=count * size * width // 4,
        after=[placed],
    )
    (other,) = partners(send, [{"col": 1}])
    (apex,) = whole_call(place_apex_kernel, "place_apex", [solved, other], [((3, 2 * part, width), F32)])
    return (leaf_solved, mid_solved[None], top_all, apex)


def solution(mesh):
    placed = (
        P(("gz", "col"), None, None),
        P(("gz", "col"), "row", None),
        P(("gz", "col"), None, "row"),
        P(("gz", "col"), None, None, "row"),
        P(("gz", "col")),
        P(("gz", "col"), None),
        P(("gz", "col"), None, None),
        P(("gz", "col"), "row", None),
        P(("gz", "col"), None, None, "row"),
        P(("gz", "col"), None),
        P("gz", None, None),
        P("gz", "row", None),
        P("gz", None, None, "row"),
        P(),
        P(None, "row", None),
        P(None, None, "row"),
    )
    return jax.shard_map(
        two_cols if mesh.shape["col"] == 2 else any_cols,
        mesh=mesh,
        in_specs=placed,
        out_specs=(
            P(("gz", "col"), None, "row"),
            P(("gz", "col"), None, "row"),
            P("gz", None, "row"),
            P(None, "gz", "row"),
        ),
        check_vma=False,
    )
```

```python
import functools
import math

import jax
import jax.numpy as jnp
from jax import lax
from jax.experimental import pallas as pl
from jax.experimental.pallas import tpu as pltpu
from jax.sharding import PartitionSpec as P

BF16 = jnp.bfloat16
F32 = jnp.float32
LEAF_VMEM_BYTES = 56 * 1024 * 1024
OWN_VMEM_BYTES = 52 * 1024 * 1024
LARGE_VMEM_BYTES = 50 * 1024 * 1024
STEP_VMEM_BYTES = 16 * 1024 * 1024


def times_transposed(left, right):
    return lax.dot_general(left, right, (((1,), (1,)), ((), ())), preferred_element_type=F32)


def masked_terms(parent_ref, wanted, rounded, mid):
    leaves = mid.shape[0]
    weights = [jnp.where(parent_ref[i] == wanted, 1.0, 0.0).astype(BF16) for i in range(leaves)]
    left = jnp.concatenate([rounded[i] * weights[i] for i in range(leaves)], axis=1)
    right = jnp.concatenate([mid[i] for i in range(leaves)], axis=1)
    return times_transposed(left, right)


def leaf_kernel(
    slots, parent_ref, rhs_ref, inv_ref, mid_ref, solved_ref, round_ref, *rest
):
    terms_refs = rest[: len(rest) - 11]
    rhs, inv, mid, solved, rounded, total, rhs_sems, inv_sems, mid_sem, out_sems, round_sems = rest[len(rest) - 11 :]
    leaves = rhs.shape[0]
    rhs_copies = [pltpu.make_async_copy(rhs_ref.at[i], rhs.at[i], rhs_sems.at[i]) for i in range(leaves)]
    inv_copies = [pltpu.make_async_copy(inv_ref.at[i], inv.at[i], inv_sems.at[i]) for i in range(leaves)]
    mid_copy = pltpu.make_async_copy(mid_ref, mid, mid_sem)
    for i in range(leaves):
        inv_copies[i].start()
        rhs_copies[i].start()
    mid_copy.start()
    out_copies = []
    for start in range(0, leaves, 2):
        group = range(start, min(start + 2, leaves))
        for i in group:
            inv_copies[i].wait()
            rhs_copies[i].wait()
        products = [times_transposed(rhs[i].astype(BF16), inv[i]) for i in group]
        for i, product in zip(group, products):
            solved[i] = product
            rounded[i] = product.astype(BF16)
        for i in group:
            out_copies.append(pltpu.make_async_copy(solved.at[i], solved_ref.at[i], out_sems.at[i]))
            out_copies.append(pltpu.make_async_copy(rounded.at[i], round_ref.at[i], round_sems.at[i]))
            for copy in out_copies[-2:]:
                copy.start()
    mid_copy.wait()
    if slots == 2:
        terms_refs[0][...] = masked_terms(parent_ref, 1 - lax.axis_index("col"), rounded, mid).astype(BF16)
    else:
        total[...] = jnp.zeros_like(total)
        for i in range(leaves):
            total[parent_ref[i]] += times_transposed(rounded[i], mid[i])
        for s, ref in enumerate(terms_refs):
            ref[...] = total[s].astype(ref.dtype)
    for copy in out_copies:
        copy.wait()


def leaf_solve(parent, rhs, inv, lower_mid, slots):
    leaves, rows, size = rhs.shape
    width = inv.shape[1]
    given = 1 if slots == 2 else slots
    hbm, vmem = pl.BlockSpec(memory_space=pltpu.HBM), pl.BlockSpec(memory_space=pltpu.VMEM)
    return pl.pallas_call(
        functools.partial(leaf_kernel, slots),
        in_specs=[pl.BlockSpec(memory_space=pltpu.SMEM), hbm, hbm, hbm],
        out_specs=[hbm, hbm] + [vmem] * given,
        out_shape=[
            jax.ShapeDtypeStruct((leaves, rows, width), F32),
            jax.ShapeDtypeStruct((leaves, rows, width), BF16),
        ]
        + [jax.ShapeDtypeStruct((rows, size), BF16)] * given,
        scratch_shapes=[
            pltpu.VMEM(rhs.shape, F32),
            pltpu.VMEM(inv.shape, BF16),
            pltpu.VMEM(lower_mid.shape, BF16),
            pltpu.VMEM((leaves, rows, width), F32),
            pltpu.VMEM((leaves, rows, width), BF16),
            pltpu.VMEM((8, 128) if slots == 2 else (slots, rows, size), F32),
            pltpu.SemaphoreType.DMA((leaves,)),
            pltpu.SemaphoreType.DMA((leaves,)),
            pltpu.SemaphoreType.DMA,
            pltpu.SemaphoreType.DMA((leaves,)),
            pltpu.SemaphoreType.DMA((leaves,)),
        ],
        compiler_params=pltpu.CompilerParams(vmem_limit_bytes=LEAF_VMEM_BYTES),
        cost_estimate=pl.CostEstimate(
            flops=4 * leaves * rows * size * width,
            bytes_accessed=leaves * (rows * size * 4 + 4 * width * size + rows * width * 6),
            transcendentals=0,
        ),
        name="leaf_solve",
    )(parent, rhs, inv, lower_mid)


def own_terms_kernel(parent_ref, round_ref, mid_ref, rhs_ref, terms_ref, rhs_rows_ref, rounded, mid, sems):
    length = rhs_rows_ref.shape[0]
    copies = [
        pltpu.make_async_copy(round_ref, rounded, sems.at[0]),
        pltpu.make_async_copy(mid_ref, mid, sems.at[1]),
        pltpu.make_async_copy(rhs_ref.at[0, piece(lax.axis_index("row"), length)], rhs_rows_ref, sems.at[2]),
    ]
    for copy in copies:
        copy.start()
    for copy in copies:
        copy.wait()
    terms_ref[...] = masked_terms(parent_ref, lax.axis_index("col"), rounded, mid).astype(BF16)


def own_terms(parent, rounded, lower_mid, mid_rhs):
    rows, size = mid_rhs.shape[1:]
    hbm, vmem = pl.BlockSpec(memory_space=pltpu.HBM), pl.BlockSpec(memory_space=pltpu.VMEM)
    return pl.pallas_call(
        own_terms_kernel,
        in_specs=[pl.BlockSpec(memory_space=pltpu.SMEM), hbm, hbm, hbm],
        out_specs=[vmem, vmem],
        out_shape=[
            jax.ShapeDtypeStruct((rows, size), BF16),
            jax.ShapeDtypeStruct((rows // lax.axis_size("row"), size), F32),
        ],
        scratch_shapes=[
            pltpu.VMEM(rounded.shape, BF16),
            pltpu.VMEM(lower_mid.shape, BF16),
            pltpu.SemaphoreType.DMA((3,)),
        ],
        compiler_params=pltpu.CompilerParams(vmem_limit_bytes=OWN_VMEM_BYTES),
        cost_estimate=pl.CostEstimate(
            flops=2 * rows * size * lower_mid.shape[0] * lower_mid.shape[2],
            bytes_accessed=2 * (math.prod(rounded.shape) + math.prod(lower_mid.shape)),
            transcendentals=0,
        ),
        name="own_terms",
    )(parent, rounded, lower_mid, mid_rhs)


def coupling_kernel(pattern_ref, round_ref, lower_ref, up_ref, rounded, lower, round_sem, sems):
    leaves, kinds = lower.shape[:2]
    round_copy = pltpu.make_async_copy(round_ref, rounded, round_sem)
    round_copy.start()
    copies = [pltpu.make_async_copy(lower_ref.at[:, k], lower.at[:, k], sems.at[k]) for k in range(kinds)]
    for copy in copies:
        copy.start()
    round_copy.wait()
    for k in range(kinds):
        copies[k].wait()
        left = [rounded[i] * pattern_ref[k, i].astype(F32).astype(BF16) for i in range(leaves)]
        right = [lower[i, k] for i in range(leaves)]
        up_ref[k] = times_transposed(jnp.concatenate(left, axis=1), jnp.concatenate(right, axis=1))


def leaf_coupling(pattern, rounded, lower):
    leaves, rows, width = rounded.shape
    kinds, size = lower.shape[1:3]
    hbm = pl.BlockSpec(memory_space=pltpu.HBM)
    return pl.pallas_call(
        coupling_kernel,
        in_specs=[pl.BlockSpec(memory_space=pltpu.SMEM), hbm, hbm],
        out_specs=pl.BlockSpec(memory_space=pltpu.VMEM),
        out_shape=jax.ShapeDtypeStruct((kinds, rows, size), F32),
        scratch_shapes=[
            pltpu.VMEM(rounded.shape, BF16),
            pltpu.VMEM(lower.shape, BF16),
            pltpu.SemaphoreType.DMA,
            pltpu.SemaphoreType.DMA((kinds,)),
        ],
        compiler_params=pltpu.CompilerParams(vmem_limit_bytes=LARGE_VMEM_BYTES),
        cost_estimate=pl.CostEstimate(
            flops=2 * leaves * kinds * rows * size * width,
            bytes_accessed=leaves * (rows * width * 2 + kinds * size * width * 2) + kinds * rows * size * 4,
            transcendentals=0,
        ),
        name="leaf_coupling",
    )(pattern, rounded, lower)


def swap(block, axis, bit):
    count = lax.axis_size(axis)
    return lax.ppermute(block, axis, [(i, i ^ 1 << bit) for i in range(count)])


def swap_sum(halves, axis, bit):
    here = lax.axis_index(axis) >> bit & 1
    kept = lax.dynamic_index_in_dim(halves, here, 0, keepdims=False)
    given = lax.dynamic_index_in_dim(halves, 1 - here, 0, keepdims=False)
    return kept.astype(F32) + swap(given.astype(BF16), axis, bit).astype(F32)


def exchange(pieces, axis):
    return lax.all_to_all(pieces, axis, split_axis=0, concat_axis=0, tiled=True)


def scatter_sum(pieces, axis):
    return jnp.sum(exchange(pieces.astype(BF16), axis).astype(F32), axis=0)


def col_sum(pieces):
    if pieces.shape[0] == 2:
        return swap_sum(pieces, "col", 0)
    return scatter_sum(pieces, "col")


def spread(piece, axis):
    count = lax.axis_size(axis)
    return exchange(jnp.broadcast_to(piece[None], (count,) + piece.shape), axis)


def col_spread(piece):
    if lax.axis_size("col") == 2:
        other = swap(piece, "col", 0)
        first = lax.axis_index("col") == 0
        return jnp.stack([jnp.where(first, piece, other), jnp.where(first, other, piece)])
    return spread(piece, "col")


def any_cols(
    leaf_rhs,
    leaf_inv,
    leaf_lower_mid,
    leaf_lower_coupling,
    leaf_parent,
    leaf_pattern,
    mid_rhs,
    parent_diagonal_inverse,
    mid_lower,
    mid_pattern,
    top_rhs,
    top_inv,
    top_lower,
    apex_rhs,
    apex_inv,
    apex_lower,
):
    cols = lax.axis_size("col")
    rows = lax.axis_size("row")
    col = lax.axis_index("col")
    row = lax.axis_index("row")
    gz = lax.axis_index("gz")
    pair, core = gz // 2, gz % 2
    rhs_count, size = leaf_rhs.shape[1:]
    part = rhs_count // (4 * cols)

    leaf_solved, leaf_round, *terms = leaf_solve(leaf_parent, leaf_rhs, leaf_inv, leaf_lower_mid, cols)
    if cols == 2:
        own, _ = own_terms(leaf_parent, leaf_round, leaf_lower_mid, mid_rhs)
        mid_part = own.astype(F32) + swap(terms[0], "col", 0).astype(F32)
    else:
        mid_part = scatter_sum(jnp.stack(terms), "col")
    layer_up = leaf_coupling(leaf_pattern.T, leaf_round, leaf_lower_coupling)
    quarter = rhs_count // rows
    mid_sum = scatter_sum(mid_part.reshape(rows, quarter, size), "row")
    mid_total = lax.dynamic_slice_in_dim(mid_rhs[0], row * quarter, quarter, 0) - mid_sum
    mid_ready = spread(mid_total.astype(BF16), "row").reshape(rhs_count, size)
    mid_solved = times_transposed(mid_ready, parent_diagonal_inverse[0])
    mid_round = mid_solved.astype(BF16)
    mid_weight = mid_pattern[0].astype(F32)

    top_part = layer_up[0] + times_transposed(mid_round, mid_lower[0, 0])
    top_part = top_part.astype(BF16).reshape(rows, cols, part, size).swapaxes(0, 1)
    top_sum = scatter_sum(top_part.reshape(rows * cols, part, size), ("col", "row"))
    top_start = (row * cols + col) * part
    top_total = lax.dynamic_slice_in_dim(top_rhs[0], top_start, part, 0) - top_sum
    top_ready = spread(top_total.astype(BF16), "row").reshape(rows * part, size)
    top_solved = times_transposed(top_ready, top_inv[0])
    top_round = top_solved.astype(BF16)

    late = jnp.stack([layer_up[k] + mid_weight[k - 1] * times_transposed(mid_round, mid_lower[0, k]) for k in (1, 2)])
    late = late.reshape(2, 2, 2, cols, part, size)
    late = swap_sum(late.transpose(2, 0, 1, 3, 4, 5), "gz", 0)
    late = col_sum(late.transpose(2, 0, 1, 3, 4))

    up = jnp.stack([times_transposed(top_round, top_lower[0, k]) for k in (0, 1)])
    up = swap_sum(up.reshape(2, 2, 2, part, size).transpose(2, 0, 1, 3, 4), "gz", 0) + late
    half = part // 2
    front_sum = scatter_sum(up[0].reshape(rows, half, size), "row")
    front_start = row // 2 * (rhs_count // 2) + (core * cols + col) * part + row % 2 * half
    front_rhs = lax.dynamic_slice(apex_rhs, (pair, front_start, 0), (1, half, size))[0]
    front_ready = spread((front_rhs - front_sum).astype(BF16), "row").reshape(2 * part, size)
    front_inv = lax.dynamic_index_in_dim(apex_inv, pair, 0, keepdims=False)
    front_lower = lax.dynamic_index_in_dim(apex_lower, pair, 0, keepdims=False)
    front_solved = times_transposed(front_ready, front_inv)

    own_up = times_transposed(front_solved.astype(BF16), front_lower)
    last_part = swap_sum(up[1] + own_up.reshape(2, part, size), "gz", 1)
    last_sum = jnp.sum(spread(last_part.astype(BF16), "row").astype(F32), axis=0)
    last_start = (pair * 2 * cols + core * cols + col) * part
    last_rhs = lax.dynamic_slice_in_dim(apex_rhs[2], last_start, part, 0)
    last_solved = times_transposed((last_rhs - last_sum).astype(BF16), apex_inv[2])

    width = last_solved.shape[1]
    front_solved = front_solved.reshape(2, part, width)
    own_front = lax.dynamic_index_in_dim(front_solved, pair, 0, keepdims=False)
    other_front = swap(lax.dynamic_index_in_dim(front_solved, 1 - pair, 0, keepdims=False), "gz", 1)
    leading = pair == 0
    fronts = jnp.stack([jnp.where(leading, own_front, other_front), jnp.where(leading, other_front, own_front)])
    fronts = col_spread(fronts).swapaxes(0, 1).reshape(2, cols * part, width)
    last = col_spread(last_solved).reshape(1, cols * part, width)
    top_all = col_spread(top_solved.reshape(rows, part, width)).swapaxes(0, 1).reshape(1, rhs_count, width)
    return (leaf_solved, mid_solved[None], top_all, jnp.concatenate([fronts, last], axis=0))


def partners(block, moves):
    blocks = block if isinstance(block, (list, tuple)) else [block] * len(moves)
    arrived = []
    for item, move in zip(blocks, moves):
        axes = tuple(move)
        sizes = [lax.axis_size(axis) for axis in axes]
        route = []
        for source in range(math.prod(sizes)):
            place, rest = [], source
            for count in reversed(sizes):
                place.insert(0, rest % count)
                rest //= count
            target = 0
            for at, count, axis in zip(place, sizes, axes):
                target = target * count + (at ^ move[axis])
            route.append((source, target))
        arrived.append(lax.ppermute(item, axes, route))
    return arrived


def whole_call(kernel, name, operands, results, flops=0, scratch=(), scalars=0, after=(), hbm_results=0):
    moved = sum(math.prod(a.shape) * a.dtype.itemsize for a in operands)
    moved += sum(math.prod(shape) * jnp.dtype(kind).itemsize for shape, kind in results)
    smem, vmem = pl.BlockSpec(memory_space=pltpu.SMEM), pl.BlockSpec(memory_space=pltpu.VMEM)

    def body(*refs):
        kernel(*refs[len(after) :])

    return pl.pallas_call(
        body,
        in_specs=[pl.BlockSpec(memory_space=pl.ANY)] * len(after)
        + [smem] * scalars
        + [vmem] * (len(operands) - scalars),
        out_specs=[vmem] * (len(results) - hbm_results) + [pl.BlockSpec(memory_space=pltpu.HBM)] * hbm_results,
        out_shape=[jax.ShapeDtypeStruct(shape, kind) for shape, kind in results],
        scratch_shapes=list(scratch),
        compiler_params=pltpu.CompilerParams(vmem_limit_bytes=STEP_VMEM_BYTES),
        cost_estimate=pl.CostEstimate(flops=flops, bytes_accessed=moved, transcendentals=0),
        name=name,
    )(*after, *operands)


def piece(index, length):
    return pl.ds(pl.multiple_of(index * length, length), length)


def widened(*refs):
    total = refs[0][...].astype(F32)
    for ref in refs[1:]:
        total = total + ref[...].astype(F32)
    return total


ROW_MOVES = [{"row": d} for d in (3, 2, 1)]


def mid_pieces_kernel(rhs_ref, terms_ref, other_ref, kept_ref, *given_refs):
    row, length = lax.axis_index("row"), kept_ref.shape[0]
    for d, ref in zip((0, 3, 2, 1), (kept_ref,) + given_refs):
        at = piece(row ^ d, length)
        total = terms_ref[at].astype(F32) + other_ref[at].astype(F32)
        ref[...] = rhs_ref[...] - total if d == 0 else total.astype(BF16)


def mid_total_kernel(kept_ref, r1, r2, r3, ready_ref):
    ready_ref[...] = (kept_ref[...] - widened(r1, r2, r3)).astype(BF16)


def mid_solve_kernel(
    pattern_ref, p0, p3, p2, p1, inv_ref, lower_ref, up_ref,
    top_ref, top_given_ref, late_ref, late_given_ref, solved_ref, solved, rounded, total, sem,
):
    row, col, core = lax.axis_index("row"), lax.axis_index("col"), lax.axis_index("gz") & 1
    length, part = p0.shape[0], top_ref.shape[1]
    for d, ref in zip((0, 3, 2, 1), (p0, p3, p2, p1)):
        at = piece(row ^ d, length)
        product = times_transposed(ref[...], inv_ref[0])
        solved[at] = product
        rounded[at] = product.astype(BF16)
    copy = pltpu.make_async_copy(solved, solved_ref, sem)
    copy.start()
    total[0] = up_ref[0] + times_transposed(rounded[...], lower_ref[0, 0])
    for i in range(4):
        top_ref[i] = total[0, piece(i * 2 + col, part)]
        top_given_ref[i] = total[0, piece(i * 2 + 1 - col, part)].astype(BF16)
    for k in (1, 2):
        weight = pattern_ref[0, k - 1].astype(F32)
        total[k] = up_ref[k] + weight * times_transposed(rounded[...], lower_ref[0, k])
        for half in (0, 1):
            late_ref[k - 1, half] = total[k, piece(half * 2 + core, length)]
            late_given_ref[k - 1, half] = total[k, piece(half * 2 + 1 - core, length)].astype(BF16)
    copy.wait()


def top_share_kernel(inv_ref, share_ref):
    length = share_ref.shape[1]
    share_ref[...] = inv_ref[0, :, piece(lax.axis_index("col"), length)]


def half_top_kernel(p0, p3, p2, p1, half_ref):
    row = lax.axis_index("row")
    for d, ref in zip((0, 3, 2, 1), (p0, p3, p2, p1)):
        half_ref[piece(row ^ d, ref.shape[0])] = ref[...]


def whole_top_kernel(own_ref, other_ref, whole_ref):
    col, length = lax.axis_index("col"), own_ref.shape[1]
    whole_ref[:, piece(col, length)] = own_ref[...]
    whole_ref[:, piece(1 - col, length)] = other_ref[...]


def on_first_row(rhs):
    return jnp.where(lax.axis_index("row") == 0, rhs, 0.0)


def late_pieces_kernel(late_ref, other_ref, out_ref, given_ref):
    col, part = lax.axis_index("col"), out_ref.shape[2]
    for k in (0, 1):
        for half in (0, 1):
            for ref, side in ((out_ref, col), (given_ref, 1 - col)):
                at = piece(side, part)
                total = late_ref[k, half, at] + other_ref[k, half, at].astype(F32)
                ref[k, half] = total.astype(ref.dtype)


def top_blocks_kernel(rhs_ref, top_ref, other_ref, inv_ref, kept_ref, g3, g2, g1, ready, solved):
    row, col, part = lax.axis_index("row"), lax.axis_index("col"), top_ref.shape[1]
    for i in range(4):
        total = top_ref[i] + other_ref[i].astype(F32)
        ready[pl.ds(i * part, part)] = (on_first_row(rhs_ref[0, piece(i * 2 + col, part)]) - total).astype(BF16)
    solved[...] = times_transposed(ready[...], inv_ref[...])
    for d, ref in zip((0, 3, 2, 1), (kept_ref, g3, g2, g1)):
        ref[...] = solved[:, piece(row ^ d, ref.shape[1])].astype(ref.dtype)


def top_up_kernel(
    kept_ref, r3, r2, r1, lower_ref, late_ref, late_other_ref, solved_ref, send_ref, out_ref, given_ref, total
):
    core = lax.axis_index("gz") & 1
    part = solved_ref.shape[1]
    solved = widened(kept_ref, r3, r2, r1)
    rounded = solved.astype(BF16)
    for i in range(4):
        solved_ref[i] = solved[i * part : (i + 1) * part]
        send_ref[i] = rounded[i * part : (i + 1) * part]
    for k in (0, 1):
        total[...] = times_transposed(rounded, lower_ref[0, k])
        for half in (0, 1):
            late = late_ref[k, half] + late_other_ref[k, half].astype(F32)
            out_ref[k, half] = total[piece(half * 2 + core, part)] + late
            given_ref[k, half] = total[piece(half * 2 + 1 - core, part)].astype(BF16)


def front_pieces_kernel(kept_ref, other_ref, own_ref, send_ref, last_ref):
    part = kept_ref.shape[2]
    for half in (0, 1):
        at = pl.ds(half * part, part)
        total = kept_ref[0, half] + other_ref[0, half].astype(F32)
        own_ref[at] = total
        send_ref[at] = total.astype(BF16)
        last_ref[half] = kept_ref[1, half] + other_ref[1, half].astype(F32)


def apex_rows(rhs_ref, which, half, part):
    core, col = lax.axis_index("gz") & 1, lax.axis_index("col")
    return rhs_ref[which, piece(half * 4 + core * 2 + col, part)]


def front_solve_kernel(rhs_ref, own_ref, r3, r2, r1, inv_ref, lower_ref, last_ref, front_ref, kept_ref, given_ref, total, fronts):
    pair = lax.axis_index("gz") >> 1
    part, size = kept_ref.shape
    rhs = jnp.concatenate([apex_rows(rhs_ref, pair, half, part) for half in (0, 1)])
    ready = (rhs - widened(own_ref, r3, r2, r1)).astype(BF16)
    fronts[...] = times_transposed(ready, inv_ref[pair])
    total[...] = times_transposed(fronts[...].astype(BF16), lower_ref[pair])
    front_ref[...] = fronts[piece(pair, part)]
    kept_ref[...] = total[piece(pair, part)] + last_ref[pair]
    given_ref[:, :size] = (total[piece(1 - pair, part)] + last_ref[1 - pair]).astype(BF16)
    given_ref[:, size:] = fronts[piece(1 - pair, part)].astype(BF16)


def last_pieces_kernel(kept_ref, other_ref, own_ref, send_ref):
    total = kept_ref[...] + other_ref[:, : own_ref.shape[1]].astype(F32)
    own_ref[...] = total
    send_ref[...] = total.astype(BF16)


def place_top_kernel(top_ref, other_ref, top_all_ref, done_ref):
    done_ref[...] = jnp.zeros_like(done_ref)
    col, part = lax.axis_index("col"), top_ref.shape[1]
    for i in range(top_ref.shape[0]):
        top_all_ref[0, piece(i * 2 + col, part)] = top_ref[i]
        top_all_ref[0, piece(i * 2 + 1 - col, part)] = other_ref[i].astype(F32)


def last_solve_kernel(rhs_ref, inv_ref, own_ref, r3, r2, r1, front_ref, other_ref, solved_ref, send_ref):
    pair = lax.axis_index("gz") >> 1
    part, size = own_ref.shape
    ready = (apex_rows(rhs_ref, 2, pair, part) - widened(own_ref, r3, r2, r1)).astype(BF16)
    solved_ref[2] = times_transposed(ready, inv_ref[2])
    solved_ref[pair] = front_ref[...]
    solved_ref[1 - pair] = other_ref[:, size:].astype(F32)
    send_ref[...] = solved_ref[...].astype(BF16)


def place_apex_kernel(solved_ref, other_ref, apex_ref):
    col, part = lax.axis_index("col"), solved_ref.shape[1]
    for k in range(3):
        apex_ref[k, piece(col, part)] = solved_ref[k]
        apex_ref[k, piece(1 - col, part)] = other_ref[k].astype(F32)


def two_cols(
    leaf_rhs,
    leaf_inv,
    leaf_lower_mid,
    leaf_lower_coupling,
    leaf_parent,
    leaf_pattern,
    mid_rhs,
    parent_diagonal_inverse,
    mid_lower,
    mid_pattern,
    top_rhs,
    top_inv,
    top_lower,
    apex_rhs,
    apex_inv,
    apex_lower,
):
    count, size = leaf_rhs.shape[1:]
    width = leaf_inv.shape[1]
    quarter, part = count // 4, count // 8

    rows = lax.axis_size("row")

    leaf_solved, leaf_round, other_terms = leaf_solve(leaf_parent, leaf_rhs, leaf_inv, leaf_lower_mid, 2)
    (other_terms,) = partners(other_terms, [{"col": 1}])
    layer_up = leaf_coupling(leaf_pattern.T, leaf_round, leaf_lower_coupling)

    (share,) = whole_call(top_share_kernel, "top_share", [top_inv], [((width, size // 2), BF16)])
    shares = partners(share, ROW_MOVES)

    terms, rhs_rows = own_terms(leaf_parent, leaf_round, leaf_lower_mid, mid_rhs)
    kept, *given = whole_call(
        mid_pieces_kernel, "mid_pieces", [rhs_rows, terms, other_terms],
        [((quarter, size), F32)] + [((quarter, size), BF16)] * 3,
        after=shares,
    )
    arrived = partners(given, ROW_MOVES)
    (top_half,) = whole_call(half_top_kernel, "half_top", [share, *shares], [((size, size // 2), BF16)], after=[kept])
    (top_other,) = partners(top_half, [{"col": 1}])
    (ready,) = whole_call(
        mid_total_kernel, "mid_total", [kept, *arrived], [((quarter, size), BF16)], after=[layer_up]
    )
    arrived = partners(ready, ROW_MOVES)
    (top_whole,) = whole_call(whole_top_kernel, "whole_top", [top_half, top_other], [((size, size), BF16)])
    kept, given, late_kept, late_given, mid_solved = whole_call(
        mid_solve_kernel, "mid_solve", [mid_pattern, ready, *arrived, parent_diagonal_inverse, mid_lower, layer_up],
        [((4, part, size), F32), ((4, part, size), BF16), ((2, 2, quarter, size), F32), ((2, 2, quarter, size), BF16)]
        + [((count, width), F32)],
        flops=8 * count * size * width,
        scratch=[
            pltpu.VMEM((count, width), F32),
            pltpu.VMEM((count, width), BF16),
            pltpu.VMEM((3, count, size), F32),
            pltpu.SemaphoreType.DMA,
        ],
        scalars=1,
        after=[top_whole],
        hbm_results=1,
    )

    (other,) = partners(given, [{"col": 1}])
    (late_other,) = partners(late_given, [{"gz": 1}])
    late_kept, late_given = whole_call(
        late_pieces_kernel, "late_pieces", [late_kept, late_other],
        [((2, 2, part, size), F32), ((2, 2, part, size), BF16)],
    )
    (late_other,) = partners(late_given, [{"col": 1}])
    kept, *given = whole_call(
        top_blocks_kernel, "top_blocks", [top_rhs, kept, other, top_whole],
        [((count // 2, width), F32)] + [((count // 2, width), BF16)] * 3,
        flops=count * size * size,
        scratch=[pltpu.VMEM((count // 2, size), BF16), pltpu.VMEM((count // 2, size), F32)],
        after=[late_given],
    )
    arrived = partners(given, ROW_MOVES)
    top_solved, top_send, kept, given = whole_call(
        top_up_kernel, "top_up", [kept, *arrived, top_lower, late_kept, late_other],
        [((4, part, width), F32), ((4, part, width), BF16), ((2, 2, part, size), F32), ((2, 2, part, size), BF16)],
        flops=2 * count * size * width,
        scratch=[pltpu.VMEM((4 * part, size), F32)],
    )
    (other,) = partners(given, [{"gz": 1}])
    (other_top,) = partners(top_send, [{"col": 1}])

    own, send, last = whole_call(
        front_pieces_kernel, "front_pieces", [kept, other],
        [((2 * part, size), F32), ((2 * part, size), BF16), ((2, part, size), F32)],
    )
    arrived = partners(send, ROW_MOVES)
    front, kept, given = whole_call(
        front_solve_kernel, "front_solve", [apex_rhs, own, *arrived, apex_inv, apex_lower, last],
        [((part, width), F32), ((part, size), F32), ((part, size + width), BF16)],
        flops=count * size * width,
        scratch=[pltpu.VMEM((2 * part, size), F32), pltpu.VMEM((2 * part, width), F32)],
    )

    (other,) = partners(given, [{"gz": 2}])
    own, send = whole_call(
        last_pieces_kernel, "last_pieces", [kept, other], [((part, size), F32), ((part, size), BF16)]
    )
    arrived = partners(send, ROW_MOVES)
    top_all, placed = whole_call(
        place_top_kernel, "place_top", [top_solved, other_top], [((1, count, width), F32), ((8, width), F32)], after=[own]
    )
    solved, send = whole_call(
        last_solve_kernel, "last_solve", [apex_rhs, apex_inv, own, *arrived, front, other],
        [((3, part, width), F32), ((3, part, width), BF16)],
        flops=count * size * width // 4,
        after=[placed],
    )
    (other,) = partners(send, [{"col": 1}])
    (apex,) = whole_call(place_apex_kernel, "place_apex", [solved, other], [((3, 2 * part, width), F32)])
    return (leaf_solved, mid_solved[None], top_all, apex)


def solution(mesh):
    placed = (
        P(("gz", "col"), None, None),
        P(("gz", "col"), "row", None),
        P(("gz", "col"), None, "row"),
        P(("gz", "col"), None, None, "row"),
        P(("gz", "col")),
        P(("gz", "col"), None),
        P(("gz", "col"), None, None),
        P(("gz", "col"), "row", None),
        P(("gz", "col"), None, None, "row"),
        P(("gz", "col"), None),
        P("gz", None, None),
        P("gz", "row", None),
        P("gz", None, None, "row"),
        P(),
        P(None, "row", None),
        P(None, None, "row"),
    )
    return jax.shard_map(
        two_cols if mesh.shape["col"] == 2 else any_cols,
        mesh=mesh,
        in_specs=placed,
        out_specs=(
            P(("gz", "col"), None, "row"),
            P(("gz", "col"), None, "row"),
            P("gz", None, "row"),
            P(None, "gz", "row"),
        ),
        check_vma=False,
    )
```

```python
import functools
import math

import jax
import jax.numpy as jnp
from jax import lax
from jax.experimental import pallas as pl
from jax.experimental.pallas import tpu as pltpu
from jax.sharding import PartitionSpec as P

BF16 = jnp.bfloat16
F32 = jnp.float32
LEAF_VMEM_BYTES = 56 * 1024 * 1024
OWN_VMEM_BYTES = 52 * 1024 * 1024
LARGE_VMEM_BYTES = 50 * 1024 * 1024
STEP_VMEM_BYTES = 16 * 1024 * 1024


def times_transposed(left, right):
    return lax.dot_general(left, right, (((1,), (1,)), ((), ())), preferred_element_type=F32)


def masked_terms(parent_ref, wanted, rounded, mid):
    leaves = mid.shape[0]
    weights = [jnp.where(parent_ref[i] == wanted, 1.0, 0.0).astype(BF16) for i in range(leaves)]
    left = jnp.concatenate([rounded[i] * weights[i] for i in range(leaves)], axis=1)
    right = jnp.concatenate([mid[i] for i in range(leaves)], axis=1)
    return times_transposed(left, right)


def leaf_kernel(
    slots, parent_ref, rhs_ref, inv_ref, mid_ref, solved_ref, round_ref, *rest
):
    terms_refs = rest[: len(rest) - 11]
    rhs, inv, mid, solved, rounded, total, rhs_sems, inv_sems, mid_sem, out_sems, round_sems = rest[len(rest) - 11 :]
    leaves = rhs.shape[0]
    rhs_copies = [pltpu.make_async_copy(rhs_ref.at[i], rhs.at[i], rhs_sems.at[i]) for i in range(leaves)]
    inv_copies = [pltpu.make_async_copy(inv_ref.at[i], inv.at[i], inv_sems.at[i]) for i in range(leaves)]
    mid_copy = pltpu.make_async_copy(mid_ref, mid, mid_sem)
    for i in range(leaves):
        inv_copies[i].start()
        rhs_copies[i].start()
    mid_copy.start()
    out_copies = []
    for start in range(0, leaves, 2):
        group = range(start, min(start + 2, leaves))
        for i in group:
            inv_copies[i].wait()
            rhs_copies[i].wait()
        products = [times_transposed(rhs[i].astype(BF16), inv[i]) for i in group]
        for i, product in zip(group, products):
            solved[i] = product
            rounded[i] = product.astype(BF16)
        for i in group:
            out_copies.append(pltpu.make_async_copy(solved.at[i], solved_ref.at[i], out_sems.at[i]))
            out_copies.append(pltpu.make_async_copy(rounded.at[i], round_ref.at[i], round_sems.at[i]))
            for copy in out_copies[-2:]:
                copy.start()
    mid_copy.wait()
    if slots == 2:
        terms_refs[0][...] = masked_terms(parent_ref, 1 - lax.axis_index("col"), rounded, mid).astype(BF16)
    else:
        total[...] = jnp.zeros_like(total)
        for i in range(leaves):
            total[parent_ref[i]] += times_transposed(rounded[i], mid[i])
        for s, ref in enumerate(terms_refs):
            ref[...] = total[s].astype(ref.dtype)
    for copy in out_copies:
        copy.wait()


def leaf_solve(parent, rhs, inv, lower_mid, slots):
    leaves, rows, size = rhs.shape
    width = inv.shape[1]
    given = 1 if slots == 2 else slots
    hbm, vmem = pl.BlockSpec(memory_space=pltpu.HBM), pl.BlockSpec(memory_space=pltpu.VMEM)
    return pl.pallas_call(
        functools.partial(leaf_kernel, slots),
        in_specs=[pl.BlockSpec(memory_space=pltpu.SMEM), hbm, hbm, hbm],
        out_specs=[hbm, hbm] + [vmem] * given,
        out_shape=[
            jax.ShapeDtypeStruct((leaves, rows, width), F32),
            jax.ShapeDtypeStruct((leaves, rows, width), BF16),
        ]
        + [jax.ShapeDtypeStruct((rows, size), BF16)] * given,
        scratch_shapes=[
            pltpu.VMEM(rhs.shape, F32),
            pltpu.VMEM(inv.shape, BF16),
            pltpu.VMEM(lower_mid.shape, BF16),
            pltpu.VMEM((leaves, rows, width), F32),
            pltpu.VMEM((leaves, rows, width), BF16),
            pltpu.VMEM((8, 128) if slots == 2 else (slots, rows, size), F32),
            pltpu.SemaphoreType.DMA((leaves,)),
            pltpu.SemaphoreType.DMA((leaves,)),
            pltpu.SemaphoreType.DMA,
            pltpu.SemaphoreType.DMA((leaves,)),
            pltpu.SemaphoreType.DMA((leaves,)),
        ],
        compiler_params=pltpu.CompilerParams(vmem_limit_bytes=LEAF_VMEM_BYTES),
        cost_estimate=pl.CostEstimate(
            flops=4 * leaves * rows * size * width,
            bytes_accessed=leaves * (rows * size * 4 + 4 * width * size + rows * width * 6),
            transcendentals=0,
        ),
        name="leaf_solve",
    )(parent, rhs, inv, lower_mid)


def own_terms_kernel(parent_ref, round_ref, mid_ref, rhs_ref, terms_ref, rhs_rows_ref, rounded, mid, sems):
    length = rhs_rows_ref.shape[0]
    copies = [
        pltpu.make_async_copy(round_ref, rounded, sems.at[0]),
        pltpu.make_async_copy(mid_ref, mid, sems.at[1]),
        pltpu.make_async_copy(rhs_ref.at[0, piece(lax.axis_index("row"), length)], rhs_rows_ref, sems.at[2]),
    ]
    for copy in copies:
        copy.start()
    for copy in copies:
        copy.wait()
    terms_ref[...] = masked_terms(parent_ref, lax.axis_index("col"), rounded, mid).astype(BF16)


def own_terms(parent, rounded, lower_mid, mid_rhs):
    rows, size = mid_rhs.shape[1:]
    hbm, vmem = pl.BlockSpec(memory_space=pltpu.HBM), pl.BlockSpec(memory_space=pltpu.VMEM)
    return pl.pallas_call(
        own_terms_kernel,
        in_specs=[pl.BlockSpec(memory_space=pltpu.SMEM), hbm, hbm, hbm],
        out_specs=[vmem, vmem],
        out_shape=[
            jax.ShapeDtypeStruct((rows, size), BF16),
            jax.ShapeDtypeStruct((rows // lax.axis_size("row"), size), F32),
        ],
        scratch_shapes=[
            pltpu.VMEM(rounded.shape, BF16),
            pltpu.VMEM(lower_mid.shape, BF16),
            pltpu.SemaphoreType.DMA((3,)),
        ],
        compiler_params=pltpu.CompilerParams(vmem_limit_bytes=OWN_VMEM_BYTES),
        cost_estimate=pl.CostEstimate(
            flops=2 * rows * size * lower_mid.shape[0] * lower_mid.shape[2],
            bytes_accessed=2 * (math.prod(rounded.shape) + math.prod(lower_mid.shape)),
            transcendentals=0,
        ),
        name="own_terms",
    )(parent, rounded, lower_mid, mid_rhs)


def coupling_kernel(pattern_ref, round_ref, lower_ref, up_ref, rounded, lower, round_sem, sems):
    leaves, kinds = lower.shape[:2]
    round_copy = pltpu.make_async_copy(round_ref, rounded, round_sem)
    round_copy.start()
    copies = [pltpu.make_async_copy(lower_ref.at[:, k], lower.at[:, k], sems.at[k]) for k in range(kinds)]
    for copy in copies:
        copy.start()
    round_copy.wait()
    for k in range(kinds):
        copies[k].wait()
        left = [rounded[i] * pattern_ref[k, i].astype(F32).astype(BF16) for i in range(leaves)]
        right = [lower[i, k] for i in range(leaves)]
        up_ref[k] = times_transposed(jnp.concatenate(left, axis=1), jnp.concatenate(right, axis=1))


def leaf_coupling(pattern, rounded, lower):
    leaves, rows, width = rounded.shape
    kinds, size = lower.shape[1:3]
    hbm = pl.BlockSpec(memory_space=pltpu.HBM)
    return pl.pallas_call(
        coupling_kernel,
        in_specs=[pl.BlockSpec(memory_space=pltpu.SMEM), hbm, hbm],
        out_specs=pl.BlockSpec(memory_space=pltpu.VMEM),
        out_shape=jax.ShapeDtypeStruct((kinds, rows, size), F32),
        scratch_shapes=[
            pltpu.VMEM(rounded.shape, BF16),
            pltpu.VMEM(lower.shape, BF16),
            pltpu.SemaphoreType.DMA,
            pltpu.SemaphoreType.DMA((kinds,)),
        ],
        compiler_params=pltpu.CompilerParams(vmem_limit_bytes=LARGE_VMEM_BYTES),
        cost_estimate=pl.CostEstimate(
            flops=2 * leaves * kinds * rows * size * width,
            bytes_accessed=leaves * (rows * width * 2 + kinds * size * width * 2) + kinds * rows * size * 4,
            transcendentals=0,
        ),
        name="leaf_coupling",
    )(pattern, rounded, lower)


def swap(block, axis, bit):
    count = lax.axis_size(axis)
    return lax.ppermute(block, axis, [(i, i ^ 1 << bit) for i in range(count)])


def swap_sum(halves, axis, bit):
    here = lax.axis_index(axis) >> bit & 1
    kept = lax.dynamic_index_in_dim(halves, here, 0, keepdims=False)
    given = lax.dynamic_index_in_dim(halves, 1 - here, 0, keepdims=False)
    return kept.astype(F32) + swap(given.astype(BF16), axis, bit).astype(F32)


def exchange(pieces, axis):
    return lax.all_to_all(pieces, axis, split_axis=0, concat_axis=0, tiled=True)


def scatter_sum(pieces, axis):
    return jnp.sum(exchange(pieces.astype(BF16), axis).astype(F32), axis=0)


def col_sum(pieces):
    if pieces.shape[0] == 2:
        return swap_sum(pieces, "col", 0)
    return scatter_sum(pieces, "col")


def spread(piece, axis):
    count = lax.axis_size(axis)
    return exchange(jnp.broadcast_to(piece[None], (count,) + piece.shape), axis)


def col_spread(piece):
    if lax.axis_size("col") == 2:
        other = swap(piece, "col", 0)
        first = lax.axis_index("col") == 0
        return jnp.stack([jnp.where(first, piece, other), jnp.where(first, other, piece)])
    return spread(piece, "col")


def any_cols(
    leaf_rhs,
    leaf_inv,
    leaf_lower_mid,
    leaf_lower_coupling,
    leaf_parent,
    leaf_pattern,
    mid_rhs,
    parent_diagonal_inverse,
    mid_lower,
    mid_pattern,
    top_rhs,
    top_inv,
    top_lower,
    apex_rhs,
    apex_inv,
    apex_lower,
):
    cols = lax.axis_size("col")
    rows = lax.axis_size("row")
    col = lax.axis_index("col")
    row = lax.axis_index("row")
    gz = lax.axis_index("gz")
    pair, core = gz // 2, gz % 2
    rhs_count, size = leaf_rhs.shape[1:]
    part = rhs_count // (4 * cols)

    leaf_solved, leaf_round, *terms = leaf_solve(leaf_parent, leaf_rhs, leaf_inv, leaf_lower_mid, cols)
    if cols == 2:
        own, _ = own_terms(leaf_parent, leaf_round, leaf_lower_mid, mid_rhs)
        mid_part = own.astype(F32) + swap(terms[0], "col", 0).astype(F32)
    else:
        mid_part = scatter_sum(jnp.stack(terms), "col")
    layer_up = leaf_coupling(leaf_pattern.T, leaf_round, leaf_lower_coupling)
    quarter = rhs_count // rows
    mid_sum = scatter_sum(mid_part.reshape(rows, quarter, size), "row")
    mid_total = lax.dynamic_slice_in_dim(mid_rhs[0], row * quarter, quarter, 0) - mid_sum
    mid_ready = spread(mid_total.astype(BF16), "row").reshape(rhs_count, size)
    mid_solved = times_transposed(mid_ready, parent_diagonal_inverse[0])
    mid_round = mid_solved.astype(BF16)
    mid_weight = mid_pattern[0].astype(F32)

    top_part = layer_up[0] + times_transposed(mid_round, mid_lower[0, 0])
    top_part = top_part.astype(BF16).reshape(rows, cols, part, size).swapaxes(0, 1)
    top_sum = scatter_sum(top_part.reshape(rows * cols, part, size), ("col", "row"))
    top_start = (row * cols + col) * part
    top_total = lax.dynamic_slice_in_dim(top_rhs[0], top_start, part, 0) - top_sum
    top_ready = spread(top_total.astype(BF16), "row").reshape(rows * part, size)
    top_solved = times_transposed(top_ready, top_inv[0])
    top_round = top_solved.astype(BF16)

    late = jnp.stack([layer_up[k] + mid_weight[k - 1] * times_transposed(mid_round, mid_lower[0, k]) for k in (1, 2)])
    late = late.reshape(2, 2, 2, cols, part, size)
    late = swap_sum(late.transpose(2, 0, 1, 3, 4, 5), "gz", 0)
    late = col_sum(late.transpose(2, 0, 1, 3, 4))

    up = jnp.stack([times_transposed(top_round, top_lower[0, k]) for k in (0, 1)])
    up = swap_sum(up.reshape(2, 2, 2, part, size).transpose(2, 0, 1, 3, 4), "gz", 0) + late
    half = part // 2
    front_sum = scatter_sum(up[0].reshape(rows, half, size), "row")
    front_start = row // 2 * (rhs_count // 2) + (core * cols + col) * part + row % 2 * half
    front_rhs = lax.dynamic_slice(apex_rhs, (pair, front_start, 0), (1, half, size))[0]
    front_ready = spread((front_rhs - front_sum).astype(BF16), "row").reshape(2 * part, size)
    front_inv = lax.dynamic_index_in_dim(apex_inv, pair, 0, keepdims=False)
    front_lower = lax.dynamic_index_in_dim(apex_lower, pair, 0, keepdims=False)
    front_solved = times_transposed(front_ready, front_inv)

    own_up = times_transposed(front_solved.astype(BF16), front_lower)
    last_part = swap_sum(up[1] + own_up.reshape(2, part, size), "gz", 1)
    last_sum = jnp.sum(spread(last_part.astype(BF16), "row").astype(F32), axis=0)
    last_start = (pair * 2 * cols + core * cols + col) * part
    last_rhs = lax.dynamic_slice_in_dim(apex_rhs[2], last_start, part, 0)
    last_solved = times_transposed((last_rhs - last_sum).astype(BF16), apex_inv[2])

    width = last_solved.shape[1]
    front_solved = front_solved.reshape(2, part, width)
    own_front = lax.dynamic_index_in_dim(front_solved, pair, 0, keepdims=False)
    other_front = swap(lax.dynamic_index_in_dim(front_solved, 1 - pair, 0, keepdims=False), "gz", 1)
    leading = pair == 0
    fronts = jnp.stack([jnp.where(leading, own_front, other_front), jnp.where(leading, other_front, own_front)])
    fronts = col_spread(fronts).swapaxes(0, 1).reshape(2, cols * part, width)
    last = col_spread(last_solved).reshape(1, cols * part, width)
    top_all = col_spread(top_solved.reshape(rows, part, width)).swapaxes(0, 1).reshape(1, rhs_count, width)
    return (leaf_solved, mid_solved[None], top_all, jnp.concatenate([fronts, last], axis=0))


def partners(block, moves):
    blocks = block if isinstance(block, (list, tuple)) else [block] * len(moves)
    arrived = []
    for item, move in zip(blocks, moves):
        axes = tuple(move)
        sizes = [lax.axis_size(axis) for axis in axes]
        route = []
        for source in range(math.prod(sizes)):
            place, rest = [], source
            for count in reversed(sizes):
                place.insert(0, rest % count)
                rest //= count
            target = 0
            for at, count, axis in zip(place, sizes, axes):
                target = target * count + (at ^ move[axis])
            route.append((source, target))
        arrived.append(lax.ppermute(item, axes, route))
    return arrived


def whole_call(kernel, name, operands, results, flops=0, scratch=(), scalars=0, after=(), hbm_results=0):
    moved = sum(math.prod(a.shape) * a.dtype.itemsize for a in operands)
    moved += sum(math.prod(shape) * jnp.dtype(kind).itemsize for shape, kind in results)
    smem, vmem = pl.BlockSpec(memory_space=pltpu.SMEM), pl.BlockSpec(memory_space=pltpu.VMEM)

    def body(*refs):
        kernel(*refs[len(after) :])

    return pl.pallas_call(
        body,
        in_specs=[pl.BlockSpec(memory_space=pl.ANY)] * len(after)
        + [smem] * scalars
        + [vmem] * (len(operands) - scalars),
        out_specs=[vmem] * (len(results) - hbm_results) + [pl.BlockSpec(memory_space=pltpu.HBM)] * hbm_results,
        out_shape=[jax.ShapeDtypeStruct(shape, kind) for shape, kind in results],
        scratch_shapes=list(scratch),
        compiler_params=pltpu.CompilerParams(vmem_limit_bytes=STEP_VMEM_BYTES),
        cost_estimate=pl.CostEstimate(flops=flops, bytes_accessed=moved, transcendentals=0),
        name=name,
    )(*after, *operands)


def piece(index, length):
    return pl.ds(pl.multiple_of(index * length, length), length)


def widened(*refs):
    total = refs[0][...].astype(F32)
    for ref in refs[1:]:
        total = total + ref[...].astype(F32)
    return total


ROW_MOVES = [{"row": d} for d in (3, 2, 1)]


def mid_pieces_kernel(rhs_ref, terms_ref, other_ref, kept_ref, *given_refs):
    row, length = lax.axis_index("row"), kept_ref.shape[0]
    for d, ref in zip((0, 3, 2, 1), (kept_ref,) + given_refs):
        at = piece(row ^ d, length)
        total = terms_ref[at].astype(F32) + other_ref[at].astype(F32)
        ref[...] = rhs_ref[...] - total if d == 0 else total.astype(BF16)


def mid_total_kernel(kept_ref, r1, r2, r3, ready_ref):
    ready_ref[...] = (kept_ref[...] - widened(r1, r2, r3)).astype(BF16)


def mid_solve_kernel(
    pattern_ref, p0, p3, p2, p1, inv_ref, lower_ref, up_ref,
    top_ref, top_given_ref, late_ref, late_given_ref, solved_ref, solved, rounded, total, sem,
):
    row, col, core = lax.axis_index("row"), lax.axis_index("col"), lax.axis_index("gz") & 1
    length, part = p0.shape[0], top_ref.shape[1]
    for d, ref in zip((0, 3, 2, 1), (p0, p3, p2, p1)):
        at = piece(row ^ d, length)
        product = times_transposed(ref[...], inv_ref[0])
        solved[at] = product
        rounded[at] = product.astype(BF16)
    copy = pltpu.make_async_copy(solved, solved_ref, sem)
    copy.start()
    total[0] = up_ref[0] + times_transposed(rounded[...], lower_ref[0, 0])
    for i in range(4):
        top_ref[i] = total[0, piece(i * 2 + col, part)]
        top_given_ref[i] = total[0, piece(i * 2 + 1 - col, part)].astype(BF16)
    for k in (1, 2):
        weight = pattern_ref[0, k - 1].astype(F32)
        total[k] = up_ref[k] + weight * times_transposed(rounded[...], lower_ref[0, k])
        for half in (0, 1):
            late_ref[k - 1, half] = total[k, piece(half * 2 + core, length)]
            late_given_ref[k - 1, half] = total[k, piece(half * 2 + 1 - core, length)].astype(BF16)
    copy.wait()


def top_share_kernel(inv_ref, share_ref):
    length = share_ref.shape[1]
    share_ref[...] = inv_ref[0, :, piece(lax.axis_index("col"), length)]


def half_top_kernel(p0, p3, p2, p1, half_ref):
    row = lax.axis_index("row")
    for d, ref in zip((0, 3, 2, 1), (p0, p3, p2, p1)):
        half_ref[piece(row ^ d, ref.shape[0])] = ref[...]


def whole_top_kernel(own_ref, other_ref, whole_ref):
    col, length = lax.axis_index("col"), own_ref.shape[1]
    whole_ref[:, piece(col, length)] = own_ref[...]
    whole_ref[:, piece(1 - col, length)] = other_ref[...]


def apex_share_kernel(inv_ref, lower_ref, share_ref):
    gz, block = lax.axis_index("gz"), share_ref.shape[1]
    quarter = piece((gz & 1) * 2 + lax.axis_index("col"), block)
    share_ref[0] = inv_ref[gz >> 1, :, quarter]
    share_ref[1] = lower_ref[gz >> 1, quarter, :]


def rows_of_shares_kernel(p0, p3, p2, p1, share_ref):
    row = lax.axis_index("row")
    for d, ref in zip((0, 3, 2, 1), (p0, p3, p2, p1)):
        share_ref[row ^ d] = ref[...]


def whole_front_kernel(own_ref, col_ref, core_ref, both_ref, front_ref, lower_ref):
    core, col = lax.axis_index("gz") & 1, lax.axis_index("col")
    block = own_ref.shape[2]
    for d, ref in enumerate((own_ref, col_ref, core_ref, both_ref)):
        quarter = piece((core ^ d >> 1) * 2 + (col ^ d & 1), block)
        for r in range(own_ref.shape[0]):
            at = pl.ds(r * block, block)
            front_ref[at, quarter] = ref[r, 0]
            lower_ref[quarter, at] = ref[r, 1]


def on_first_row(rhs):
    return jnp.where(lax.axis_index("row") == 0, rhs, 0.0)


def late_pieces_kernel(late_ref, other_ref, out_ref, given_ref):
    col, part = lax.axis_index("col"), out_ref.shape[2]
    for k in (0, 1):
        for half in (0, 1):
            for ref, side in ((out_ref, col), (given_ref, 1 - col)):
                at = piece(side, part)
                total = late_ref[k, half, at] + other_ref[k, half, at].astype(F32)
                ref[k, half] = total.astype(ref.dtype)


def top_blocks_kernel(rhs_ref, top_ref, other_ref, inv_ref, kept_ref, g3, g2, g1, ready, solved):
    row, col, part = lax.axis_index("row"), lax.axis_index("col"), top_ref.shape[1]
    for i in range(4):
        total = top_ref[i] + other_ref[i].astype(F32)
        ready[pl.ds(i * part, part)] = (on_first_row(rhs_ref[0, piece(i * 2 + col, part)]) - total).astype(BF16)
    solved[...] = times_transposed(ready[...], inv_ref[...])
    for d, ref in zip((0, 3, 2, 1), (kept_ref, g3, g2, g1)):
        ref[...] = solved[:, piece(row ^ d, ref.shape[1])].astype(ref.dtype)


def top_up_kernel(
    kept_ref, r3, r2, r1, lower_ref, late_ref, late_other_ref, solved_ref, send_ref, out_ref, given_ref, total
):
    core = lax.axis_index("gz") & 1
    part = solved_ref.shape[1]
    solved = widened(kept_ref, r3, r2, r1)
    rounded = solved.astype(BF16)
    for i in range(4):
        solved_ref[i] = solved[i * part : (i + 1) * part]
        send_ref[i] = rounded[i * part : (i + 1) * part]
    for k in (0, 1):
        total[...] = times_transposed(rounded, lower_ref[0, k])
        for half in (0, 1):
            late = late_ref[k, half] + late_other_ref[k, half].astype(F32)
            out_ref[k, half] = total[piece(half * 2 + core, part)] + late
            given_ref[k, half] = total[piece(half * 2 + 1 - core, part)].astype(BF16)


def apex_rows(rhs_ref, which, half, part):
    core, col = lax.axis_index("gz") & 1, lax.axis_index("col")
    return rhs_ref[which, piece(half * 4 + core * 2 + col, part)]


def front_kernel(rhs_ref, kept_ref, other_ref, inv_ref, lower_ref, front_ref, last_ref, given_ref, ready, fronts, ups):
    pair, part = lax.axis_index("gz") >> 1, last_ref.shape[0]
    for half in (0, 1):
        total = kept_ref[0, half] + other_ref[0, half].astype(F32)
        ready[pl.ds(half * part, part)] = (on_first_row(apex_rows(rhs_ref, pair, half, part)) - total).astype(BF16)
    fronts[...] = times_transposed(ready[...], inv_ref[...])
    front_ref[...] = fronts[piece(pair, part)].astype(BF16)
    given_ref[0] = fronts[piece(1 - pair, part)].astype(BF16)
    ups[...] = times_transposed(fronts[...].astype(BF16), lower_ref[...])
    for half in (0, 1):
        ups[pl.ds(half * part, part)] += kept_ref[1, half] + other_ref[1, half].astype(F32)
    last_ref[...] = ups[piece(pair, part)]
    given_ref[1] = ups[piece(1 - pair, part)].astype(BF16)


def last_pieces_kernel(front_ref, last_ref, other_ref, own_ref, fronts_ref, *given_refs):
    row, pair = lax.axis_index("row"), lax.axis_index("gz") >> 1
    size, width = last_ref.shape[1], fronts_ref.shape[2]
    total = last_ref[...] + other_ref[1].astype(F32)
    own_ref[...] = total
    fronts_ref[pair] = front_ref[:, piece(row, width)].astype(F32)
    fronts_ref[1 - pair] = other_ref[0, :, piece(row, width)].astype(F32)
    for d, ref in zip((3, 2, 1), given_refs):
        at = piece(row ^ d, width)
        ref[:, :size] = total.astype(BF16)
        ref[:, pl.ds(pl.multiple_of(size + pair * width, width), width)] = front_ref[:, at]
        ref[:, pl.ds(pl.multiple_of(size + (1 - pair) * width, width), width)] = other_ref[0, :, at]


def place_top_kernel(top_ref, other_ref, top_all_ref, done_ref):
    done_ref[...] = jnp.zeros_like(done_ref)
    col, part = lax.axis_index("col"), top_ref.shape[1]
    for i in range(top_ref.shape[0]):
        top_all_ref[0, piece(i * 2 + col, part)] = top_ref[i]
        top_all_ref[0, piece(i * 2 + 1 - col, part)] = other_ref[i].astype(F32)


def last_solve_kernel(rhs_ref, inv_ref, own_ref, fronts_ref, r3, r2, r1, solved_ref, send_ref):
    part, size = own_ref.shape
    width = fronts_ref.shape[2]
    total = own_ref[...]
    for ref in (r3, r2, r1):
        total = total + ref[:, :size].astype(F32)
    ready = (apex_rows(rhs_ref, 2, lax.axis_index("gz") >> 1, part) - total).astype(BF16)
    solved_ref[2] = times_transposed(ready, inv_ref[2])
    for j in (0, 1):
        at = slice(size + j * width, size + (j + 1) * width)
        solved_ref[j] = fronts_ref[j] + (r3[:, at].astype(F32) + r2[:, at].astype(F32) + r1[:, at].astype(F32))
    send_ref[...] = solved_ref[...].astype(BF16)


def place_apex_kernel(solved_ref, other_ref, apex_ref):
    col, part = lax.axis_index("col"), solved_ref.shape[1]
    for k in range(3):
        apex_ref[k, piece(col, part)] = solved_ref[k]
        apex_ref[k, piece(1 - col, part)] = other_ref[k].astype(F32)


def two_cols(
    leaf_rhs,
    leaf_inv,
    leaf_lower_mid,
    leaf_lower_coupling,
    leaf_parent,
    leaf_pattern,
    mid_rhs,
    parent_diagonal_inverse,
    mid_lower,
    mid_pattern,
    top_rhs,
    top_inv,
    top_lower,
    apex_rhs,
    apex_inv,
    apex_lower,
):
    count, size = leaf_rhs.shape[1:]
    width = leaf_inv.shape[1]
    quarter, part = count // 4, count // 8

    rows = lax.axis_size("row")

    leaf_solved, leaf_round, other_terms = leaf_solve(leaf_parent, leaf_rhs, leaf_inv, leaf_lower_mid, 2)
    (other_terms,) = partners(other_terms, [{"col": 1}])
    layer_up = leaf_coupling(leaf_pattern.T, leaf_round, leaf_lower_coupling)

    (share,) = whole_call(top_share_kernel, "top_share", [top_inv], [((width, size // 2), BF16)])
    shares = partners(share, ROW_MOVES)

    terms, rhs_rows = own_terms(leaf_parent, leaf_round, leaf_lower_mid, mid_rhs)
    kept, *given = whole_call(
        mid_pieces_kernel, "mid_pieces", [rhs_rows, terms, other_terms],
        [((quarter, size), F32)] + [((quarter, size), BF16)] * 3,
        after=shares,
    )
    arrived = partners(given, ROW_MOVES)
    (top_half,) = whole_call(half_top_kernel, "half_top", [share, *shares], [((size, size // 2), BF16)], after=[kept])
    (top_other,) = partners(top_half, [{"col": 1}])
    (ready,) = whole_call(
        mid_total_kernel, "mid_total", [kept, *arrived], [((quarter, size), BF16)], after=[layer_up]
    )
    arrived = partners(ready, ROW_MOVES)
    (top_whole,) = whole_call(whole_top_kernel, "whole_top", [top_half, top_other], [((size, size), BF16)])
    (share,) = whole_call(apex_share_kernel, "apex_share", [apex_inv, apex_lower], [((2, width, width), BF16)], after=[ready])
    shares = partners(share, ROW_MOVES)
    kept, given, late_kept, late_given, mid_solved = whole_call(
        mid_solve_kernel, "mid_solve", [mid_pattern, ready, *arrived, parent_diagonal_inverse, mid_lower, layer_up],
        [((4, part, size), F32), ((4, part, size), BF16), ((2, 2, quarter, size), F32), ((2, 2, quarter, size), BF16)]
        + [((count, width), F32)],
        flops=8 * count * size * width,
        scratch=[
            pltpu.VMEM((count, width), F32),
            pltpu.VMEM((count, width), BF16),
            pltpu.VMEM((3, count, size), F32),
            pltpu.SemaphoreType.DMA,
        ],
        scalars=1,
        after=[top_whole],
        hbm_results=1,
    )

    (other,) = partners(given, [{"col": 1}])
    (late_other,) = partners(late_given, [{"gz": 1}])
    late_kept, late_given = whole_call(
        late_pieces_kernel, "late_pieces", [late_kept, late_other],
        [((2, 2, part, size), F32), ((2, 2, part, size), BF16)],
    )
    (late_other,) = partners(late_given, [{"col": 1}])
    kept, *given = whole_call(
        top_blocks_kernel, "top_blocks", [top_rhs, kept, other, top_whole],
        [((count // 2, width), F32)] + [((count // 2, width), BF16)] * 3,
        flops=count * size * size,
        scratch=[pltpu.VMEM((count // 2, size), BF16), pltpu.VMEM((count // 2, size), F32)],
        after=[late_given],
    )
    held, _ = lax.optimization_barrier((share, other))
    (front_share,) = whole_call(
        rows_of_shares_kernel, "front_share", [held, *shares], [((4, 2, width, width), BF16)], after=[kept]
    )
    (col_share,) = partners(front_share, [{"col": 1}])
    arrived = partners(given, ROW_MOVES)
    top_solved, top_send, kept, given = whole_call(
        top_up_kernel, "top_up", [kept, *arrived, top_lower, late_kept, late_other],
        [((4, part, width), F32), ((4, part, width), BF16), ((2, 2, part, size), F32), ((2, 2, part, size), BF16)],
        flops=2 * count * size * width,
        scratch=[pltpu.VMEM((4 * part, size), F32)],
    )
    (other,) = partners(given, [{"gz": 1}])
    held, col_held, *_ = lax.optimization_barrier((front_share, col_share, *arrived))
    core_share, both_share = partners([held, col_held], [{"gz": 1}] * 2)
    front_whole, lower_whole = whole_call(
        whole_front_kernel, "whole_front", [front_share, col_share, core_share, both_share], [((size, size), BF16)] * 2
    )
    (other_top,) = partners(top_send, [{"col": 1}])

    front, last, given = whole_call(
        front_kernel, "front", [apex_rhs, kept, other, front_whole, lower_whole],
        [((part, size), BF16), ((part, size), F32), ((2, part, size), BF16)],
        flops=count * size * size // 2,
        scratch=[pltpu.VMEM((2 * part, size), BF16)] + [pltpu.VMEM((2 * part, size), F32)] * 2,
    )

    (other,) = partners(given, [{"gz": 2}])
    own, fronts, *given = whole_call(
        last_pieces_kernel, "last_pieces", [front, last, other],
        [((part, size), F32), ((2, part, width), F32)] + [((part, size + 2 * width), BF16)] * 3,
    )
    arrived = partners(given, ROW_MOVES)
    top_all, placed = whole_call(
        place_top_kernel, "place_top", [top_solved, other_top], [((1, count, width), F32), ((8, width), F32)], after=[own]
    )
    solved, send = whole_call(
        last_solve_kernel, "last_solve", [apex_rhs, apex_inv, own, fronts, *arrived],
        [((3, part, width), F32), ((3, part, width), BF16)],
        flops=count * size * width // 4,
        after=[placed],
    )
    (other,) = partners(send, [{"col": 1}])
    (apex,) = whole_call(place_apex_kernel, "place_apex", [solved, other], [((3, 2 * part, width), F32)])
    return (leaf_solved, mid_solved[None], top_all, apex)


def solution(mesh):
    placed = (
        P(("gz", "col"), None, None),
        P(("gz", "col"), "row", None),
        P(("gz", "col"), None, "row"),
        P(("gz", "col"), None, None, "row"),
        P(("gz", "col")),
        P(("gz", "col"), None),
        P(("gz", "col"), None, None),
        P(("gz", "col"), "row", None),
        P(("gz", "col"), None, None, "row"),
        P(("gz", "col"), None),
        P("gz", None, None),
        P("gz", "row", None),
        P("gz", None, None, "row"),
        P(),
        P(None, "row", None),
        P(None, None, "row"),
    )
    return jax.shard_map(
        two_cols if mesh.shape["col"] == 2 else any_cols,
        mesh=mesh,
        in_specs=placed,
        out_specs=(
            P(("gz", "col"), None, "row"),
            P(("gz", "col"), None, "row"),
            P("gz", None, "row"),
            P(None, "gz", "row"),
        ),
        check_vma=False,
    )
```

```python
import functools
import math

import jax
import jax.numpy as jnp
from jax import lax
from jax.experimental import pallas as pl
from jax.experimental.pallas import tpu as pltpu
from jax.sharding import PartitionSpec as P

BF16 = jnp.bfloat16
F32 = jnp.float32
LEAF_VMEM_BYTES = 56 * 1024 * 1024
OWN_VMEM_BYTES = 52 * 1024 * 1024
LARGE_VMEM_BYTES = 50 * 1024 * 1024
STEP_VMEM_BYTES = 16 * 1024 * 1024


def times_transposed(left, right):
    return lax.dot_general(left, right, (((1,), (1,)), ((), ())), preferred_element_type=F32)


def masked_terms(parent_ref, wanted, rounded, mid):
    leaves = mid.shape[0]
    weights = [jnp.where(parent_ref[i] == wanted, 1.0, 0.0).astype(BF16) for i in range(leaves)]
    left = jnp.concatenate([rounded[i] * weights[i] for i in range(leaves)], axis=1)
    right = jnp.concatenate([mid[i] for i in range(leaves)], axis=1)
    return times_transposed(left, right)


def leaf_kernel(
    slots, parent_ref, rhs_ref, inv_ref, mid_ref, solved_ref, round_ref, *rest
):
    terms_refs = rest[: len(rest) - 11]
    rhs, inv, mid, solved, rounded, total, rhs_sems, inv_sems, mid_sem, out_sems, round_sems = rest[len(rest) - 11 :]
    leaves = rhs.shape[0]
    rhs_copies = [pltpu.make_async_copy(rhs_ref.at[i], rhs.at[i], rhs_sems.at[i]) for i in range(leaves)]
    inv_copies = [pltpu.make_async_copy(inv_ref.at[i], inv.at[i], inv_sems.at[i]) for i in range(leaves)]
    mid_copy = pltpu.make_async_copy(mid_ref, mid, mid_sem)
    for i in range(leaves):
        inv_copies[i].start()
        rhs_copies[i].start()
    mid_copy.start()
    out_copies = []
    for start in range(0, leaves, 2):
        group = range(start, min(start + 2, leaves))
        for i in group:
            inv_copies[i].wait()
            rhs_copies[i].wait()
        products = [times_transposed(rhs[i].astype(BF16), inv[i]) for i in group]
        for i, product in zip(group, products):
            solved[i] = product
            rounded[i] = product.astype(BF16)
        for i in group:
            out_copies.append(pltpu.make_async_copy(solved.at[i], solved_ref.at[i], out_sems.at[i]))
            out_copies.append(pltpu.make_async_copy(rounded.at[i], round_ref.at[i], round_sems.at[i]))
            for copy in out_copies[-2:]:
                copy.start()
    mid_copy.wait()
    if slots == 2:
        terms_refs[0][...] = masked_terms(parent_ref, 1 - lax.axis_index("col"), rounded, mid).astype(BF16)
    else:
        total[...] = jnp.zeros_like(total)
        for i in range(leaves):
            total[parent_ref[i]] += times_transposed(rounded[i], mid[i])
        for s, ref in enumerate(terms_refs):
            ref[...] = total[s].astype(ref.dtype)
    for copy in out_copies:
        copy.wait()


def leaf_solve(parent, rhs, inv, lower_mid, slots):
    leaves, rows, size = rhs.shape
    width = inv.shape[1]
    given = 1 if slots == 2 else slots
    hbm, vmem = pl.BlockSpec(memory_space=pltpu.HBM), pl.BlockSpec(memory_space=pltpu.VMEM)
    return pl.pallas_call(
        functools.partial(leaf_kernel, slots),
        in_specs=[pl.BlockSpec(memory_space=pltpu.SMEM), hbm, hbm, hbm],
        out_specs=[hbm, hbm] + [vmem] * given,
        out_shape=[
            jax.ShapeDtypeStruct((leaves, rows, width), F32),
            jax.ShapeDtypeStruct((leaves, rows, width), BF16),
        ]
        + [jax.ShapeDtypeStruct((rows, size), BF16)] * given,
        scratch_shapes=[
            pltpu.VMEM(rhs.shape, F32),
            pltpu.VMEM(inv.shape, BF16),
            pltpu.VMEM(lower_mid.shape, BF16),
            pltpu.VMEM((leaves, rows, width), F32),
            pltpu.VMEM((leaves, rows, width), BF16),
            pltpu.VMEM((8, 128) if slots == 2 else (slots, rows, size), F32),
            pltpu.SemaphoreType.DMA((leaves,)),
            pltpu.SemaphoreType.DMA((leaves,)),
            pltpu.SemaphoreType.DMA,
            pltpu.SemaphoreType.DMA((leaves,)),
            pltpu.SemaphoreType.DMA((leaves,)),
        ],
        compiler_params=pltpu.CompilerParams(vmem_limit_bytes=LEAF_VMEM_BYTES),
        cost_estimate=pl.CostEstimate(
            flops=4 * leaves * rows * size * width,
            bytes_accessed=leaves * (rows * size * 4 + 4 * width * size + rows * width * 6),
            transcendentals=0,
        ),
        name="leaf_solve",
    )(parent, rhs, inv, lower_mid)


def own_terms_kernel(parent_ref, round_ref, mid_ref, rhs_ref, terms_ref, rhs_rows_ref, rounded, mid, sems):
    length = rhs_rows_ref.shape[0]
    copies = [
        pltpu.make_async_copy(round_ref, rounded, sems.at[0]),
        pltpu.make_async_copy(mid_ref, mid, sems.at[1]),
        pltpu.make_async_copy(rhs_ref.at[0, piece(lax.axis_index("row"), length)], rhs_rows_ref, sems.at[2]),
    ]
    for copy in copies:
        copy.start()
    for copy in copies:
        copy.wait()
    terms_ref[...] = masked_terms(parent_ref, lax.axis_index("col"), rounded, mid).astype(BF16)


def own_terms(parent, rounded, lower_mid, mid_rhs):
    rows, size = mid_rhs.shape[1:]
    hbm, vmem = pl.BlockSpec(memory_space=pltpu.HBM), pl.BlockSpec(memory_space=pltpu.VMEM)
    return pl.pallas_call(
        own_terms_kernel,
        in_specs=[pl.BlockSpec(memory_space=pltpu.SMEM), hbm, hbm, hbm],
        out_specs=[vmem, vmem],
        out_shape=[
            jax.ShapeDtypeStruct((rows, size), BF16),
            jax.ShapeDtypeStruct((rows // lax.axis_size("row"), size), F32),
        ],
        scratch_shapes=[
            pltpu.VMEM(rounded.shape, BF16),
            pltpu.VMEM(lower_mid.shape, BF16),
            pltpu.SemaphoreType.DMA((3,)),
        ],
        compiler_params=pltpu.CompilerParams(vmem_limit_bytes=OWN_VMEM_BYTES),
        cost_estimate=pl.CostEstimate(
            flops=2 * rows * size * lower_mid.shape[0] * lower_mid.shape[2],
            bytes_accessed=2 * (math.prod(rounded.shape) + math.prod(lower_mid.shape)),
            transcendentals=0,
        ),
        name="own_terms",
    )(parent, rounded, lower_mid, mid_rhs)


def coupling_kernel(pattern_ref, round_ref, lower_ref, up_ref, rounded, lower, round_sem, sems):
    leaves, kinds = lower.shape[:2]
    round_copy = pltpu.make_async_copy(round_ref, rounded, round_sem)
    round_copy.start()
    copies = [pltpu.make_async_copy(lower_ref.at[:, k], lower.at[:, k], sems.at[k]) for k in range(kinds)]
    for copy in copies:
        copy.start()
    round_copy.wait()
    for k in range(kinds):
        copies[k].wait()
        left = [rounded[i] * pattern_ref[k, i].astype(F32).astype(BF16) for i in range(leaves)]
        right = [lower[i, k] for i in range(leaves)]
        up_ref[k] = times_transposed(jnp.concatenate(left, axis=1), jnp.concatenate(right, axis=1))


def leaf_coupling(pattern, rounded, lower):
    leaves, rows, width = rounded.shape
    kinds, size = lower.shape[1:3]
    hbm = pl.BlockSpec(memory_space=pltpu.HBM)
    return pl.pallas_call(
        coupling_kernel,
        in_specs=[pl.BlockSpec(memory_space=pltpu.SMEM), hbm, hbm],
        out_specs=pl.BlockSpec(memory_space=pltpu.VMEM),
        out_shape=jax.ShapeDtypeStruct((kinds, rows, size), F32),
        scratch_shapes=[
            pltpu.VMEM(rounded.shape, BF16),
            pltpu.VMEM(lower.shape, BF16),
            pltpu.SemaphoreType.DMA,
            pltpu.SemaphoreType.DMA((kinds,)),
        ],
        compiler_params=pltpu.CompilerParams(vmem_limit_bytes=LARGE_VMEM_BYTES),
        cost_estimate=pl.CostEstimate(
            flops=2 * leaves * kinds * rows * size * width,
            bytes_accessed=leaves * (rows * width * 2 + kinds * size * width * 2) + kinds * rows * size * 4,
            transcendentals=0,
        ),
        name="leaf_coupling",
    )(pattern, rounded, lower)


def swap(block, axis, bit):
    count = lax.axis_size(axis)
    return lax.ppermute(block, axis, [(i, i ^ 1 << bit) for i in range(count)])


def swap_sum(halves, axis, bit):
    here = lax.axis_index(axis) >> bit & 1
    kept = lax.dynamic_index_in_dim(halves, here, 0, keepdims=False)
    given = lax.dynamic_index_in_dim(halves, 1 - here, 0, keepdims=False)
    return kept.astype(F32) + swap(given.astype(BF16), axis, bit).astype(F32)


def exchange(pieces, axis):
    return lax.all_to_all(pieces, axis, split_axis=0, concat_axis=0, tiled=True)


def scatter_sum(pieces, axis):
    return jnp.sum(exchange(pieces.astype(BF16), axis).astype(F32), axis=0)


def col_sum(pieces):
    if pieces.shape[0] == 2:
        return swap_sum(pieces, "col", 0)
    return scatter_sum(pieces, "col")


def spread(piece, axis):
    count = lax.axis_size(axis)
    return exchange(jnp.broadcast_to(piece[None], (count,) + piece.shape), axis)


def col_spread(piece):
    if lax.axis_size("col") == 2:
        other = swap(piece, "col", 0)
        first = lax.axis_index("col") == 0
        return jnp.stack([jnp.where(first, piece, other), jnp.where(first, other, piece)])
    return spread(piece, "col")


def any_cols(
    leaf_rhs,
    leaf_inv,
    leaf_lower_mid,
    leaf_lower_coupling,
    leaf_parent,
    leaf_pattern,
    mid_rhs,
    parent_diagonal_inverse,
    mid_lower,
    mid_pattern,
    top_rhs,
    top_inv,
    top_lower,
    apex_rhs,
    apex_inv,
    apex_lower,
):
    cols = lax.axis_size("col")
    rows = lax.axis_size("row")
    col = lax.axis_index("col")
    row = lax.axis_index("row")
    gz = lax.axis_index("gz")
    pair, core = gz // 2, gz % 2
    rhs_count, size = leaf_rhs.shape[1:]
    part = rhs_count // (4 * cols)

    leaf_solved, leaf_round, *terms = leaf_solve(leaf_parent, leaf_rhs, leaf_inv, leaf_lower_mid, cols)
    if cols == 2:
        own, _ = own_terms(leaf_parent, leaf_round, leaf_lower_mid, mid_rhs)
        mid_part = own.astype(F32) + swap(terms[0], "col", 0).astype(F32)
    else:
        mid_part = scatter_sum(jnp.stack(terms), "col")
    layer_up = leaf_coupling(leaf_pattern.T, leaf_round, leaf_lower_coupling)
    quarter = rhs_count // rows
    mid_sum = scatter_sum(mid_part.reshape(rows, quarter, size), "row")
    mid_total = lax.dynamic_slice_in_dim(mid_rhs[0], row * quarter, quarter, 0) - mid_sum
    mid_ready = spread(mid_total.astype(BF16), "row").reshape(rhs_count, size)
    mid_solved = times_transposed(mid_ready, parent_diagonal_inverse[0])
    mid_round = mid_solved.astype(BF16)
    mid_weight = mid_pattern[0].astype(F32)

    top_part = layer_up[0] + times_transposed(mid_round, mid_lower[0, 0])
    top_part = top_part.astype(BF16).reshape(rows, cols, part, size).swapaxes(0, 1)
    top_sum = scatter_sum(top_part.reshape(rows * cols, part, size), ("col", "row"))
    top_start = (row * cols + col) * part
    top_total = lax.dynamic_slice_in_dim(top_rhs[0], top_start, part, 0) - top_sum
    top_ready = spread(top_total.astype(BF16), "row").reshape(rows * part, size)
    top_solved = times_transposed(top_ready, top_inv[0])
    top_round = top_solved.astype(BF16)

    late = jnp.stack([layer_up[k] + mid_weight[k - 1] * times_transposed(mid_round, mid_lower[0, k]) for k in (1, 2)])
    late = late.reshape(2, 2, 2, cols, part, size)
    late = swap_sum(late.transpose(2, 0, 1, 3, 4, 5), "gz", 0)
    late = col_sum(late.transpose(2, 0, 1, 3, 4))

    up = jnp.stack([times_transposed(top_round, top_lower[0, k]) for k in (0, 1)])
    up = swap_sum(up.reshape(2, 2, 2, part, size).transpose(2, 0, 1, 3, 4), "gz", 0) + late
    half = part // 2
    front_sum = scatter_sum(up[0].reshape(rows, half, size), "row")
    front_start = row // 2 * (rhs_count // 2) + (core * cols + col) * part + row % 2 * half
    front_rhs = lax.dynamic_slice(apex_rhs, (pair, front_start, 0), (1, half, size))[0]
    front_ready = spread((front_rhs - front_sum).astype(BF16), "row").reshape(2 * part, size)
    front_inv = lax.dynamic_index_in_dim(apex_inv, pair, 0, keepdims=False)
    front_lower = lax.dynamic_index_in_dim(apex_lower, pair, 0, keepdims=False)
    front_solved = times_transposed(front_ready, front_inv)

    own_up = times_transposed(front_solved.astype(BF16), front_lower)
    last_part = swap_sum(up[1] + own_up.reshape(2, part, size), "gz", 1)
    last_sum = jnp.sum(spread(last_part.astype(BF16), "row").astype(F32), axis=0)
    last_start = (pair * 2 * cols + core * cols + col) * part
    last_rhs = lax.dynamic_slice_in_dim(apex_rhs[2], last_start, part, 0)
    last_solved = times_transposed((last_rhs - last_sum).astype(BF16), apex_inv[2])

    width = last_solved.shape[1]
    front_solved = front_solved.reshape(2, part, width)
    own_front = lax.dynamic_index_in_dim(front_solved, pair, 0, keepdims=False)
    other_front = swap(lax.dynamic_index_in_dim(front_solved, 1 - pair, 0, keepdims=False), "gz", 1)
    leading = pair == 0
    fronts = jnp.stack([jnp.where(leading, own_front, other_front), jnp.where(leading, other_front, own_front)])
    fronts = col_spread(fronts).swapaxes(0, 1).reshape(2, cols * part, width)
    last = col_spread(last_solved).reshape(1, cols * part, width)
    top_all = col_spread(top_solved.reshape(rows, part, width)).swapaxes(0, 1).reshape(1, rhs_count, width)
    return (leaf_solved, mid_solved[None], top_all, jnp.concatenate([fronts, last], axis=0))


def partners(block, moves):
    blocks = block if isinstance(block, (list, tuple)) else [block] * len(moves)
    arrived = []
    for item, move in zip(blocks, moves):
        axes = tuple(move)
        sizes = [lax.axis_size(axis) for axis in axes]
        route = []
        for source in range(math.prod(sizes)):
            place, rest = [], source
            for count in reversed(sizes):
                place.insert(0, rest % count)
                rest //= count
            target = 0
            for at, count, axis in zip(place, sizes, axes):
                target = target * count + (at ^ move[axis])
            route.append((source, target))
        arrived.append(lax.ppermute(item, axes, route))
    return arrived


def whole_call(kernel, name, operands, results, flops=0, scratch=(), scalars=0, after=(), hbm_results=0):
    moved = sum(math.prod(a.shape) * a.dtype.itemsize for a in operands)
    moved += sum(math.prod(shape) * jnp.dtype(kind).itemsize for shape, kind in results)
    smem, vmem = pl.BlockSpec(memory_space=pltpu.SMEM), pl.BlockSpec(memory_space=pltpu.VMEM)

    def body(*refs):
        kernel(*refs[len(after) :])

    return pl.pallas_call(
        body,
        in_specs=[pl.BlockSpec(memory_space=pl.ANY)] * len(after)
        + [smem] * scalars
        + [vmem] * (len(operands) - scalars),
        out_specs=[vmem] * (len(results) - hbm_results) + [pl.BlockSpec(memory_space=pltpu.HBM)] * hbm_results,
        out_shape=[jax.ShapeDtypeStruct(shape, kind) for shape, kind in results],
        scratch_shapes=list(scratch),
        compiler_params=pltpu.CompilerParams(vmem_limit_bytes=STEP_VMEM_BYTES),
        cost_estimate=pl.CostEstimate(flops=flops, bytes_accessed=moved, transcendentals=0),
        name=name,
    )(*after, *operands)


def piece(index, length):
    return pl.ds(pl.multiple_of(index * length, length), length)


def widened(*refs):
    total = refs[0][...].astype(F32)
    for ref in refs[1:]:
        total = total + ref[...].astype(F32)
    return total


ROW_MOVES = [{"row": d} for d in (3, 2, 1)]


def mid_pieces_kernel(rhs_ref, terms_ref, other_ref, kept_ref, *given_refs):
    row, length = lax.axis_index("row"), kept_ref.shape[0]
    for d, ref in zip((0, 3, 2, 1), (kept_ref,) + given_refs):
        at = piece(row ^ d, length)
        total = terms_ref[at].astype(F32) + other_ref[at].astype(F32)
        ref[...] = rhs_ref[...] - total if d == 0 else total.astype(BF16)


def mid_total_kernel(kept_ref, r1, r2, r3, ready_ref):
    ready_ref[...] = (kept_ref[...] - widened(r1, r2, r3)).astype(BF16)


def mid_solve_kernel(
    pattern_ref, p0, p3, p2, p1, inv_ref, lower_ref, up_ref,
    top_ref, top_given_ref, late_ref, late_given_ref, solved_ref, solved, rounded, total, sem,
):
    row, col, core = lax.axis_index("row"), lax.axis_index("col"), lax.axis_index("gz") & 1
    length, part = p0.shape[0], top_ref.shape[1]
    for d, ref in zip((0, 3, 2, 1), (p0, p3, p2, p1)):
        at = piece(row ^ d, length)
        product = times_transposed(ref[...], inv_ref[0])
        solved[at] = product
        rounded[at] = product.astype(BF16)
    copy = pltpu.make_async_copy(solved, solved_ref, sem)
    copy.start()
    total[0] = up_ref[0] + times_transposed(rounded[...], lower_ref[0, 0])
    for i in range(4):
        top_ref[i] = total[0, piece(i * 2 + col, part)]
        top_given_ref[i] = total[0, piece(i * 2 + 1 - col, part)].astype(BF16)
    for k in (1, 2):
        weight = pattern_ref[0, k - 1].astype(F32)
        total[k] = up_ref[k] + weight * times_transposed(rounded[...], lower_ref[0, k])
        for half in (0, 1):
            late_ref[k - 1, half] = total[k, piece(half * 2 + core, length)]
            late_given_ref[k - 1, half] = total[k, piece(half * 2 + 1 - core, length)].astype(BF16)
    copy.wait()


def top_share_kernel(inv_ref, share_ref):
    length = share_ref.shape[1]
    share_ref[...] = inv_ref[0, :, piece(lax.axis_index("col"), length)]


def half_top_kernel(p0, p3, p2, p1, half_ref):
    row = lax.axis_index("row")
    for d, ref in zip((0, 3, 2, 1), (p0, p3, p2, p1)):
        half_ref[piece(row ^ d, ref.shape[0])] = ref[...]


def whole_top_kernel(own_ref, other_ref, whole_ref):
    col, length = lax.axis_index("col"), own_ref.shape[1]
    whole_ref[:, piece(col, length)] = own_ref[...]
    whole_ref[:, piece(1 - col, length)] = other_ref[...]


def apex_share_kernel(inv_ref, lower_ref, share_ref):
    gz, block = lax.axis_index("gz"), share_ref.shape[1]
    quarter = piece((gz & 1) * 2 + lax.axis_index("col"), block)
    share_ref[0] = inv_ref[gz >> 1, :, quarter]
    share_ref[1] = lower_ref[gz >> 1, quarter, :]


def rows_of_shares_kernel(p0, p3, p2, p1, share_ref):
    row = lax.axis_index("row")
    for d, ref in zip((0, 3, 2, 1), (p0, p3, p2, p1)):
        share_ref[row ^ d] = ref[...]


def whole_front_kernel(own_ref, col_ref, core_ref, both_ref, front_ref, lower_ref):
    core, col = lax.axis_index("gz") & 1, lax.axis_index("col")
    block = own_ref.shape[2]
    for d, ref in enumerate((own_ref, col_ref, core_ref, both_ref)):
        quarter = piece((core ^ d >> 1) * 2 + (col ^ d & 1), block)
        for r in range(own_ref.shape[0]):
            at = pl.ds(r * block, block)
            front_ref[at, quarter] = ref[r, 0]
            lower_ref[quarter, at] = ref[r, 1]


def on_first_row(rhs):
    return jnp.where(lax.axis_index("row") == 0, rhs, 0.0)


def late_pieces_kernel(late_ref, other_ref, out_ref, given_ref):
    col, part = lax.axis_index("col"), out_ref.shape[2]
    for k in (0, 1):
        for half in (0, 1):
            for ref, side in ((out_ref, col), (given_ref, 1 - col)):
                at = piece(side, part)
                total = late_ref[k, half, at] + other_ref[k, half, at].astype(F32)
                ref[k, half] = total.astype(ref.dtype)


def top_blocks_kernel(rhs_ref, top_ref, other_ref, inv_ref, kept_ref, g3, g2, g1, ready, solved):
    row, col, part = lax.axis_index("row"), lax.axis_index("col"), top_ref.shape[1]
    for i in range(4):
        total = top_ref[i] + other_ref[i].astype(F32)
        ready[pl.ds(i * part, part)] = (on_first_row(rhs_ref[0, piece(i * 2 + col, part)]) - total).astype(BF16)
    solved[...] = times_transposed(ready[...], inv_ref[...])
    for d, ref in zip((0, 3, 2, 1), (kept_ref, g3, g2, g1)):
        ref[...] = solved[:, piece(row ^ d, ref.shape[1])].astype(ref.dtype)


def top_up_kernel(
    kept_ref, r3, r2, r1, lower_ref, late_ref, late_other_ref, solved_ref, send_ref, out_ref, given_ref, total
):
    core = lax.axis_index("gz") & 1
    part = solved_ref.shape[1]
    solved = widened(kept_ref, r3, r2, r1)
    rounded = solved.astype(BF16)
    for i in range(4):
        solved_ref[i] = solved[i * part : (i + 1) * part]
        send_ref[i] = rounded[i * part : (i + 1) * part]
    for k in (0, 1):
        total[...] = times_transposed(rounded, lower_ref[0, k])
        for half in (0, 1):
            late = late_ref[k, half] + late_other_ref[k, half].astype(F32)
            out_ref[k, half] = total[piece(half * 2 + core, part)] + late
            given_ref[k, half] = total[piece(half * 2 + 1 - core, part)].astype(BF16)


def apex_rows(rhs_ref, which, half, part):
    core, col = lax.axis_index("gz") & 1, lax.axis_index("col")
    return rhs_ref[which, piece(half * 4 + core * 2 + col, part)]


def front_kernel(rhs_ref, kept_ref, other_ref, inv_ref, lower_ref, front_ref, last_ref, given_ref, ready, fronts, ups):
    pair, part = lax.axis_index("gz") >> 1, last_ref.shape[0]
    for half in (0, 1):
        total = kept_ref[0, half] + other_ref[0, half].astype(F32)
        ready[pl.ds(half * part, part)] = (on_first_row(apex_rows(rhs_ref, pair, half, part)) - total).astype(BF16)
    fronts[...] = times_transposed(ready[...], inv_ref[...])
    front_ref[...] = fronts[piece(pair, part)].astype(BF16)
    given_ref[0] = fronts[piece(1 - pair, part)].astype(BF16)
    ups[...] = times_transposed(fronts[...].astype(BF16), lower_ref[...])
    for half in (0, 1):
        ups[pl.ds(half * part, part)] += kept_ref[1, half] + other_ref[1, half].astype(F32)
    last_ref[...] = ups[piece(pair, part)]
    given_ref[1] = ups[piece(1 - pair, part)].astype(BF16)


def last_pieces_kernel(front_ref, last_ref, other_ref, own_ref, fronts_ref, *given_refs):
    row, pair = lax.axis_index("row"), lax.axis_index("gz") >> 1
    size, width = last_ref.shape[1], fronts_ref.shape[2]
    total = last_ref[...] + other_ref[1].astype(F32)
    own_ref[...] = total
    fronts_ref[pair] = front_ref[:, piece(row, width)].astype(F32)
    fronts_ref[1 - pair] = other_ref[0, :, piece(row, width)].astype(F32)
    for d, ref in zip((3, 2, 1), given_refs):
        at = piece(row ^ d, width)
        ref[:, :size] = total.astype(BF16)
        ref[:, pl.ds(pl.multiple_of(size + pair * width, width), width)] = front_ref[:, at]
        ref[:, pl.ds(pl.multiple_of(size + (1 - pair) * width, width), width)] = other_ref[0, :, at]


def place_top_kernel(top_ref, other_ref, top_all_ref, done_ref):
    done_ref[...] = jnp.zeros_like(done_ref)
    col, part = lax.axis_index("col"), top_ref.shape[1]
    for i in range(top_ref.shape[0]):
        top_all_ref[0, piece(i * 2 + col, part)] = top_ref[i]
        top_all_ref[0, piece(i * 2 + 1 - col, part)] = other_ref[i].astype(F32)


def last_solve_kernel(rhs_ref, inv_ref, own_ref, fronts_ref, r3, r2, r1, solved_ref, send_ref):
    part, size = own_ref.shape
    width = fronts_ref.shape[2]
    total = own_ref[...]
    for ref in (r3, r2, r1):
        total = total + ref[:, :size].astype(F32)
    ready = (apex_rows(rhs_ref, 2, lax.axis_index("gz") >> 1, part) - total).astype(BF16)
    solved_ref[2] = times_transposed(ready, inv_ref[2])
    for j in (0, 1):
        at = slice(size + j * width, size + (j + 1) * width)
        solved_ref[j] = fronts_ref[j] + (r3[:, at].astype(F32) + r2[:, at].astype(F32) + r1[:, at].astype(F32))
    send_ref[...] = solved_ref[...].astype(BF16)


def place_apex_kernel(solved_ref, other_ref, apex_ref):
    col, part = lax.axis_index("col"), solved_ref.shape[1]
    for k in range(3):
        apex_ref[k, piece(col, part)] = solved_ref[k]
        apex_ref[k, piece(1 - col, part)] = other_ref[k].astype(F32)


def two_cols(
    leaf_rhs,
    leaf_inv,
    leaf_lower_mid,
    leaf_lower_coupling,
    leaf_parent,
    leaf_pattern,
    mid_rhs,
    parent_diagonal_inverse,
    mid_lower,
    mid_pattern,
    top_rhs,
    top_inv,
    top_lower,
    apex_rhs,
    apex_inv,
    apex_lower,
):
    count, size = leaf_rhs.shape[1:]
    width = leaf_inv.shape[1]
    quarter, part = count // 4, count // 8

    rows = lax.axis_size("row")

    leaf_solved, leaf_round, other_terms = leaf_solve(leaf_parent, leaf_rhs, leaf_inv, leaf_lower_mid, 2)
    (other_terms,) = partners(other_terms, [{"col": 1}])
    layer_up = leaf_coupling(leaf_pattern.T, leaf_round, leaf_lower_coupling)

    (share,) = whole_call(top_share_kernel, "top_share", [top_inv], [((width, size // 2), BF16)])
    shares = partners(share, ROW_MOVES)

    terms, rhs_rows = own_terms(leaf_parent, leaf_round, leaf_lower_mid, mid_rhs)
    kept, *given = whole_call(
        mid_pieces_kernel, "mid_pieces", [rhs_rows, terms, other_terms],
        [((quarter, size), F32)] + [((quarter, size), BF16)] * 3,
        after=shares,
    )
    arrived = partners(given, ROW_MOVES)
    (top_half,) = whole_call(half_top_kernel, "half_top", [share, *shares], [((size, size // 2), BF16)], after=[kept])
    (top_other,) = partners(top_half, [{"col": 1}])
    (ready,) = whole_call(
        mid_total_kernel, "mid_total", [kept, *arrived], [((quarter, size), BF16)], after=[layer_up]
    )
    arrived = partners(ready, ROW_MOVES)
    (top_whole,) = whole_call(whole_top_kernel, "whole_top", [top_half, top_other], [((size, size), BF16)])
    (share,) = whole_call(apex_share_kernel, "apex_share", [apex_inv, apex_lower], [((2, width, width), BF16)], after=[ready])
    shares = partners(share, ROW_MOVES)
    kept, given, late_kept, late_given, mid_solved = whole_call(
        mid_solve_kernel, "mid_solve", [mid_pattern, ready, *arrived, parent_diagonal_inverse, mid_lower, layer_up],
        [((4, part, size), F32), ((4, part, size), BF16), ((2, 2, quarter, size), F32), ((2, 2, quarter, size), BF16)]
        + [((count, width), F32)],
        flops=8 * count * size * width,
        scratch=[
            pltpu.VMEM((count, width), F32),
            pltpu.VMEM((count, width), BF16),
            pltpu.VMEM((3, count, size), F32),
            pltpu.SemaphoreType.DMA,
        ],
        scalars=1,
        after=[top_whole],
        hbm_results=1,
    )

    (other,) = partners(given, [{"col": 1}])
    (late_other,) = partners(late_given, [{"gz": 1}])
    late_kept, late_given = whole_call(
        late_pieces_kernel, "late_pieces", [late_kept, late_other],
        [((2, 2, part, size), F32), ((2, 2, part, size), BF16)],
    )
    (late_other,) = partners(late_given, [{"col": 1}])
    kept, *given = whole_call(
        top_blocks_kernel, "top_blocks", [top_rhs, kept, other, top_whole],
        [((count // 2, width), F32)] + [((count // 2, width), BF16)] * 3,
        flops=count * size * size,
        scratch=[pltpu.VMEM((count // 2, size), BF16), pltpu.VMEM((count // 2, size), F32)],
        after=[late_given],
    )
    held, _ = lax.optimization_barrier((share, other))
    (front_share,) = whole_call(
        rows_of_shares_kernel, "front_share", [held, *shares], [((4, 2, width, width), BF16)], after=[kept]
    )
    (col_share,) = partners(front_share, [{"col": 1}])
    arrived = partners(given, ROW_MOVES)
    top_solved, top_send, kept, given = whole_call(
        top_up_kernel, "top_up", [kept, *arrived, top_lower, late_kept, late_other],
        [((4, part, width), F32), ((4, part, width), BF16), ((2, 2, part, size), F32), ((2, 2, part, size), BF16)],
        flops=2 * count * size * width,
        scratch=[pltpu.VMEM((4 * part, size), F32)],
    )
    (other,) = partners(given, [{"gz": 1}])
    held, col_held, *_ = lax.optimization_barrier((front_share, col_share, *arrived))
    core_share, both_share = partners([held, col_held], [{"gz": 1}] * 2)
    front_whole, lower_whole = whole_call(
        whole_front_kernel, "whole_front", [front_share, col_share, core_share, both_share], [((size, size), BF16)] * 2
    )
    (other_top,) = partners(top_send, [{"col": 1}])

    front, last, given = whole_call(
        front_kernel, "front", [apex_rhs, kept, other, front_whole, lower_whole],
        [((part, size), BF16), ((part, size), F32), ((2, part, size), BF16)],
        flops=count * size * size // 2,
        scratch=[pltpu.VMEM((2 * part, size), BF16)] + [pltpu.VMEM((2 * part, size), F32)] * 2,
    )

    (other,) = partners(given, [{"gz": 2}])
    own, fronts, *given = whole_call(
        last_pieces_kernel, "last_pieces", [front, last, other],
        [((part, size), F32), ((2, part, width), F32)] + [((part, size + 2 * width), BF16)] * 3,
        after=[other_top],
    )
    arrived = partners(given, ROW_MOVES)
    top_all, placed = whole_call(
        place_top_kernel, "place_top", [top_solved, other_top], [((1, count, width), F32), ((8, width), F32)], after=[own]
    )
    solved, send = whole_call(
        last_solve_kernel, "last_solve", [apex_rhs, apex_inv, own, fronts, *arrived],
        [((3, part, width), F32), ((3, part, width), BF16)],
        flops=count * size * width // 4,
        after=[placed],
    )
    (other,) = partners(send, [{"col": 1}])
    (apex,) = whole_call(place_apex_kernel, "place_apex", [solved, other], [((3, 2 * part, width), F32)])
    return (leaf_solved, mid_solved[None], top_all, apex)


def solution(mesh):
    placed = (
        P(("gz", "col"), None, None),
        P(("gz", "col"), "row", None),
        P(("gz", "col"), None, "row"),
        P(("gz", "col"), None, None, "row"),
        P(("gz", "col")),
        P(("gz", "col"), None),
        P(("gz", "col"), None, None),
        P(("gz", "col"), "row", None),
        P(("gz", "col"), None, None, "row"),
        P(("gz", "col"), None),
        P("gz", None, None),
        P("gz", "row", None),
        P("gz", None, None, "row"),
        P(),
        P(None, "row", None),
        P(None, None, "row"),
    )
    return jax.shard_map(
        two_cols if mesh.shape["col"] == 2 else any_cols,
        mesh=mesh,
        in_specs=placed,
        out_specs=(
            P(("gz", "col"), None, "row"),
            P(("gz", "col"), None, "row"),
            P("gz", None, "row"),
            P(None, "gz", "row"),
        ),
        check_vma=False,
    )
```

```python
import functools
import math

import jax
import jax.numpy as jnp
from jax import lax
from jax.experimental import pallas as pl
from jax.experimental.pallas import tpu as pltpu
from jax.sharding import PartitionSpec as P

BF16 = jnp.bfloat16
F32 = jnp.float32
LEAF_VMEM_BYTES = 56 * 1024 * 1024
OWN_VMEM_BYTES = 52 * 1024 * 1024
LARGE_VMEM_BYTES = 50 * 1024 * 1024
STEP_VMEM_BYTES = 16 * 1024 * 1024


def times_transposed(left, right):
    return lax.dot_general(left, right, (((1,), (1,)), ((), ())), preferred_element_type=F32)


def masked_terms(parent_ref, wanted, rounded, mid):
    leaves = mid.shape[0]
    weights = [jnp.where(parent_ref[i] == wanted, 1.0, 0.0).astype(BF16) for i in range(leaves)]
    left = jnp.concatenate([rounded[i] * weights[i] for i in range(leaves)], axis=1)
    right = jnp.concatenate([mid[i] for i in range(leaves)], axis=1)
    return times_transposed(left, right)


def leaf_kernel(
    slots, parent_ref, rhs_ref, inv_ref, mid_ref, solved_ref, round_ref, *rest
):
    terms_refs = rest[: len(rest) - 11]
    rhs, inv, mid, solved, rounded, total, rhs_sems, inv_sems, mid_sem, out_sems, round_sems = rest[len(rest) - 11 :]
    leaves = rhs.shape[0]
    rhs_copies = [pltpu.make_async_copy(rhs_ref.at[i], rhs.at[i], rhs_sems.at[i]) for i in range(leaves)]
    inv_copies = [pltpu.make_async_copy(inv_ref.at[i], inv.at[i], inv_sems.at[i]) for i in range(leaves)]
    mid_copy = pltpu.make_async_copy(mid_ref, mid, mid_sem)
    for i in range(leaves):
        inv_copies[i].start()
        rhs_copies[i].start()
    mid_copy.start()
    out_copies = []
    for start in range(0, leaves, 4):
        group = range(start, min(start + 4, leaves))
        for i in group:
            inv_copies[i].wait()
            rhs_copies[i].wait()
        products = [times_transposed(rhs[i].astype(BF16), inv[i]) for i in group]
        for i, product in zip(group, products):
            solved[i] = product
            rounded[i] = product.astype(BF16)
        for i in group:
            out_copies.append(pltpu.make_async_copy(solved.at[i], solved_ref.at[i], out_sems.at[i]))
            out_copies.append(pltpu.make_async_copy(rounded.at[i], round_ref.at[i], round_sems.at[i]))
            for copy in out_copies[-2:]:
                copy.start()
    mid_copy.wait()
    if slots == 2:
        terms_refs[0][...] = masked_terms(parent_ref, 1 - lax.axis_index("col"), rounded, mid).astype(BF16)
    else:
        total[...] = jnp.zeros_like(total)
        for i in range(leaves):
            total[parent_ref[i]] += times_transposed(rounded[i], mid[i])
        for s, ref in enumerate(terms_refs):
            ref[...] = total[s].astype(ref.dtype)
    for copy in out_copies:
        copy.wait()


def leaf_solve(parent, rhs, inv, lower_mid, slots):
    leaves, rows, size = rhs.shape
    width = inv.shape[1]
    given = 1 if slots == 2 else slots
    hbm, vmem = pl.BlockSpec(memory_space=pltpu.HBM), pl.BlockSpec(memory_space=pltpu.VMEM)
    return pl.pallas_call(
        functools.partial(leaf_kernel, slots),
        in_specs=[pl.BlockSpec(memory_space=pltpu.SMEM), hbm, hbm, hbm],
        out_specs=[hbm, hbm] + [vmem] * given,
        out_shape=[
            jax.ShapeDtypeStruct((leaves, rows, width), F32),
            jax.ShapeDtypeStruct((leaves, rows, width), BF16),
        ]
        + [jax.ShapeDtypeStruct((rows, size), BF16)] * given,
        scratch_shapes=[
            pltpu.VMEM(rhs.shape, F32),
            pltpu.VMEM(inv.shape, BF16),
            pltpu.VMEM(lower_mid.shape, BF16),
            pltpu.VMEM((leaves, rows, width), F32),
            pltpu.VMEM((leaves, rows, width), BF16),
            pltpu.VMEM((8, 128) if slots == 2 else (slots, rows, size), F32),
            pltpu.SemaphoreType.DMA((leaves,)),
            pltpu.SemaphoreType.DMA((leaves,)),
            pltpu.SemaphoreType.DMA,
            pltpu.SemaphoreType.DMA((leaves,)),
            pltpu.SemaphoreType.DMA((leaves,)),
        ],
        compiler_params=pltpu.CompilerParams(vmem_limit_bytes=LEAF_VMEM_BYTES),
        cost_estimate=pl.CostEstimate(
            flops=4 * leaves * rows * size * width,
            bytes_accessed=leaves * (rows * size * 4 + 4 * width * size + rows * width * 6),
            transcendentals=0,
        ),
        name="leaf_solve",
    )(parent, rhs, inv, lower_mid)


def own_terms_kernel(parent_ref, round_ref, mid_ref, rhs_ref, terms_ref, rhs_rows_ref, rounded, mid, sems):
    length = rhs_rows_ref.shape[0]
    copies = [
        pltpu.make_async_copy(round_ref, rounded, sems.at[0]),
        pltpu.make_async_copy(mid_ref, mid, sems.at[1]),
        pltpu.make_async_copy(rhs_ref.at[0, piece(lax.axis_index("row"), length)], rhs_rows_ref, sems.at[2]),
    ]
    for copy in copies:
        copy.start()
    for copy in copies:
        copy.wait()
    terms_ref[...] = masked_terms(parent_ref, lax.axis_index("col"), rounded, mid).astype(BF16)


def own_terms(parent, rounded, lower_mid, mid_rhs):
    rows, size = mid_rhs.shape[1:]
    hbm, vmem = pl.BlockSpec(memory_space=pltpu.HBM), pl.BlockSpec(memory_space=pltpu.VMEM)
    return pl.pallas_call(
        own_terms_kernel,
        in_specs=[pl.BlockSpec(memory_space=pltpu.SMEM), hbm, hbm, hbm],
        out_specs=[vmem, vmem],
        out_shape=[
            jax.ShapeDtypeStruct((rows, size), BF16),
            jax.ShapeDtypeStruct((rows // lax.axis_size("row"), size), F32),
        ],
        scratch_shapes=[
            pltpu.VMEM(rounded.shape, BF16),
            pltpu.VMEM(lower_mid.shape, BF16),
            pltpu.SemaphoreType.DMA((3,)),
        ],
        compiler_params=pltpu.CompilerParams(vmem_limit_bytes=OWN_VMEM_BYTES),
        cost_estimate=pl.CostEstimate(
            flops=2 * rows * size * lower_mid.shape[0] * lower_mid.shape[2],
            bytes_accessed=2 * (math.prod(rounded.shape) + math.prod(lower_mid.shape)),
            transcendentals=0,
        ),
        name="own_terms",
    )(parent, rounded, lower_mid, mid_rhs)


def coupling_kernel(pattern_ref, round_ref, lower_ref, up_ref, rounded, lower, round_sem, sems):
    leaves, kinds = lower.shape[:2]
    round_copy = pltpu.make_async_copy(round_ref, rounded, round_sem)
    round_copy.start()
    copies = [pltpu.make_async_copy(lower_ref.at[:, k], lower.at[:, k], sems.at[k]) for k in range(kinds)]
    for copy in copies:
        copy.start()
    round_copy.wait()
    for k in range(kinds):
        copies[k].wait()
        left = [rounded[i] * pattern_ref[k, i].astype(F32).astype(BF16) for i in range(leaves)]
        right = [lower[i, k] for i in range(leaves)]
        up_ref[k] = times_transposed(jnp.concatenate(left, axis=1), jnp.concatenate(right, axis=1))


def leaf_coupling(pattern, rounded, lower):
    leaves, rows, width = rounded.shape
    kinds, size = lower.shape[1:3]
    hbm = pl.BlockSpec(memory_space=pltpu.HBM)
    return pl.pallas_call(
        coupling_kernel,
        in_specs=[pl.BlockSpec(memory_space=pltpu.SMEM), hbm, hbm],
        out_specs=pl.BlockSpec(memory_space=pltpu.VMEM),
        out_shape=jax.ShapeDtypeStruct((kinds, rows, size), F32),
        scratch_shapes=[
            pltpu.VMEM(rounded.shape, BF16),
            pltpu.VMEM(lower.shape, BF16),
            pltpu.SemaphoreType.DMA,
            pltpu.SemaphoreType.DMA((kinds,)),
        ],
        compiler_params=pltpu.CompilerParams(vmem_limit_bytes=LARGE_VMEM_BYTES),
        cost_estimate=pl.CostEstimate(
            flops=2 * leaves * kinds * rows * size * width,
            bytes_accessed=leaves * (rows * width * 2 + kinds * size * width * 2) + kinds * rows * size * 4,
            transcendentals=0,
        ),
        name="leaf_coupling",
    )(pattern, rounded, lower)


def swap(block, axis, bit):
    count = lax.axis_size(axis)
    return lax.ppermute(block, axis, [(i, i ^ 1 << bit) for i in range(count)])


def swap_sum(halves, axis, bit):
    here = lax.axis_index(axis) >> bit & 1
    kept = lax.dynamic_index_in_dim(halves, here, 0, keepdims=False)
    given = lax.dynamic_index_in_dim(halves, 1 - here, 0, keepdims=False)
    return kept.astype(F32) + swap(given.astype(BF16), axis, bit).astype(F32)


def exchange(pieces, axis):
    return lax.all_to_all(pieces, axis, split_axis=0, concat_axis=0, tiled=True)


def scatter_sum(pieces, axis):
    return jnp.sum(exchange(pieces.astype(BF16), axis).astype(F32), axis=0)


def col_sum(pieces):
    if pieces.shape[0] == 2:
        return swap_sum(pieces, "col", 0)
    return scatter_sum(pieces, "col")


def spread(piece, axis):
    count = lax.axis_size(axis)
    return exchange(jnp.broadcast_to(piece[None], (count,) + piece.shape), axis)


def col_spread(piece):
    if lax.axis_size("col") == 2:
        other = swap(piece, "col", 0)
        first = lax.axis_index("col") == 0
        return jnp.stack([jnp.where(first, piece, other), jnp.where(first, other, piece)])
    return spread(piece, "col")


def any_cols(
    leaf_rhs,
    leaf_inv,
    leaf_lower_mid,
    leaf_lower_coupling,
    leaf_parent,
    leaf_pattern,
    mid_rhs,
    parent_diagonal_inverse,
    mid_lower,
    mid_pattern,
    top_rhs,
    top_inv,
    top_lower,
    apex_rhs,
    apex_inv,
    apex_lower,
):
    cols = lax.axis_size("col")
    rows = lax.axis_size("row")
    col = lax.axis_index("col")
    row = lax.axis_index("row")
    gz = lax.axis_index("gz")
    pair, core = gz // 2, gz % 2
    rhs_count, size = leaf_rhs.shape[1:]
    part = rhs_count // (4 * cols)

    leaf_solved, leaf_round, *terms = leaf_solve(leaf_parent, leaf_rhs, leaf_inv, leaf_lower_mid, cols)
    if cols == 2:
        own, _ = own_terms(leaf_parent, leaf_round, leaf_lower_mid, mid_rhs)
        mid_part = own.astype(F32) + swap(terms[0], "col", 0).astype(F32)
    else:
        mid_part = scatter_sum(jnp.stack(terms), "col")
    layer_up = leaf_coupling(leaf_pattern.T, leaf_round, leaf_lower_coupling)
    quarter = rhs_count // rows
    mid_sum = scatter_sum(mid_part.reshape(rows, quarter, size), "row")
    mid_total = lax.dynamic_slice_in_dim(mid_rhs[0], row * quarter, quarter, 0) - mid_sum
    mid_ready = spread(mid_total.astype(BF16), "row").reshape(rhs_count, size)
    mid_solved = times_transposed(mid_ready, parent_diagonal_inverse[0])
    mid_round = mid_solved.astype(BF16)
    mid_weight = mid_pattern[0].astype(F32)

    top_part = layer_up[0] + times_transposed(mid_round, mid_lower[0, 0])
    top_part = top_part.astype(BF16).reshape(rows, cols, part, size).swapaxes(0, 1)
    top_sum = scatter_sum(top_part.reshape(rows * cols, part, size), ("col", "row"))
    top_start = (row * cols + col) * part
    top_total = lax.dynamic_slice_in_dim(top_rhs[0], top_start, part, 0) - top_sum
    top_ready = spread(top_total.astype(BF16), "row").reshape(rows * part, size)
    top_solved = times_transposed(top_ready, top_inv[0])
    top_round = top_solved.astype(BF16)

    late = jnp.stack([layer_up[k] + mid_weight[k - 1] * times_transposed(mid_round, mid_lower[0, k]) for k in (1, 2)])
    late = late.reshape(2, 2, 2, cols, part, size)
    late = swap_sum(late.transpose(2, 0, 1, 3, 4, 5), "gz", 0)
    late = col_sum(late.transpose(2, 0, 1, 3, 4))

    up = jnp.stack([times_transposed(top_round, top_lower[0, k]) for k in (0, 1)])
    up = swap_sum(up.reshape(2, 2, 2, part, size).transpose(2, 0, 1, 3, 4), "gz", 0) + late
    half = part // 2
    front_sum = scatter_sum(up[0].reshape(rows, half, size), "row")
    front_start = row // 2 * (rhs_count // 2) + (core * cols + col) * part + row % 2 * half
    front_rhs = lax.dynamic_slice(apex_rhs, (pair, front_start, 0), (1, half, size))[0]
    front_ready = spread((front_rhs - front_sum).astype(BF16), "row").reshape(2 * part, size)
    front_inv = lax.dynamic_index_in_dim(apex_inv, pair, 0, keepdims=False)
    front_lower = lax.dynamic_index_in_dim(apex_lower, pair, 0, keepdims=False)
    front_solved = times_transposed(front_ready, front_inv)

    own_up = times_transposed(front_solved.astype(BF16), front_lower)
    last_part = swap_sum(up[1] + own_up.reshape(2, part, size), "gz", 1)
    last_sum = jnp.sum(spread(last_part.astype(BF16), "row").astype(F32), axis=0)
    last_start = (pair * 2 * cols + core * cols + col) * part
    last_rhs = lax.dynamic_slice_in_dim(apex_rhs[2], last_start, part, 0)
    last_solved = times_transposed((last_rhs - last_sum).astype(BF16), apex_inv[2])

    width = last_solved.shape[1]
    front_solved = front_solved.reshape(2, part, width)
    own_front = lax.dynamic_index_in_dim(front_solved, pair, 0, keepdims=False)
    other_front = swap(lax.dynamic_index_in_dim(front_solved, 1 - pair, 0, keepdims=False), "gz", 1)
    leading = pair == 0
    fronts = jnp.stack([jnp.where(leading, own_front, other_front), jnp.where(leading, other_front, own_front)])
    fronts = col_spread(fronts).swapaxes(0, 1).reshape(2, cols * part, width)
    last = col_spread(last_solved).reshape(1, cols * part, width)
    top_all = col_spread(top_solved.reshape(rows, part, width)).swapaxes(0, 1).reshape(1, rhs_count, width)
    return (leaf_solved, mid_solved[None], top_all, jnp.concatenate([fronts, last], axis=0))


def partners(block, moves):
    blocks = block if isinstance(block, (list, tuple)) else [block] * len(moves)
    arrived = []
    for item, move in zip(blocks, moves):
        axes = tuple(move)
        sizes = [lax.axis_size(axis) for axis in axes]
        route = []
        for source in range(math.prod(sizes)):
            place, rest = [], source
            for count in reversed(sizes):
                place.insert(0, rest % count)
                rest //= count
            target = 0
            for at, count, axis in zip(place, sizes, axes):
                target = target * count + (at ^ move[axis])
            route.append((source, target))
        arrived.append(lax.ppermute(item, axes, route))
    return arrived


def whole_call(kernel, name, operands, results, flops=0, scratch=(), scalars=0, after=(), hbm_results=0):
    moved = sum(math.prod(a.shape) * a.dtype.itemsize for a in operands)
    moved += sum(math.prod(shape) * jnp.dtype(kind).itemsize for shape, kind in results)
    smem, vmem = pl.BlockSpec(memory_space=pltpu.SMEM), pl.BlockSpec(memory_space=pltpu.VMEM)

    def body(*refs):
        kernel(*refs[len(after) :])

    return pl.pallas_call(
        body,
        in_specs=[pl.BlockSpec(memory_space=pl.ANY)] * len(after)
        + [smem] * scalars
        + [vmem] * (len(operands) - scalars),
        out_specs=[vmem] * (len(results) - hbm_results) + [pl.BlockSpec(memory_space=pltpu.HBM)] * hbm_results,
        out_shape=[jax.ShapeDtypeStruct(shape, kind) for shape, kind in results],
        scratch_shapes=list(scratch),
        compiler_params=pltpu.CompilerParams(vmem_limit_bytes=STEP_VMEM_BYTES),
        cost_estimate=pl.CostEstimate(flops=flops, bytes_accessed=moved, transcendentals=0),
        name=name,
    )(*after, *operands)


def piece(index, length):
    return pl.ds(pl.multiple_of(index * length, length), length)


def widened(*refs):
    total = refs[0][...].astype(F32)
    for ref in refs[1:]:
        total = total + ref[...].astype(F32)
    return total


ROW_MOVES = [{"row": d} for d in (3, 2, 1)]


def mid_pieces_kernel(rhs_ref, terms_ref, other_ref, kept_ref, *given_refs):
    row, length = lax.axis_index("row"), kept_ref.shape[0]
    for d, ref in zip((0, 3, 2, 1), (kept_ref,) + given_refs):
        at = piece(row ^ d, length)
        total = terms_ref[at].astype(F32) + other_ref[at].astype(F32)
        ref[...] = rhs_ref[...] - total if d == 0 else total.astype(BF16)


def mid_total_kernel(kept_ref, r1, r2, r3, ready_ref):
    ready_ref[...] = (kept_ref[...] - widened(r1, r2, r3)).astype(BF16)


def mid_solve_kernel(
    pattern_ref, p0, p3, p2, p1, inv_ref, lower_ref, up_ref,
    top_ref, top_given_ref, late_ref, late_given_ref, solved_ref, solved, rounded, total, sem,
):
    row, col, core = lax.axis_index("row"), lax.axis_index("col"), lax.axis_index("gz") & 1
    length, part = p0.shape[0], top_ref.shape[1]
    for d, ref in zip((0, 3, 2, 1), (p0, p3, p2, p1)):
        at = piece(row ^ d, length)
        product = times_transposed(ref[...], inv_ref[0])
        solved[at] = product
        rounded[at] = product.astype(BF16)
    copy = pltpu.make_async_copy(solved, solved_ref, sem)
    copy.start()
    total[0] = up_ref[0] + times_transposed(rounded[...], lower_ref[0, 0])
    for i in range(4):
        top_ref[i] = total[0, piece(i * 2 + col, part)]
        top_given_ref[i] = total[0, piece(i * 2 + 1 - col, part)].astype(BF16)
    for k in (1, 2):
        weight = pattern_ref[0, k - 1].astype(F32)
        total[k] = up_ref[k] + weight * times_transposed(rounded[...], lower_ref[0, k])
        for half in (0, 1):
            late_ref[k - 1, half] = total[k, piece(half * 2 + core, length)]
            late_given_ref[k - 1, half] = total[k, piece(half * 2 + 1 - core, length)].astype(BF16)
    copy.wait()


def top_share_kernel(inv_ref, share_ref):
    length = share_ref.shape[1]
    share_ref[...] = inv_ref[0, :, piece(lax.axis_index("col"), length)]


def half_top_kernel(p0, p3, p2, p1, half_ref):
    row = lax.axis_index("row")
    for d, ref in zip((0, 3, 2, 1), (p0, p3, p2, p1)):
        half_ref[piece(row ^ d, ref.shape[0])] = ref[...]


def whole_top_kernel(own_ref, other_ref, whole_ref):
    col, length = lax.axis_index("col"), own_ref.shape[1]
    whole_ref[:, piece(col, length)] = own_ref[...]
    whole_ref[:, piece(1 - col, length)] = other_ref[...]


def apex_share_kernel(inv_ref, lower_ref, share_ref):
    gz, block = lax.axis_index("gz"), share_ref.shape[1]
    quarter = piece((gz & 1) * 2 + lax.axis_index("col"), block)
    share_ref[0] = inv_ref[gz >> 1, :, quarter]
    share_ref[1] = lower_ref[gz >> 1, quarter, :]


def rows_of_shares_kernel(p0, p3, p2, p1, share_ref):
    row = lax.axis_index("row")
    for d, ref in zip((0, 3, 2, 1), (p0, p3, p2, p1)):
        share_ref[row ^ d] = ref[...]


def whole_front_kernel(own_ref, col_ref, core_ref, both_ref, front_ref, lower_ref):
    core, col = lax.axis_index("gz") & 1, lax.axis_index("col")
    block = own_ref.shape[2]
    for d, ref in enumerate((own_ref, col_ref, core_ref, both_ref)):
        quarter = piece((core ^ d >> 1) * 2 + (col ^ d & 1), block)
        for r in range(own_ref.shape[0]):
            at = pl.ds(r * block, block)
            front_ref[at, quarter] = ref[r, 0]
            lower_ref[quarter, at] = ref[r, 1]


def on_first_row(rhs):
    return jnp.where(lax.axis_index("row") == 0, rhs, 0.0)


def late_pieces_kernel(late_ref, other_ref, out_ref, given_ref):
    col, part = lax.axis_index("col"), out_ref.shape[2]
    for k in (0, 1):
        for half in (0, 1):
            for ref, side in ((out_ref, col), (given_ref, 1 - col)):
                at = piece(side, part)
                total = late_ref[k, half, at] + other_ref[k, half, at].astype(F32)
                ref[k, half] = total.astype(ref.dtype)


def top_blocks_kernel(rhs_ref, top_ref, other_ref, inv_ref, kept_ref, g3, g2, g1, ready, solved):
    row, col, part = lax.axis_index("row"), lax.axis_index("col"), top_ref.shape[1]
    for i in range(4):
        total = top_ref[i] + other_ref[i].astype(F32)
        ready[pl.ds(i * part, part)] = (on_first_row(rhs_ref[0, piece(i * 2 + col, part)]) - total).astype(BF16)
    solved[...] = times_transposed(ready[...], inv_ref[...])
    for d, ref in zip((0, 3, 2, 1), (kept_ref, g3, g2, g1)):
        ref[...] = solved[:, piece(row ^ d, ref.shape[1])].astype(ref.dtype)


def top_up_kernel(
    kept_ref, r3, r2, r1, lower_ref, late_ref, late_other_ref, solved_ref, send_ref, out_ref, given_ref, total
):
    core = lax.axis_index("gz") & 1
    part = solved_ref.shape[1]
    solved = widened(kept_ref, r3, r2, r1)
    rounded = solved.astype(BF16)
    for i in range(4):
        solved_ref[i] = solved[i * part : (i + 1) * part]
        send_ref[i] = rounded[i * part : (i + 1) * part]
    for k in (0, 1):
        total[...] = times_transposed(rounded, lower_ref[0, k])
        for half in (0, 1):
            late = late_ref[k, half] + late_other_ref[k, half].astype(F32)
            out_ref[k, half] = total[piece(half * 2 + core, part)] + late
            given_ref[k, half] = total[piece(half * 2 + 1 - core, part)].astype(BF16)


def apex_rows(rhs_ref, which, half, part):
    core, col = lax.axis_index("gz") & 1, lax.axis_index("col")
    return rhs_ref[which, piece(half * 4 + core * 2 + col, part)]


def front_kernel(rhs_ref, kept_ref, other_ref, inv_ref, lower_ref, front_ref, last_ref, given_ref, ready, fronts, ups):
    pair, part = lax.axis_index("gz") >> 1, last_ref.shape[0]
    for half in (0, 1):
        total = kept_ref[0, half] + other_ref[0, half].astype(F32)
        ready[pl.ds(half * part, part)] = (on_first_row(apex_rows(rhs_ref, pair, half, part)) - total).astype(BF16)
    fronts[...] = times_transposed(ready[...], inv_ref[...])
    front_ref[...] = fronts[piece(pair, part)].astype(BF16)
    given_ref[0] = fronts[piece(1 - pair, part)].astype(BF16)
    ups[...] = times_transposed(fronts[...].astype(BF16), lower_ref[...])
    for half in (0, 1):
        ups[pl.ds(half * part, part)] += kept_ref[1, half] + other_ref[1, half].astype(F32)
    last_ref[...] = ups[piece(pair, part)]
    given_ref[1] = ups[piece(1 - pair, part)].astype(BF16)


def last_pieces_kernel(front_ref, last_ref, other_ref, own_ref, fronts_ref, *given_refs):
    row, pair = lax.axis_index("row"), lax.axis_index("gz") >> 1
    size, width = last_ref.shape[1], fronts_ref.shape[2]
    total = last_ref[...] + other_ref[1].astype(F32)
    own_ref[...] = total
    fronts_ref[pair] = front_ref[:, piece(row, width)].astype(F32)
    fronts_ref[1 - pair] = other_ref[0, :, piece(row, width)].astype(F32)
    for d, ref in zip((3, 2, 1), given_refs):
        at = piece(row ^ d, width)
        ref[:, :size] = total.astype(BF16)
        ref[:, pl.ds(pl.multiple_of(size + pair * width, width), width)] = front_ref[:, at]
        ref[:, pl.ds(pl.multiple_of(size + (1 - pair) * width, width), width)] = other_ref[0, :, at]


def place_top_kernel(top_ref, other_ref, top_all_ref, done_ref):
    done_ref[...] = jnp.zeros_like(done_ref)
    col, part = lax.axis_index("col"), top_ref.shape[1]
    for i in range(top_ref.shape[0]):
        top_all_ref[0, piece(i * 2 + col, part)] = top_ref[i]
        top_all_ref[0, piece(i * 2 + 1 - col, part)] = other_ref[i].astype(F32)


def last_solve_kernel(rhs_ref, inv_ref, own_ref, fronts_ref, r3, r2, r1, solved_ref, send_ref):
    part, size = own_ref.shape
    width = fronts_ref.shape[2]
    total = own_ref[...]
    for ref in (r3, r2, r1):
        total = total + ref[:, :size].astype(F32)
    ready = (apex_rows(rhs_ref, 2, lax.axis_index("gz") >> 1, part) - total).astype(BF16)
    solved_ref[2] = times_transposed(ready, inv_ref[2])
    for j in (0, 1):
        at = slice(size + j * width, size + (j + 1) * width)
        solved_ref[j] = fronts_ref[j] + (r3[:, at].astype(F32) + r2[:, at].astype(F32) + r1[:, at].astype(F32))
    send_ref[...] = solved_ref[...].astype(BF16)


def place_apex_kernel(solved_ref, other_ref, apex_ref):
    col, part = lax.axis_index("col"), solved_ref.shape[1]
    for k in range(3):
        apex_ref[k, piece(col, part)] = solved_ref[k]
        apex_ref[k, piece(1 - col, part)] = other_ref[k].astype(F32)


def two_cols(
    leaf_rhs,
    leaf_inv,
    leaf_lower_mid,
    leaf_lower_coupling,
    leaf_parent,
    leaf_pattern,
    mid_rhs,
    parent_diagonal_inverse,
    mid_lower,
    mid_pattern,
    top_rhs,
    top_inv,
    top_lower,
    apex_rhs,
    apex_inv,
    apex_lower,
):
    count, size = leaf_rhs.shape[1:]
    width = leaf_inv.shape[1]
    quarter, part = count // 4, count // 8

    rows = lax.axis_size("row")

    leaf_solved, leaf_round, other_terms = leaf_solve(leaf_parent, leaf_rhs, leaf_inv, leaf_lower_mid, 2)
    (other_terms,) = partners(other_terms, [{"col": 1}])
    layer_up = leaf_coupling(leaf_pattern.T, leaf_round, leaf_lower_coupling)

    (share,) = whole_call(top_share_kernel, "top_share", [top_inv], [((width, size // 2), BF16)])
    shares = partners(share, ROW_MOVES)

    terms, rhs_rows = own_terms(leaf_parent, leaf_round, leaf_lower_mid, mid_rhs)
    kept, *given = whole_call(
        mid_pieces_kernel, "mid_pieces", [rhs_rows, terms, other_terms],
        [((quarter, size), F32)] + [((quarter, size), BF16)] * 3,
        after=shares,
    )
    arrived = partners(given, ROW_MOVES)
    (top_half,) = whole_call(half_top_kernel, "half_top", [share, *shares], [((size, size // 2), BF16)], after=[kept])
    (top_other,) = partners(top_half, [{"col": 1}])
    (ready,) = whole_call(
        mid_total_kernel, "mid_total", [kept, *arrived], [((quarter, size), BF16)], after=[layer_up]
    )
    arrived = partners(ready, ROW_MOVES)
    (top_whole,) = whole_call(whole_top_kernel, "whole_top", [top_half, top_other], [((size, size), BF16)])
    (share,) = whole_call(apex_share_kernel, "apex_share", [apex_inv, apex_lower], [((2, width, width), BF16)], after=[ready])
    shares = partners(share, ROW_MOVES)
    kept, given, late_kept, late_given, mid_solved = whole_call(
        mid_solve_kernel, "mid_solve", [mid_pattern, ready, *arrived, parent_diagonal_inverse, mid_lower, layer_up],
        [((4, part, size), F32), ((4, part, size), BF16), ((2, 2, quarter, size), F32), ((2, 2, quarter, size), BF16)]
        + [((count, width), F32)],
        flops=8 * count * size * width,
        scratch=[
            pltpu.VMEM((count, width), F32),
            pltpu.VMEM((count, width), BF16),
            pltpu.VMEM((3, count, size), F32),
            pltpu.SemaphoreType.DMA,
        ],
        scalars=1,
        after=[top_whole],
        hbm_results=1,
    )

    (other,) = partners(given, [{"col": 1}])
    (late_other,) = partners(late_given, [{"gz": 1}])
    late_kept, late_given = whole_call(
        late_pieces_kernel, "late_pieces", [late_kept, late_other],
        [((2, 2, part, size), F32), ((2, 2, part, size), BF16)],
    )
    (late_other,) = partners(late_given, [{"col": 1}])
    kept, *given = whole_call(
        top_blocks_kernel, "top_blocks", [top_rhs, kept, other, top_whole],
        [((count // 2, width), F32)] + [((count // 2, width), BF16)] * 3,
        flops=count * size * size,
        scratch=[pltpu.VMEM((count // 2, size), BF16), pltpu.VMEM((count // 2, size), F32)],
        after=[late_given],
    )
    held, _ = lax.optimization_barrier((share, other))
    (front_share,) = whole_call(
        rows_of_shares_kernel, "front_share", [held, *shares], [((4, 2, width, width), BF16)], after=[kept]
    )
    (col_share,) = partners(front_share, [{"col": 1}])
    arrived = partners(given, ROW_MOVES)
    top_solved, top_send, kept, given = whole_call(
        top_up_kernel, "top_up", [kept, *arrived, top_lower, late_kept, late_other],
        [((4, part, width), F32), ((4, part, width), BF16), ((2, 2, part, size), F32), ((2, 2, part, size), BF16)],
        flops=2 * count * size * width,
        scratch=[pltpu.VMEM((4 * part, size), F32)],
    )
    (other,) = partners(given, [{"gz": 1}])
    held, col_held, *_ = lax.optimization_barrier((front_share, col_share, *arrived))
    core_share, both_share = partners([held, col_held], [{"gz": 1}] * 2)
    front_whole, lower_whole = whole_call(
        whole_front_kernel, "whole_front", [front_share, col_share, core_share, both_share], [((size, size), BF16)] * 2
    )
    (other_top,) = partners(top_send, [{"col": 1}])

    front, last, given = whole_call(
        front_kernel, "front", [apex_rhs, kept, other, front_whole, lower_whole],
        [((part, size), BF16), ((part, size), F32), ((2, part, size), BF16)],
        flops=count * size * size // 2,
        scratch=[pltpu.VMEM((2 * part, size), BF16)] + [pltpu.VMEM((2 * part, size), F32)] * 2,
    )

    (other,) = partners(given, [{"gz": 2}])
    own, fronts, *given = whole_call(
        last_pieces_kernel, "last_pieces", [front, last, other],
        [((part, size), F32), ((2, part, width), F32)] + [((part, size + 2 * width), BF16)] * 3,
        after=[other_top],
    )
    arrived = partners(given, ROW_MOVES)
    top_all, placed = whole_call(
        place_top_kernel, "place_top", [top_solved, other_top], [((1, count, width), F32), ((8, width), F32)], after=[own]
    )
    solved, send = whole_call(
        last_solve_kernel, "last_solve", [apex_rhs, apex_inv, own, fronts, *arrived],
        [((3, part, width), F32), ((3, part, width), BF16)],
        flops=count * size * width // 4,
        after=[placed],
    )
    (other,) = partners(send, [{"col": 1}])
    (apex,) = whole_call(place_apex_kernel, "place_apex", [solved, other], [((3, 2 * part, width), F32)])
    return (leaf_solved, mid_solved[None], top_all, apex)


def solution(mesh):
    placed = (
        P(("gz", "col"), None, None),
        P(("gz", "col"), "row", None),
        P(("gz", "col"), None, "row"),
        P(("gz", "col"), None, None, "row"),
        P(("gz", "col")),
        P(("gz", "col"), None),
        P(("gz", "col"), None, None),
        P(("gz", "col"), "row", None),
        P(("gz", "col"), None, None, "row"),
        P(("gz", "col"), None),
        P("gz", None, None),
        P("gz", "row", None),
        P("gz", None, None, "row"),
        P(),
        P(None, "row", None),
        P(None, None, "row"),
    )
    return jax.shard_map(
        two_cols if mesh.shape["col"] == 2 else any_cols,
        mesh=mesh,
        in_specs=placed,
        out_specs=(
            P(("gz", "col"), None, "row"),
            P(("gz", "col"), None, "row"),
            P("gz", None, "row"),
            P(None, "gz", "row"),
        ),
        check_vma=False,
    )
```
